128 devices in a mesh: dp: 8 (over z, x_hi), ctx: 16 (over y, x_lo, core).
Axes of the slice: x: 4 (x_hi: 2, x_lo: 2; x = x_hi * 2 + x_lo), y: 4, z: 4, core: 2. Of those that a mesh axis runs over, the one named last changes fastest.
Arguments:
- hidden: bfloat16 [8, 4096, 2048], P('dp', 'ctx'), may hold values from -6 to 6
- x_weight: bfloat16 [2048, 2048], replicated, may hold values from -0.125 to 0.125
- state_weight: bfloat16 [2048, 160], replicated, may hold values from -0.125 to 0.125
- log_rates: float32 [32], replicated, as said below
- step_bias: float32 [32], replicated, may hold values from -1 to 1
- out_gain: float32 [2048], replicated, may hold values from 0.5 to 1.5
- cotangent: bfloat16 [8, 4096, 2048], P('dp', 'ctx'), may hold values from -6 to 6
Outputs:
- mixed: bfloat16 [8, 4096, 2048], P('dp', 'ctx')
- grad_x: float32 [2048, 2048], P('ctx')
- grad_small: float32 [2048, 160], P('ctx')
The draws below stay inside these ranges and needn't reach their ends.
Inputs may be any that keep to these rules, and one draw needn't show every extreme that they name: Each head's rate exp(log_rates) lies between 0.05 / 4096 and 1 / 30.
All inputs are finite; a program needn't handle non-finite values.
Results may differ from the reference program's by a relative error of at most 0.0049.
Values may be sent and summed in bfloat16 or wider, within the bound.
A program may use at most 192 MiB of HBM per device.

```python
import jax
import jax.numpy as jnp
from jax import lax

D = 2048
HEAD = 64
STATE = 64
ROWS = 256
HEADS = 32
SMALL_WIDTH = 160
LENGTH = 4096
SEQS = 8
N_CTX = 16


def draw_log_rates(key, part):
    key = jax.random.fold_in(key, 11)
    first_key, second_key, third_key, fourth_key = jax.random.split(key, 4)
    fast_count = HEADS // 4
    middle_count = HEADS // 4
    ranking = jax.random.permutation(first_key, HEADS)
    fast_rates = jnp.log(jax.random.uniform(second_key, (HEADS,), minval=1.0 / 50.0, maxval=1.0 / 30.0))
    middle_rates = jnp.log(jax.random.uniform(fourth_key, (HEADS,), minval=1.0 / 800.0, maxval=1.0 / 300.0))
    slow_rates = jnp.log(jax.random.uniform(third_key, (HEADS,), minval=0.05, maxval=0.5) / LENGTH)
    chosen = jnp.where(ranking < fast_count, fast_rates, jnp.where(ranking < fast_count + middle_count, middle_rates, slow_rates))
    return chosen.astype(jnp.float32)


def levels(rng, shape, shards, least, top_value):
    def one(dim, parts):
        steps = jax.random.uniform(jax.random.fold_in(jax.random.fold_in(rng, 6), dim), (parts,), jnp.float32, least / len(shards), top_value / len(shards))
        return jnp.repeat(jnp.exp(steps), shape[dim] // parts).reshape((-1,) + (1,) * (len(shape) - dim - 1))

    gain = one(*shards[0])
    for cut in shards[1:]:
        gain = gain * one(*cut)
    return gain


def bell_draw(own_key, extent, width, bound, cuts=(), kind=jnp.bfloat16):
    level = levels(own_key, extent, cuts, -0.22, 0.18) if cuts else 1.0
    entries = jax.random.normal(own_key, extent, jnp.float32) * width * level
    return jnp.minimum(jnp.maximum(entries, -bound), bound).astype(kind)


def setup_inputs(seed: int = 0) -> dict:
    key_list = jax.random.split(jax.random.key(seed), 8)
    hidden = bell_draw(key_list[0], (SEQS, LENGTH, D), 1.0, 6.0, ((0, 8), (1, 16)))
    x_weight = bell_draw(key_list[1], (D, D), D ** -0.5, 0.125)
    state_weight = bell_draw(key_list[2], (D, SMALL_WIDTH), D ** -0.5, 0.125)
    log_rates = draw_log_rates(jax.random.fold_in(key_list[7], 71), 0)
    step_bias = jnp.clip(jax.random.uniform(key_list[4], (HEADS,), jnp.float32, -1.0, 1.0), -1.0, 1.0)
    out_gain = jnp.clip(1.0 + 0.1 * jax.random.normal(key_list[5], (D,), jnp.float32), 0.5, 1.5)
    cotangent = bell_draw(key_list[6], (SEQS, LENGTH, D), 1.0, 6.0, ((0, 8), (1, 16)))
    return {"hidden": hidden, "x_weight": x_weight, "state_weight": state_weight, "log_rates": log_rates, "step_bias": step_bias, "out_gain": out_gain, "cotangent": cotangent}


precise = lax.Precision.HIGHEST

def split_small(projected, log_rates, step_bias):
    inputs_b = projected[:, :STATE]
    inputs_c = projected[:, STATE:2 * STATE]
    step_size = jax.nn.softplus(projected[:, 2 * STATE:] + step_bias[None, :])
    cumlog = jnp.cumsum(-jnp.exp(log_rates)[None, :] * step_size, axis=0)
    return (inputs_b, inputs_c, step_size, cumlog)

def block_state(values_in, projected, log_rates, step_bias):
    inputs_b, inputs_c, step_size, cumlog = split_small(projected, log_rates, step_bias)
    block_rows, channels = values_in.shape
    head_count = channels // HEAD
    per_head = values_in.reshape(block_rows, head_count, HEAD)
    weighting = jnp.exp(cumlog[-1][None, :] - cumlog) * step_size
    local_end = jnp.einsum('sh,shp,sn->hpn', weighting, per_head, inputs_b, precision=precise)
    return (jnp.exp(cumlog[-1]), local_end)

def forward_y(values_in, projected, state_in, log_rates, step_bias, out_gain):
    inputs_b, inputs_c, step_size, cumlog = split_small(projected, log_rates, step_bias)
    block_rows, channels = values_in.shape
    head_count = channels // HEAD
    per_head = values_in.reshape(block_rows, head_count, HEAD)
    log_heads = cumlog.T
    log_gap = log_heads[:, :, None] - log_heads[:, None, :]
    position = jnp.arange(block_rows)
    causal = position[:, None] >= position[None, :]
    decay_mat = jnp.exp(jnp.where(causal[None, :, :], log_gap, -jnp.inf)) * step_size.T[:, None, :]
    scores = jnp.dot(inputs_c, inputs_b.T, precision=precise)
    mixing = decay_mat * scores[None, :, :]
    inner = jnp.einsum('hts,shp->thp', mixing, per_head, precision=precise)
    readout = jnp.einsum('tn,hpn->thp', inputs_c, state_in, precision=precise) * jnp.exp(cumlog)[:, :, None]
    unnormed = (inner + readout).reshape(block_rows, channels)
    rescale = lax.rsqrt(lax.optimization_barrier(jnp.mean(unnormed * unnormed, axis=1, keepdims=True)) + 1e-05)
    return unnormed * rescale * out_gain[None, :]

def run_stream(values_all, projected_all, log_rates, step_bias, out_gain):
    head_count = D // HEAD

    def one_sequence(members):
        value_blocks = members[0].reshape(N_CTX, ROWS, D)
        proj_blocks = members[1].reshape(N_CTX, ROWS, members[1].shape[-1])

        def advance(carried, blocks):
            output = forward_y(blocks[0], blocks[1], carried, log_rates, step_bias, out_gain)
            totals, local_end = block_state(blocks[0], blocks[1], log_rates, step_bias)
            return (totals[:, None, None] * carried + local_end, output)
        initial = jnp.zeros((head_count, HEAD, STATE), jnp.float32)
        ignored, outputs = lax.scan(jax.checkpoint(advance), initial, (value_blocks, proj_blocks))
        return outputs.reshape(LENGTH, D)
    return lax.map(one_sequence, (values_all, projected_all))

def reference(hidden, x_weight, state_weight, log_rates, step_bias, out_gain, cotangent):
    rows_fwd = hidden.reshape(-1, D)
    rows_rc = hidden[:, ::-1, ::-1].reshape(-1, D)

    def project(rows_in):
        values = jnp.dot(rows_in, x_weight, preferred_element_type=jnp.float32).astype(jnp.bfloat16)
        projected = jnp.dot(rows_in, state_weight, preferred_element_type=jnp.float32)
        return (values.astype(jnp.float32).reshape(SEQS, LENGTH, D), projected.reshape(SEQS, LENGTH, -1))
    values_fwd, proj_fwd = project(rows_fwd)
    values_rc, proj_rc = project(rows_rc)

    def both_branches(first_values, first_proj, second_values, second_proj):
        return (run_stream(first_values, first_proj, log_rates, step_bias, out_gain), run_stream(second_values, second_proj, log_rates, step_bias, out_gain))
    outputs, pullback = jax.vjp(both_branches, values_fwd, proj_fwd, values_rc, proj_rc)
    back = outputs[1].astype(jnp.bfloat16)[:, ::-1, ::-1]
    mixed = (outputs[0] + back.astype(jnp.float32)).astype(jnp.bfloat16)
    cot_fwd = cotangent.astype(jnp.float32)
    cot_rc = cotangent[:, ::-1, ::-1].astype(jnp.float32)
    grad_vf, grad_pf, grad_vr, grad_pr = pullback((cot_fwd, cot_rc))
    grad_vf = grad_vf.astype(jnp.bfloat16).reshape(-1, D)
    grad_vr = grad_vr.astype(jnp.bfloat16).reshape(-1, D)
    grad_pf = grad_pf.astype(jnp.bfloat16).reshape(-1, grad_pf.shape[-1])
    grad_pr = grad_pr.astype(jnp.bfloat16).reshape(-1, grad_pr.shape[-1])
    grad_x = jnp.dot(rows_fwd.T, grad_vf, preferred_element_type=jnp.float32) + jnp.dot(rows_rc.T, grad_vr, preferred_element_type=jnp.float32)
    grad_small = jnp.dot(rows_fwd.T, grad_pf, preferred_element_type=jnp.float32) + jnp.dot(rows_rc.T, grad_pr, preferred_element_type=jnp.float32)
    return (mixed, grad_x, grad_small)
```

```python
import jax
import jax.numpy as jnp
from jax import lax
from jax.experimental import pallas as pl
from jax.experimental.pallas import tpu as pltpu
from jax.sharding import PartitionSpec as P

HEAD = 64
STATE = 64
D = 2048
ROWS = 256
T2 = 2 * ROWS
HEADS = 32
PAIRS = 16
PEERS = 16
SLOT = 144
WIDE = 2304
PARTS = 3
COLS = WIDE // PARTS
MESH = pl.DeviceIdType.MESH
BF = jnp.bfloat16
F32 = jnp.float32
LOG2E = 1.4426950408889634

NN = (((1,), (0,)), ((), ()))
NT = (((1,), (1,)), ((), ()))
TN = (((0,), (0,)), ((), ()))


def dot(a, b, dims=NN):
    return lax.dot_general(a, b, dims, preferred_element_type=F32)


def dot_exact(a, b, dims=NN):
    return lax.dot_general(
        a, b, dims, preferred_element_type=F32, precision=lax.Precision.HIGHEST
    )


def iota2(shape, dim):
    return lax.broadcasted_iota(jnp.int32, shape, dim)


def flip_matrix(n):
    return (iota2((n, n), 0) + iota2((n, n), 1) == n - 1).astype(F32).astype(BF)


def project_kernel(rows_ref, wx_ref, ws_ref, rt_ref, xt_ref, proj_ref, r_ref):
    step = pl.program_id(0)

    @pl.when(step == 0)
    def _():
        flip = flip_matrix(256)
        for blk in range(8):
            part = rows_ref[:, blk * 256 : (blk + 1) * 256]
            r_ref[0:ROWS, blk * 256 : (blk + 1) * 256] = part
            r_ref[ROWS:T2, (7 - blk) * 256 : (8 - blk) * 256] = dot(part, flip).astype(BF)
            across = part.T
            rt_ref[blk * 256 : (blk + 1) * 256, 0:ROWS] = across
            rt_ref[(7 - blk) * 256 : (8 - blk) * 256, ROWS:T2] = dot(flip, across).astype(BF)
        proj_ref[...] = jnp.zeros_like(proj_ref)
        proj_ref[:, 0:160] = dot(r_ref[...], ws_ref[...])

    xt_ref[...] = dot(r_ref[...], wx_ref[...]).astype(BF).T


def project(rows, x_weight, state_weight):
    cols = 256
    return pl.pallas_call(
        project_kernel,
        grid=(D // cols,),
        in_specs=[
            pl.BlockSpec((ROWS, D), lambda i: (0, 0)),
            pl.BlockSpec((D, cols), lambda i: (0, i)),
            pl.BlockSpec((D, 160), lambda i: (0, 0)),
        ],
        out_specs=[
            pl.BlockSpec((D, T2), lambda i: (0, 0)),
            pl.BlockSpec((cols, T2), lambda i: (i, 0)),
            pl.BlockSpec((T2, 256), lambda i: (0, 0)),
        ],
        out_shape=[
            jax.ShapeDtypeStruct((D, T2), BF),
            jax.ShapeDtypeStruct((D, T2), BF),
            jax.ShapeDtypeStruct((T2, 256), F32),
        ],
        scratch_shapes=[pltpu.VMEM((T2, D), BF)],
        compiler_params=pltpu.CompilerParams(vmem_limit_bytes=48 * 2**20),
        name="project",
    )(rows, x_weight, state_weight)


def scan_kernel(
    xt_ref, proj_ref, cot_ref, gain_ref, lr_ref, sb_ref,
    mixed_ref, dxt_ref,
    small, zt, step_t, weight, l2_t, l2_n, el_t, bdb, bdbt, bdc, bdct, scm, dsc,
    wx, ct, u, g, du, vdu, mst, dec, tot, prow, qrow, q2row, asrow,
    send_a, recv_a, send_a2, recv_a2, send_b, recv_b, send_b2, recv_b2, up,
    sa, ra, sa2, ra2, sb, rb, sb2, rb2,
):
    me = lax.axis_index("ctx")
    barrier = pltpu.get_barrier_semaphore()

    def greet(j, c):
        @pl.when(j != me)
        def _():
            pl.semaphore_signal(barrier, inc=1, device_id={"ctx": j}, device_id_type=MESH)
        return c

    lax.fori_loop(0, PEERS, greet, 0)

    def copy(src, dst, ssem, rsem, to, slot):
        return pltpu.make_async_remote_copy(
            src_ref=src.at[to], dst_ref=dst.at[slot], send_sem=ssem.at[to],
            recv_sem=rsem.at[slot], device_id={"ctx": to}, device_id_type=MESH,
        )

    def send_all(src, dst, ssem, rsem):
        def one(k, c):
            j = lax.rem(me + k, PEERS)
            copy(src, dst, ssem, rsem, j, me).start()
            return c
        lax.fori_loop(1, PEERS, one, 0)

    def recv_all(src, dst, ssem, rsem):
        def one(k, c):
            j = lax.rem(me + k, PEERS)
            copy(src, dst, ssem, rsem, j, j).wait_recv()
            return c
        lax.fori_loop(1, PEERS, one, 0)

    def sent_all(src, dst, ssem, rsem):
        def one(k, c):
            j = lax.rem(me + k, PEERS)
            copy(src, dst, ssem, rsem, j, me).wait_send()
            return c
        lax.fori_loop(1, PEERS, one, 0)

    low = iota2((1, 128), 1) < 64
    row_i = iota2((ROWS, ROWS), 0)
    col_i = iota2((ROWS, ROWS), 1)
    causal = (row_i >= col_i, row_i <= col_i)
    tri = [m.astype(F32) for m in causal]
    halves = (slice(0, ROWS), slice(ROWS, T2))

    small[...] = jnp.zeros_like(small)
    small[0:1, 0:HEADS] = -jnp.exp(lr_ref[...])
    small[1:2, 0:HEADS] = sb_ref[...]
    neg_rate = small[0:1, :]
    z = proj_ref[:, 128:256] + small[1:2, :]
    step_n = jnp.maximum(z, 0.0) + jnp.log1p(jnp.exp(-jnp.abs(z)))
    log_n = step_n * (neg_rate * LOG2E)
    zt[...] = z.T[0:HEADS]
    step_t[...] = step_n.T[0:HEADS]
    for b in range(2):
        l2 = dot_exact(tri[b], log_n[halves[b]])
        l2_n[b] = l2
        l2_t[:, halves[b]] = l2.T[0:HEADS]
    el_t[...] = jnp.exp2(l2_t[...])
    ends = (l2_t[:, ROWS - 1 : ROWS], l2_t[:, ROWS : ROWS + 1])
    tot[...] = jnp.exp2(jnp.where(low, ends[0], ends[1]))
    for b in range(2):
        weight[:, halves[b]] = step_t[:, halves[b]] * jnp.exp2(ends[b] - l2_t[:, halves[b]])

    both = proj_ref[:, 0:128]
    turned = pltpu.roll(both, 64, 1)
    own = (iota2((T2, 128), 0) < ROWS) == (iota2((T2, 128), 1) < 64)
    maps_b = jnp.where(low, both, turned)
    maps_c = jnp.where(low, turned, both)
    b_diag = jnp.where(own, maps_b, 0.0)
    c_diag = jnp.where(own, maps_c, 0.0)
    for full, by_rows, by_cols in ((b_diag, bdb, bdbt), (c_diag, bdc, bdct)):
        coarse = full.astype(BF).astype(F32)
        for k, term in enumerate((coarse, full - coarse)):
            by_rows[:, k * 128 : (k + 1) * 128] = term.astype(BF)
            by_cols[k * 128 : (k + 1) * 128, :] = term.T.astype(BF)

    def to_state(lhs, by_rows):
        out = dot(lhs, by_rows[...])
        return (out[:, 0:128] + out[:, 128:256]).astype(BF)

    def from_state(state, by_cols):
        return dot(jnp.concatenate([state, state], axis=1), by_cols[...])

    def local_end(hp, c):
        base = pl.multiple_of(hp * 128, 128)
        for hh in range(2):
            rows = pl.ds(pl.multiple_of(base + hh * 64, 64), 64)
            h = pl.ds(2 * hp + hh, 1)
            wx[rows, :] = (xt_ref[rows, :].astype(F32) * weight[h, :]).astype(BF)
        send_a[hp, 0:128, :] = to_state(wx[pl.ds(base, 128), :], bdb)
        t0 = tot[pl.ds(2 * hp, 1), :]
        t1 = tot[pl.ds(2 * hp + 1, 1), :]
        h0 = t0.astype(BF).astype(F32)
        h1 = t1.astype(BF).astype(F32)
        at = iota2((16, 128), 0)
        extra = jnp.where(at == 0, h0, jnp.where(at == 1, t0 - h0, jnp.where(at == 2, h1, t1 - h1)))
        send_a[hp, 128:144, :] = extra.astype(BF)
        return c

    lax.fori_loop(0, PAIRS, local_end, 0)
    recv_a[me] = send_a[me]
    pl.semaphore_wait(barrier, PEERS - 1)
    send_all(send_a, recv_a, sa, ra)

    for b in range(2):
        sc = dot_exact(
            jnp.where(low, maps_c[halves[b]], 0.0), maps_b[halves[b]], NT
        )
        scm[b] = jnp.where(causal[b], sc, 0.0)

    zero_half = jnp.zeros((128, 128), BF)
    blocks = (((0, 0), (1, 0), (1, 1)), ((0, 0), (0, 1), (1, 1)))

    def span(i):
        return slice(i * 128, (i + 1) * 128)

    def forward(hp, c):
        for hh in range(2):
            h = 2 * hp + hh
            rows = pl.ds(pl.multiple_of(h * 64, 64), 64)
            for b in range(2):
                column = pltpu.roll(l2_n[b], 128 - h, 1)[:, 0:1]
                line = l2_t[pl.ds(h, 1), halves[b]]
                size = step_t[pl.ds(h, 1), halves[b]]
                for i, j in blocks[b]:
                    d = jnp.exp2(jnp.minimum(column[span(i)] - line[:, span(j)], 0.0))
                    d = d * size[:, span(j)]
                    dec[b, h, span(i), span(j)] = d.astype(BF)
                    mst[b, h, span(i), span(j)] = (d * scm[b, span(i), span(j)]).astype(BF)
                mst[b, h, span(b), span(1 - b)] = zero_half
                u[rows, halves[b]] = dot(xt_ref[rows, halves[b]], mst[b, h], NT)
        return c

    def chain(recv, out, fwd_up):
        def totals(i):
            t = recv_a[i, 128:144, :].astype(F32)
            rows = iota2((128, 128), 0) < 64
            return jnp.where(rows, t[0:1] + t[1:2], t[2:3] + t[3:4])

        def climb(i, carry):
            up[i] = carry
            return totals(i) * carry + recv[i, 0:128, :].astype(F32)

        zero = jnp.zeros((128, 128), F32)
        lax.fori_loop(0, PEERS, climb, zero)

        def descend(k, carry):
            i = PEERS - 1 - k
            pick = low if fwd_up else jnp.logical_not(low)
            out[i] = jnp.where(pick, up[i], carry).astype(BF)
            return totals(i) * carry + recv[i, 0:128, :].astype(F32)

        lax.fori_loop(0, PEERS, descend, zero)

    lax.fori_loop(0, PAIRS // 2, forward, 0)
    recv_all(send_a, recv_a, sa, ra)
    chain(recv_a, send_a2, True)
    recv_a2[me] = send_a2[me]
    send_all(send_a2, recv_a2, sa2, ra2)
    lax.fori_loop(PAIRS // 2, PAIRS, forward, 0)

    flip = flip_matrix(256)
    for blk in range(8):
        turned_c = cot_ref[:, blk * 256 : (blk + 1) * 256].T
        ct[blk * 256 : (blk + 1) * 256, 0:ROWS] = turned_c
        ct[(7 - blk) * 256 : (8 - blk) * 256, ROWS:T2] = dot(flip, turned_c).astype(BF)

    recv_all(send_a2, recv_a2, sa2, ra2)

    def gains(hp):
        lane = pl.ds(pl.multiple_of(hp * 128, 128), 128)
        column = jnp.broadcast_to(gain_ref[:, lane], (128, 128)).T
        return jnp.concatenate([column] * 4, axis=1)

    def readout(hp, c):
        q, e = c
        base = pl.multiple_of(hp * 128, 128)
        out = from_state(recv_a2[hp], bdct)
        gain = gains(hp)
        for hh in range(2):
            rows = pl.ds(pl.multiple_of(base + hh * 64, 64), 64)
            part = slice(hh * 64, hh * 64 + 64)
            v = u[rows, :] + out[part] * el_t[pl.ds(2 * hp + hh, 1), :]
            u[rows, :] = v
            q = q + jnp.sum(v * v, axis=0, keepdims=True)
            e = e + jnp.sum(v * gain[part] * ct[rows, :].astype(F32), axis=0, keepdims=True)
        return q, e

    none = jnp.zeros((1, T2), F32)
    q, e = lax.fori_loop(0, PAIRS, readout, (none, none))
    scale = lax.rsqrt(q * (1.0 / D) + 1e-05)
    pull = scale * scale * scale * e * (1.0 / D)

    def normed(hp, c):
        base = pl.multiple_of(hp * 128, 128)
        gain = gains(hp)
        for hh in range(2):
            rows = pl.ds(pl.multiple_of(base + hh * 64, 64), 64)
            h = pl.ds(2 * hp + hh, 1)
            part = slice(hh * 64, hh * 64 + 64)
            v = u[rows, :]
            gs = gain[part] * scale
            back = gs * ct[rows, :].astype(F32) - v * pull
            vdu[rows, :] = (back * el_t[h, :]).astype(BF)
            back = back.astype(BF)
            du[rows, :] = back
            prow[h, :] = jnp.sum(back.astype(F32) * v, axis=0, keepdims=True)
            u[rows, :] = v * gs
        send_b[hp] = to_state(vdu[pl.ds(base, 128), :], bdc)
        return c

    lax.fori_loop(0, PAIRS, normed, 0)
    recv_b[me] = send_b[me]
    send_all(send_b, recv_b, sb, rb)
    dsc[...] = jnp.zeros_like(dsc)

    def backward(hp, c):
        for b in range(2):
            pair = []
            for hh in range(2):
                h = 2 * hp + hh
                rows = pl.ds(pl.multiple_of(h * 64, 64), 64)
                d = du[rows, halves[b]]
                g[rows, halves[b]] = dot(d, mst[b, h])
                pair.append(dot(d, xt_ref[rows, halves[b]], TN))
            for i, j in blocks[b]:
                acc = dsc[b, span(i), span(j)]
                for hh in range(2):
                    acc = acc + pair[hh][span(i), span(j)] * dec[
                        b, 2 * hp + hh, span(i), span(j)
                    ].astype(F32)
                dsc[b, span(i), span(j)] = acc
        return c

    lax.fori_loop(0, PAIRS // 2, backward, 0)
    recv_all(send_b, recv_b, sb, rb)
    chain(recv_b, send_b2, False)
    recv_b2[me] = send_b2[me]
    send_all(send_b2, recv_b2, sb2, rb2)
    lax.fori_loop(PAIRS // 2, PAIRS, backward, 0)

    for blk in range(8):
        y_rc = u[(7 - blk) * 256 : (8 - blk) * 256, ROWS:T2].astype(BF)
        y = u[blk * 256 : (blk + 1) * 256, 0:ROWS] + dot(flip, y_rc)
        mixed_ref[:, blk * 256 : (blk + 1) * 256] = y.astype(BF).T

    def read_maps(hp, acc):
        return acc + dot(recv_a2[hp], vdu[pl.ds(pl.multiple_of(hp * 128, 128), 128), :], TN)

    dc_state = lax.fori_loop(0, PAIRS, read_maps, jnp.zeros((128, T2), F32))

    recv_all(send_b2, recv_b2, sb2, rb2)

    def finish(hp, acc):
        base = pl.multiple_of(hp * 128, 128)
        after = recv_b2[hp]
        acc = acc + dot(after, wx[pl.ds(base, 128), :], TN)
        out = from_state(after, bdbt)
        meet = after.astype(F32) * recv_a2[hp].astype(F32)
        for hh in range(2):
            rows = pl.ds(pl.multiple_of(base + hh * 64, 64), 64)
            h = pl.ds(2 * hp + hh, 1)
            part = slice(hh * 64, hh * 64 + 64)
            asrow[h, :] = jnp.sum(meet[part], axis=0, keepdims=True)
            far = out[part] * weight[h, :]
            whole = g[rows, :] + far
            dxt_ref[rows, :] = whole.astype(BF)
            x = xt_ref[rows, :].astype(F32)
            qrow[h, :] = jnp.sum(x * whole, axis=0, keepdims=True)
            q2row[h, :] = jnp.sum(x * far, axis=0, keepdims=True)
        return acc

    db_state = lax.fori_loop(0, PAIRS, finish, jnp.zeros((128, T2), F32))

    met = asrow[...] * tot[...]
    neg_col = jnp.broadcast_to(neg_rate, (128, 128)).T[0:HEADS, 0:1]
    for b in range(2):
        lanes = halves[b]
        mine = low if b == 0 else jnp.logical_not(low)
        end_grad = jnp.sum(jnp.where(mine, met, 0.0), axis=1, keepdims=True) + jnp.sum(
            q2row[:, lanes], axis=1, keepdims=True
        )
        dl = prow[:, lanes] - qrow[:, lanes]
        da = dot_exact(dl, tri[b]) + end_grad
        zb = zt[:, lanes]
        small_e = jnp.exp(-jnp.abs(zb))
        sig = jnp.where(zb >= 0, 1.0, small_e) / (1.0 + small_e)
        ratio = jnp.where(zb < -20.0, 1.0, sig / step_t[:, lanes])
        dz = qrow[:, lanes] * ratio + da * neg_col * sig
        dxt_ref[D + 128 : D + 160, lanes] = dz.astype(BF)
        d_scores = jnp.where(causal[b], dsc[b], 0.0).astype(BF)
        part = slice(b * 64, b * 64 + 64)
        dc = dot(bdbt[part, lanes], d_scores, NT) + dc_state[part, lanes]
        db = dot(bdct[part, lanes], d_scores) + db_state[part, lanes]
        dxt_ref[D : D + 64, lanes] = db.astype(BF)
        dxt_ref[D + 64 : D + 128, lanes] = dc.astype(BF)

    dxt_ref[D + 160 : WIDE, :] = jnp.zeros((WIDE - D - 160, T2), BF)
    sent_all(send_a, recv_a, sa, ra)
    sent_all(send_a2, recv_a2, sa2, ra2)
    sent_all(send_b, recv_b, sb, rb)
    sent_all(send_b2, recv_b2, sb2, rb2)


def scan(xt, proj, cot, gain, log_rates, step_bias):
    vmem = pl.BlockSpec(memory_space=pltpu.VMEM)
    V = pltpu.VMEM
    slots = [V((PEERS, SLOT, 128), BF)] * 2 + [V((PEERS, 128, 128), BF)] * 6
    return pl.pallas_call(
        scan_kernel,
        in_specs=[vmem] * 6,
        out_specs=[vmem] * 2,
        out_shape=[
            jax.ShapeDtypeStruct((ROWS, D), BF),
            jax.ShapeDtypeStruct((WIDE, T2), BF),
        ],
        scratch_shapes=[
            V((8, 128), F32),
            V((HEADS, T2), F32),
            V((HEADS, T2), F32),
            V((HEADS, T2), F32),
            V((HEADS, T2), F32),
            V((2, ROWS, 128), F32),
            V((HEADS, T2), F32),
            V((T2, 256), BF),
            V((256, T2), BF),
            V((T2, 256), BF),
            V((256, T2), BF),
            V((2, ROWS, ROWS), F32),
            V((2, ROWS, ROWS), F32),
            V((D, T2), BF),
            V((D, T2), BF),
            V((D, T2), F32),
            V((D, T2), F32),
            V((D, T2), BF),
            V((D, T2), BF),
            V((2, HEADS, ROWS, ROWS), BF),
            V((2, HEADS, ROWS, ROWS), BF),
            V((HEADS, 128), F32),
            V((HEADS, T2), F32),
            V((HEADS, T2), F32),
            V((HEADS, T2), F32),
            V((HEADS, 128), F32),
        ]
        + slots
        + [V((PEERS, 128, 128), F32)]
        + [pltpu.SemaphoreType.DMA((PEERS,))] * 8,
        compiler_params=pltpu.CompilerParams(
            collective_id=0, has_side_effects=True, vmem_limit_bytes=60 * 2**20
        ),
        name="scan",
    )(xt, proj, cot, gain, log_rates, step_bias)


def grads_kernel(
    rt_ref, dx_ref, gx_ref, gs_ref,
    rt_in, dx_in, acc, buf1, in1, buf2, in2, buf3, in3, last, out_in,
    core_s, core_r, ss, rs, out_s, out_r,
):
    dp = lax.axis_index("dp")
    ctx = lax.axis_index("ctx")
    zz, x_hi = dp // 2, dp % 2
    yy, x_lo, core = ctx // 4, (ctx // 2) % 2, ctx % 2
    xx = x_hi * 2 + x_lo
    coords = {"z": zz, "y": yy, "x": xx}

    def at(axis, v):
        if axis == "z":
            return {"dp": v * 2 + x_hi, "ctx": ctx}
        if axis == "y":
            return {"dp": dp, "ctx": (v * 2 + x_lo) * 2 + core}
        return {"dp": zz * 2 + v // 2, "ctx": (yy * 2 + v % 2) * 2 + core}

    sibling = {"dp": dp, "ctx": yy * 4 + x_lo * 2 + (1 - core)}
    barrier = pltpu.get_barrier_semaphore()
    friends = [sibling]
    friends += [{"dp": (dp + k) % 8, "ctx": ctx} for k in range(1, 8)]
    friends += [at("y", (yy + k) % 4) for k in range(1, 4)]
    friends += [at("x", (xx + k) % 4) for k in (1, 3)]
    for friend in friends:
        pl.semaphore_signal(barrier, inc=1, device_id=friend, device_id_type=MESH)
    pl.semaphore_wait(barrier, len(friends))

    def to(friend, src, dst, ssem, rsem):
        return pltpu.make_async_remote_copy(
            src_ref=src, dst_ref=dst, send_sem=ssem, recv_sem=rsem,
            device_id=friend, device_id_type=MESH,
        )

    swaps = [to(sibling, rt_ref.at[:, 1 - core], rt_in, core_s.at[3], core_r.at[3])]
    swaps += [
        to(sibling, dx_ref.at[p], dx_in.at[p], core_s.at[p], core_r.at[p])
        for p in range(PARTS)
    ]
    for swap in swaps:
        swap.start()

    for p in range(PARTS):
        def own(jj, c, p=p):
            acc[p, jj] = dot(rt_ref[jj, core], dx_ref[p], NT)
            return c
        lax.fori_loop(0, 8, own, 0)

    orders = (("z", "y", "x"), ("y", "x", "z"), ("x", "z", "y"))
    stages = ((buf1, in1), (buf2, in2), (buf3, in3))

    def moves(p, stage):
        axis = orders[p][stage]
        here = coords[axis]
        buf, into = stages[stage]
        found = []
        for k in (2, 1, 3):
            v = (here + k) % 4

            def copy(slot, v=v):
                return to(
                    at(axis, v), buf.at[p, v], into.at[p, slot],
                    ss.at[p, stage, v], rs.at[p, stage, slot],
                )

            found.append((v, lambda copy=copy: copy(here), lambda copy=copy, v=v: copy(v)))
        return found

    def launch(p, stage):
        for v, out, back in moves(p, stage):
            out().start()

    def collect(p, stage):
        buf, into = stages[stage]
        found = moves(p, stage)
        for v, out, back in found:
            back().wait_recv()
        total = buf[p, coords[orders[p][stage]]].astype(F32)
        for v, out, back in found:
            total = total + into[p, v].astype(F32)
        return total

    swaps[0].wait_recv()
    for p in range(PARTS):
        swaps[1 + p].wait_recv()

        def both(jj, c, p=p):
            tile = (acc[p, jj] + dot(rt_in[jj], dx_in[p], NT)).astype(BF)
            y_to, x_lo_to = jj // 2, jj % 2
            for k in range(8):
                where = {"z": k // 2, "y": y_to, "x": (k % 2) * 2 + x_lo_to}
                a, b, d = (where[axis] for axis in orders[p])
                buf1[p, a, b, d] = tile[k * 16 : (k + 1) * 16]
            return c
        lax.fori_loop(0, 8, both, 0)
        launch(p, 0)

    for p in range(PARTS):
        found = moves(p, 0)
        for v, out, back in found:
            back().wait_recv()
        here = coords[orders[p][0]]

        def add(i, c, p=p, here=here, found=found):
            total = buf1[p, here, i].astype(F32)
            for v, out, back in found:
                total = total + in1[p, v, i].astype(F32)
            buf2[p, i] = total.astype(BF)
            return c
        lax.fori_loop(0, 4, add, 0)
        launch(p, 1)
    for p in range(PARTS):
        buf3[p] = collect(p, 1)
        launch(p, 2)
    for p in range(PARTS):
        last[:, p * COLS : (p + 1) * COLS] = collect(p, 2).astype(BF)

    shares = []
    for k in range(1, 8):
        j = (dp + k) % 8
        friend = {"dp": j, "ctx": ctx}
        out = to(friend, last, out_in.at[dp], out_s.at[j], out_r.at[dp])
        back = to(friend, last, out_in.at[j], out_s.at[j], out_r.at[j])
        out.start()
        shares.append((j, out, back))
    out_in[dp] = last[...]
    for j, out, back in shares:
        back.wait_recv()
    for k in range(8):
        piece = out_in[k].astype(F32)
        gx_ref[k * 16 : (k + 1) * 16, :] = piece[:, 0:D]
        gs_ref[k * 16 : (k + 1) * 16, :] = piece[:, D : D + 160]

    for swap in swaps:
        swap.wait_send()
    for p in range(PARTS):
        for stage in range(3):
            for v, out, back in moves(p, stage):
                out().wait_send()
    for j, out, back in shares:
        out.wait_send()


def grads(rt, dx):
    vmem = pl.BlockSpec(memory_space=pltpu.VMEM)
    V = pltpu.VMEM
    dma = pltpu.SemaphoreType.DMA
    return pl.pallas_call(
        grads_kernel,
        in_specs=[vmem] * 2,
        out_specs=[vmem] * 2,
        out_shape=[
            jax.ShapeDtypeStruct((128, D), F32),
            jax.ShapeDtypeStruct((128, 160), F32),
        ],
        scratch_shapes=[
            V((8, 128, T2), BF),
            V((PARTS, COLS, T2), BF),
            V((PARTS, 8, 128, COLS), F32),
            V((PARTS, 4, 4, 4, 16, COLS), BF),
            V((PARTS, 4, 4, 4, 16, COLS), BF),
            V((PARTS, 4, 4, 16, COLS), BF),
            V((PARTS, 4, 4, 16, COLS), BF),
            V((PARTS, 4, 16, COLS), F32),
            V((PARTS, 4, 16, COLS), F32),
            V((16, WIDE), BF),
            V((8, 16, WIDE), BF),
            dma((4,)),
            dma((4,)),
            dma((PARTS, 3, 4)),
            dma((PARTS, 3, 4)),
            dma((8,)),
            dma((8,)),
        ],
        compiler_params=pltpu.CompilerParams(
            collective_id=1, has_side_effects=True, vmem_limit_bytes=56 * 2**20
        ),
        name="grads",
    )(rt.reshape(8, 2, 128, T2), dx.reshape(PARTS, COLS, T2))


def shards(hidden, x_weight, state_weight, log_rates, step_bias, out_gain, cotangent):
    rt, xt, proj = project(hidden[0], x_weight, state_weight)
    mixed, dx = scan(
        xt, proj, cotangent[0], out_gain[None], log_rates[None], step_bias[None]
    )
    grad_x, grad_small = grads(rt, dx)
    return (mixed[None], grad_x, grad_small)


def solution(mesh):
    return jax.shard_map(
        shards,
        mesh=mesh,
        in_specs=(P("dp", "ctx", None), P(), P(), P(), P(), P(), P("dp", "ctx", None)),
        out_specs=(P("dp", "ctx", None), P("ctx", None), P("ctx", None)),
        check_vma=False,
    )
```

```python
import jax
import jax.numpy as jnp
from jax import lax
from jax.experimental import pallas as pl
from jax.experimental.pallas import tpu as pltpu
from jax.sharding import PartitionSpec as P

HEAD = 64
STATE = 64
D = 2048
ROWS = 256
T2 = 2 * ROWS
HEADS = 32
PAIRS = 16
PEERS = 16
SLOT = 144
WIDE = 2304
PARTS = 6
COLS = WIDE // PARTS
MESH = pl.DeviceIdType.MESH
BF = jnp.bfloat16
F32 = jnp.float32
LOG2E = 1.4426950408889634

NN = (((1,), (0,)), ((), ()))
NT = (((1,), (1,)), ((), ()))
TN = (((0,), (0,)), ((), ()))


def dot(a, b, dims=NN):
    return lax.dot_general(a, b, dims, preferred_element_type=F32)


def dot_exact(a, b, dims=NN):
    return lax.dot_general(
        a, b, dims, preferred_element_type=F32, precision=lax.Precision.HIGHEST
    )


def iota2(shape, dim):
    return lax.broadcasted_iota(jnp.int32, shape, dim)


def flip_matrix(n):
    return (iota2((n, n), 0) + iota2((n, n), 1) == n - 1).astype(F32).astype(BF)


def project_kernel(rows_ref, wx_ref, ws_ref, rt_ref, xt_ref, proj_ref, r_ref):
    step = pl.program_id(0)

    @pl.when(step == 0)
    def _():
        flip = flip_matrix(256)
        for blk in range(8):
            part = rows_ref[:, blk * 256 : (blk + 1) * 256]
            r_ref[0:ROWS, blk * 256 : (blk + 1) * 256] = part
            r_ref[ROWS:T2, (7 - blk) * 256 : (8 - blk) * 256] = dot(part, flip).astype(BF)
            across = part.T
            rt_ref[blk * 256 : (blk + 1) * 256, 0:ROWS] = across
            rt_ref[(7 - blk) * 256 : (8 - blk) * 256, ROWS:T2] = dot(flip, across).astype(BF)
        proj_ref[...] = jnp.zeros_like(proj_ref)
        proj_ref[:, 0:160] = dot(r_ref[...], ws_ref[...])

    xt_ref[...] = dot(r_ref[...], wx_ref[...]).astype(BF).T


def project(rows, x_weight, state_weight):
    cols = 256
    return pl.pallas_call(
        project_kernel,
        grid=(D // cols,),
        in_specs=[
            pl.BlockSpec((ROWS, D), lambda i: (0, 0)),
            pl.BlockSpec((D, cols), lambda i: (0, i)),
            pl.BlockSpec((D, 160), lambda i: (0, 0)),
        ],
        out_specs=[
            pl.BlockSpec((D, T2), lambda i: (0, 0)),
            pl.BlockSpec((cols, T2), lambda i: (i, 0)),
            pl.BlockSpec((T2, 256), lambda i: (0, 0)),
        ],
        out_shape=[
            jax.ShapeDtypeStruct((D, T2), BF),
            jax.ShapeDtypeStruct((D, T2), BF),
            jax.ShapeDtypeStruct((T2, 256), F32),
        ],
        scratch_shapes=[pltpu.VMEM((T2, D), BF)],
        compiler_params=pltpu.CompilerParams(vmem_limit_bytes=48 * 2**20),
        name="project",
    )(rows, x_weight, state_weight)


def scan_kernel(
    xt_ref, proj_ref, cot_ref, gain_ref, lr_ref, sb_ref,
    mixed_ref, dxt_ref,
    small, zt, step_t, weight, l2_t, l2_n, el_t, bdb, bdbt, bdc, bdct, scm, dsc,
    wx, ct, u, g, du, vdu, mst, dec, tot, prow, qrow, q2row, asrow,
    send_a, recv_a, send_a2, recv_a2, send_b, recv_b, send_b2, recv_b2, up,
    sa, ra, sa2, ra2, sb, rb, sb2, rb2,
):
    me = lax.axis_index("ctx")
    barrier = pltpu.get_barrier_semaphore()

    def greet(j, c):
        @pl.when(j != me)
        def _():
            pl.semaphore_signal(barrier, inc=1, device_id={"ctx": j}, device_id_type=MESH)
        return c

    lax.fori_loop(0, PEERS, greet, 0)

    def copy(src, dst, ssem, rsem, to, slot):
        return pltpu.make_async_remote_copy(
            src_ref=src.at[to], dst_ref=dst.at[slot], send_sem=ssem.at[to],
            recv_sem=rsem.at[slot], device_id={"ctx": to}, device_id_type=MESH,
        )

    def send_all(src, dst, ssem, rsem):
        def one(k, c):
            j = lax.rem(me + k, PEERS)
            copy(src, dst, ssem, rsem, j, me).start()
            return c
        lax.fori_loop(1, PEERS, one, 0)

    def recv_all(src, dst, ssem, rsem):
        def one(k, c):
            j = lax.rem(me + k, PEERS)
            copy(src, dst, ssem, rsem, j, j).wait_recv()
            return c
        lax.fori_loop(1, PEERS, one, 0)

    def sent_all(src, dst, ssem, rsem):
        def one(k, c):
            j = lax.rem(me + k, PEERS)
            copy(src, dst, ssem, rsem, j, me).wait_send()
            return c
        lax.fori_loop(1, PEERS, one, 0)

    low = iota2((1, 128), 1) < 64
    row_i = iota2((ROWS, ROWS), 0)
    col_i = iota2((ROWS, ROWS), 1)
    causal = (row_i >= col_i, row_i <= col_i)
    tri = [m.astype(F32) for m in causal]
    halves = (slice(0, ROWS), slice(ROWS, T2))

    small[...] = jnp.zeros_like(small)
    small[0:1, 0:HEADS] = -jnp.exp(lr_ref[...])
    small[1:2, 0:HEADS] = sb_ref[...]
    neg_rate = small[0:1, :]
    z = proj_ref[:, 128:256] + small[1:2, :]
    step_n = jnp.maximum(z, 0.0) + jnp.log1p(jnp.exp(-jnp.abs(z)))
    log_n = step_n * (neg_rate * LOG2E)
    zt[...] = z.T[0:HEADS]
    step_t[...] = step_n.T[0:HEADS]
    for b in range(2):
        l2 = dot_exact(tri[b], log_n[halves[b]])
        l2_n[b] = l2
        l2_t[:, halves[b]] = l2.T[0:HEADS]
    el_t[...] = jnp.exp2(l2_t[...])
    ends = (l2_t[:, ROWS - 1 : ROWS], l2_t[:, ROWS : ROWS + 1])
    tot[...] = jnp.exp2(jnp.where(low, ends[0], ends[1]))
    for b in range(2):
        weight[:, halves[b]] = step_t[:, halves[b]] * jnp.exp2(ends[b] - l2_t[:, halves[b]])

    both = proj_ref[:, 0:128]
    turned = pltpu.roll(both, 64, 1)
    own = (iota2((T2, 128), 0) < ROWS) == (iota2((T2, 128), 1) < 64)
    maps_b = jnp.where(low, both, turned)
    maps_c = jnp.where(low, turned, both)
    b_diag = jnp.where(own, maps_b, 0.0)
    c_diag = jnp.where(own, maps_c, 0.0)
    for full, by_rows, by_cols in ((b_diag, bdb, bdbt), (c_diag, bdc, bdct)):
        coarse = full.astype(BF).astype(F32)
        for k, term in enumerate((coarse, full - coarse)):
            by_rows[:, k * 128 : (k + 1) * 128] = term.astype(BF)
            by_cols[k * 128 : (k + 1) * 128, :] = term.T.astype(BF)

    def to_state(lhs, by_rows):
        out = dot(lhs, by_rows[...])
        return (out[:, 0:128] + out[:, 128:256]).astype(BF)

    def from_state(state, by_cols):
        return dot(jnp.concatenate([state, state], axis=1), by_cols[...])

    def local_end(hp, c):
        base = pl.multiple_of(hp * 128, 128)
        for hh in range(2):
            rows = pl.ds(pl.multiple_of(base + hh * 64, 64), 64)
            h = pl.ds(2 * hp + hh, 1)
            wx[rows, :] = (xt_ref[rows, :].astype(F32) * weight[h, :]).astype(BF)
        send_a[hp, 0:128, :] = to_state(wx[pl.ds(base, 128), :], bdb)
        t0 = tot[pl.ds(2 * hp, 1), :]
        t1 = tot[pl.ds(2 * hp + 1, 1), :]
        h0 = t0.astype(BF).astype(F32)
        h1 = t1.astype(BF).astype(F32)
        at = iota2((16, 128), 0)
        extra = jnp.where(at == 0, h0, jnp.where(at == 1, t0 - h0, jnp.where(at == 2, h1, t1 - h1)))
        send_a[hp, 128:144, :] = extra.astype(BF)
        return c

    lax.fori_loop(0, PAIRS, local_end, 0, unroll=4)
    recv_a[me] = send_a[me]
    pl.semaphore_wait(barrier, PEERS - 1)
    send_all(send_a, recv_a, sa, ra)

    for b in range(2):
        sc = dot_exact(
            jnp.where(low, maps_c[halves[b]], 0.0), maps_b[halves[b]], NT
        )
        scm[b] = jnp.where(causal[b], sc, 0.0)

    zero_half = jnp.zeros((128, 128), BF)
    blocks = (((0, 0), (1, 0), (1, 1)), ((0, 0), (0, 1), (1, 1)))

    def span(i):
        return slice(i * 128, (i + 1) * 128)

    def forward(hp, c):
        for hh in range(2):
            h = 2 * hp + hh
            rows = pl.ds(pl.multiple_of(h * 64, 64), 64)
            for b in range(2):
                column = pltpu.roll(l2_n[b], 128 - h, 1)[:, 0:1]
                line = l2_t[pl.ds(h, 1), halves[b]]
                size = step_t[pl.ds(h, 1), halves[b]]
                for i, j in blocks[b]:
                    d = jnp.exp2(jnp.minimum(column[span(i)] - line[:, span(j)], 0.0))
                    d = d * size[:, span(j)]
                    dec[b, h, span(i), span(j)] = d.astype(BF)
                    mst[b, h, span(i), span(j)] = (d * scm[b, span(i), span(j)]).astype(BF)
                mst[b, h, span(b), span(1 - b)] = zero_half
                u[rows, halves[b]] = dot(xt_ref[rows, halves[b]], mst[b, h], NT)
        return c

    def chain(recv, out, fwd_up):
        def totals(i):
            t = recv_a[i, 128:144, :].astype(F32)
            rows = iota2((128, 128), 0) < 64
            return jnp.where(rows, t[0:1] + t[1:2], t[2:3] + t[3:4])

        def climb(i, carry):
            up[i] = carry
            return totals(i) * carry + recv[i, 0:128, :].astype(F32)

        zero = jnp.zeros((128, 128), F32)
        lax.fori_loop(0, PEERS, climb, zero)

        def descend(k, carry):
            i = PEERS - 1 - k
            pick = low if fwd_up else jnp.logical_not(low)
            out[i] = jnp.where(pick, up[i], carry).astype(BF)
            return totals(i) * carry + recv[i, 0:128, :].astype(F32)

        lax.fori_loop(0, PEERS, descend, zero)

    lax.fori_loop(0, PAIRS // 2, forward, 0)
    recv_all(send_a, recv_a, sa, ra)
    chain(recv_a, send_a2, True)
    recv_a2[me] = send_a2[me]
    send_all(send_a2, recv_a2, sa2, ra2)
    lax.fori_loop(PAIRS // 2, PAIRS, forward, 0)

    flip = flip_matrix(256)
    for blk in range(8):
        turned_c = cot_ref[:, blk * 256 : (blk + 1) * 256].T
        ct[blk * 256 : (blk + 1) * 256, 0:ROWS] = turned_c
        ct[(7 - blk) * 256 : (8 - blk) * 256, ROWS:T2] = dot(flip, turned_c).astype(BF)

    recv_all(send_a2, recv_a2, sa2, ra2)

    def gains(hp):
        lane = pl.ds(pl.multiple_of(hp * 128, 128), 128)
        column = jnp.broadcast_to(gain_ref[:, lane], (128, 128)).T
        return jnp.concatenate([column] * 4, axis=1)

    def readout(hp, c):
        q, e = c
        base = pl.multiple_of(hp * 128, 128)
        out = from_state(recv_a2[hp], bdct)
        gain = gains(hp)
        for hh in range(2):
            rows = pl.ds(pl.multiple_of(base + hh * 64, 64), 64)
            part = slice(hh * 64, hh * 64 + 64)
            v = u[rows, :] + out[part] * el_t[pl.ds(2 * hp + hh, 1), :]
            u[rows, :] = v
            q = q + jnp.sum(v * v, axis=0, keepdims=True)
            e = e + jnp.sum(v * gain[part] * ct[rows, :].astype(F32), axis=0, keepdims=True)
        return q, e

    none = jnp.zeros((1, T2), F32)
    q, e = lax.fori_loop(0, PAIRS, readout, (none, none), unroll=4)
    scale = lax.rsqrt(q * (1.0 / D) + 1e-05)
    pull = scale * scale * scale * e * (1.0 / D)

    def normed(hp, c):
        base = pl.multiple_of(hp * 128, 128)
        gain = gains(hp)
        for hh in range(2):
            rows = pl.ds(pl.multiple_of(base + hh * 64, 64), 64)
            h = pl.ds(2 * hp + hh, 1)
            part = slice(hh * 64, hh * 64 + 64)
            v = u[rows, :]
            gs = gain[part] * scale
            back = gs * ct[rows, :].astype(F32) - v * pull
            vdu[rows, :] = (back * el_t[h, :]).astype(BF)
            back = back.astype(BF)
            du[rows, :] = back
            prow[h, :] = jnp.sum(back.astype(F32) * v, axis=0, keepdims=True)
            u[rows, :] = v * gs
        send_b[hp] = to_state(vdu[pl.ds(base, 128), :], bdc)
        return c

    lax.fori_loop(0, PAIRS, normed, 0, unroll=4)
    recv_b[me] = send_b[me]
    send_all(send_b, recv_b, sb, rb)
    dsc[...] = jnp.zeros_like(dsc)

    def backward(hp, c):
        for b in range(2):
            pair = []
            for hh in range(2):
                h = 2 * hp + hh
                rows = pl.ds(pl.multiple_of(h * 64, 64), 64)
                d = du[rows, halves[b]]
                g[rows, halves[b]] = dot(d, mst[b, h])
                pair.append(dot(d, xt_ref[rows, halves[b]], TN))
            for i, j in blocks[b]:
                acc = dsc[b, span(i), span(j)]
                for hh in range(2):
                    acc = acc + pair[hh][span(i), span(j)] * dec[
                        b, 2 * hp + hh, span(i), span(j)
                    ].astype(F32)
                dsc[b, span(i), span(j)] = acc
        return c

    lax.fori_loop(0, PAIRS // 2, backward, 0)
    recv_all(send_b, recv_b, sb, rb)
    chain(recv_b, send_b2, False)
    recv_b2[me] = send_b2[me]
    send_all(send_b2, recv_b2, sb2, rb2)
    lax.fori_loop(PAIRS // 2, PAIRS, backward, 0)

    for blk in range(8):
        y_rc = u[(7 - blk) * 256 : (8 - blk) * 256, ROWS:T2].astype(BF)
        y = u[blk * 256 : (blk + 1) * 256, 0:ROWS] + dot(flip, y_rc)
        mixed_ref[:, blk * 256 : (blk + 1) * 256] = y.astype(BF).T

    def read_maps(hp, acc):
        return acc + dot(recv_a2[hp], vdu[pl.ds(pl.multiple_of(hp * 128, 128), 128), :], TN)

    dc_state = lax.fori_loop(0, PAIRS, read_maps, jnp.zeros((128, T2), F32), unroll=4)

    recv_all(send_b2, recv_b2, sb2, rb2)

    def finish(hp, acc):
        base = pl.multiple_of(hp * 128, 128)
        after = recv_b2[hp]
        acc = acc + dot(after, wx[pl.ds(base, 128), :], TN)
        out = from_state(after, bdbt)
        meet = after.astype(F32) * recv_a2[hp].astype(F32)
        for hh in range(2):
            rows = pl.ds(pl.multiple_of(base + hh * 64, 64), 64)
            h = pl.ds(2 * hp + hh, 1)
            part = slice(hh * 64, hh * 64 + 64)
            asrow[h, :] = jnp.sum(meet[part], axis=0, keepdims=True)
            far = out[part] * weight[h, :]
            whole = g[rows, :] + far
            dxt_ref[rows, :] = whole.astype(BF)
            x = xt_ref[rows, :].astype(F32)
            qrow[h, :] = jnp.sum(x * whole, axis=0, keepdims=True)
            q2row[h, :] = jnp.sum(x * far, axis=0, keepdims=True)
        return acc

    db_state = lax.fori_loop(0, PAIRS, finish, jnp.zeros((128, T2), F32), unroll=4)

    met = asrow[...] * tot[...]
    neg_col = jnp.broadcast_to(neg_rate, (128, 128)).T[0:HEADS, 0:1]
    for b in range(2):
        lanes = halves[b]
        mine = low if b == 0 else jnp.logical_not(low)
        end_grad = jnp.sum(jnp.where(mine, met, 0.0), axis=1, keepdims=True) + jnp.sum(
            q2row[:, lanes], axis=1, keepdims=True
        )
        dl = prow[:, lanes] - qrow[:, lanes]
        da = dot_exact(dl, tri[b]) + end_grad
        zb = zt[:, lanes]
        small_e = jnp.exp(-jnp.abs(zb))
        sig = jnp.where(zb >= 0, 1.0, small_e) / (1.0 + small_e)
        ratio = jnp.where(zb < -20.0, 1.0, sig / step_t[:, lanes])
        dz = qrow[:, lanes] * ratio + da * neg_col * sig
        dxt_ref[D + 128 : D + 160, lanes] = dz.astype(BF)
        d_scores = jnp.where(causal[b], dsc[b], 0.0)
        part = slice(b * 64, b * 64 + 64)
        fine = slice(128 + b * 64, 192 + b * 64)
        own_b = bdbt[part, lanes].astype(F32) + bdbt[fine, lanes].astype(F32)
        own_c = bdct[part, lanes].astype(F32) + bdct[fine, lanes].astype(F32)
        dc = dot_exact(own_b, d_scores, NT) + dc_state[part, lanes]
        db = dot_exact(own_c, d_scores) + db_state[part, lanes]
        dxt_ref[D : D + 64, lanes] = db.astype(BF)
        dxt_ref[D + 64 : D + 128, lanes] = dc.astype(BF)

    dxt_ref[D + 160 : WIDE, :] = jnp.zeros((WIDE - D - 160, T2), BF)
    sent_all(send_a, recv_a, sa, ra)
    sent_all(send_a2, recv_a2, sa2, ra2)
    sent_all(send_b, recv_b, sb, rb)
    sent_all(send_b2, recv_b2, sb2, rb2)


def scan(xt, proj, cot, gain, log_rates, step_bias):
    vmem = pl.BlockSpec(memory_space=pltpu.VMEM)
    V = pltpu.VMEM
    slots = [V((PEERS, SLOT, 128), BF)] * 2 + [V((PEERS, 128, 128), BF)] * 6
    return pl.pallas_call(
        scan_kernel,
        in_specs=[vmem] * 6,
        out_specs=[vmem] * 2,
        out_shape=[
            jax.ShapeDtypeStruct((ROWS, D), BF),
            jax.ShapeDtypeStruct((WIDE, T2), BF),
        ],
        scratch_shapes=[
            V((8, 128), F32),
            V((HEADS, T2), F32),
            V((HEADS, T2), F32),
            V((HEADS, T2), F32),
            V((HEADS, T2), F32),
            V((2, ROWS, 128), F32),
            V((HEADS, T2), F32),
            V((T2, 256), BF),
            V((256, T2), BF),
            V((T2, 256), BF),
            V((256, T2), BF),
            V((2, ROWS, ROWS), F32),
            V((2, ROWS, ROWS), F32),
            V((D, T2), BF),
            V((D, T2), BF),
            V((D, T2), F32),
            V((D, T2), F32),
            V((D, T2), BF),
            V((D, T2), BF),
            V((2, HEADS, ROWS, ROWS), BF),
            V((2, HEADS, ROWS, ROWS), BF),
            V((HEADS, 128), F32),
            V((HEADS, T2), F32),
            V((HEADS, T2), F32),
            V((HEADS, T2), F32),
            V((HEADS, 128), F32),
        ]
        + slots
        + [V((PEERS, 128, 128), F32)]
        + [pltpu.SemaphoreType.DMA((PEERS,))] * 8,
        compiler_params=pltpu.CompilerParams(
            collective_id=0, has_side_effects=True, vmem_limit_bytes=60 * 2**20
        ),
        name="scan",
    )(xt, proj, cot, gain, log_rates, step_bias)


def grads_kernel(
    rt_ref, dx_ref, gx_ref, gs_ref,
    rt_in, dx_in, acc, buf1, in1, buf2, in2, buf3, in3, last0, last1, last2, out0, out1, out2,
    core_s, core_r, ss, rs, out_s, out_r,
):
    dp = lax.axis_index("dp")
    ctx = lax.axis_index("ctx")
    zz, x_hi = dp // 2, dp % 2
    yy, x_lo, core = ctx // 4, (ctx // 2) % 2, ctx % 2
    xx = x_hi * 2 + x_lo
    coords = {"z": zz, "y": yy, "x": xx}

    def at(axis, v):
        if axis == "z":
            return {"dp": v * 2 + x_hi, "ctx": ctx}
        if axis == "y":
            return {"dp": dp, "ctx": (v * 2 + x_lo) * 2 + core}
        return {"dp": zz * 2 + v // 2, "ctx": (yy * 2 + v % 2) * 2 + core}

    sibling = {"dp": dp, "ctx": yy * 4 + x_lo * 2 + (1 - core)}
    barrier = pltpu.get_barrier_semaphore()
    friends = [sibling]
    friends += [{"dp": (dp + k) % 8, "ctx": ctx} for k in range(1, 8)]
    friends += [at("y", (yy + k) % 4) for k in range(1, 4)]
    friends += [at("x", (xx + k) % 4) for k in (1, 3)]
    for friend in friends:
        pl.semaphore_signal(barrier, inc=1, device_id=friend, device_id_type=MESH)
    pl.semaphore_wait(barrier, len(friends))

    def to(friend, src, dst, ssem, rsem):
        return pltpu.make_async_remote_copy(
            src_ref=src, dst_ref=dst, send_sem=ssem, recv_sem=rsem,
            device_id=friend, device_id_type=MESH,
        )

    swaps = [to(sibling, rt_ref.at[:, 1 - core], rt_in, core_s.at[PARTS], core_r.at[PARTS])]
    swaps += [
        to(sibling, dx_ref.at[p], dx_in.at[p], core_s.at[p], core_r.at[p])
        for p in range(PARTS)
    ]
    for swap in swaps:
        swap.start()

    def own(p, c):
        acc[p] = dot(rt_ref[:, core].reshape(1024, T2), dx_ref[p], NT)
        return c

    lax.fori_loop(0, PARTS, own, 0)

    orders = (("z", "y", "x"), ("y", "x", "z"), ("x", "z", "y")) * 2
    stages = ((buf1, in1), (buf2, in2), (buf3, in3))

    def moves(p, stage):
        axis = orders[p][stage]
        here = coords[axis]
        buf, into = stages[stage]
        found = []
        for k in (2, 1, 3):
            v = (here + k) % 4

            def copy(slot, v=v):
                return to(
                    at(axis, v), buf.at[p, v], into.at[p, slot],
                    ss.at[p, stage, v], rs.at[p, stage, slot],
                )

            found.append((v, lambda copy=copy: copy(here), lambda copy=copy, v=v: copy(v)))
        return found

    def launch(p, stage):
        for v, out, back in moves(p, stage):
            out().start()

    def collect(p, stage):
        buf, into = stages[stage]
        found = moves(p, stage)
        for v, out, back in found:
            back().wait_recv()
        total = buf[p, coords[orders[p][stage]]].astype(F32)
        for v, out, back in found:
            total = total + into[p, v].astype(F32)
        return total

    swaps[0].wait_recv()
    for p in range(PARTS):
        swaps[1 + p].wait_recv()

        tile = (acc[p] + dot(rt_in[...].reshape(1024, T2), dx_in[p], NT)).astype(BF)
        for k in range(64):
            jj, m = k // 8, k % 8
            where = {"z": m // 2, "y": jj // 2, "x": (m % 2) * 2 + jj % 2}
            a, b, d = (where[axis] for axis in orders[p])
            buf1[p, a, b, d] = tile[k * 16 : (k + 1) * 16]
        launch(p, 0)

    def first(p):
        found = moves(p, 0)
        for v, out, back in found:
            back().wait_recv()
        here = coords[orders[p][0]]

        def add(i, c):
            total = buf1[p, here, i].astype(F32)
            for v, out, back in found:
                total = total + in1[p, v, i].astype(F32)
            buf2[p, i] = total.astype(BF)
            return c

        lax.fori_loop(0, 4, add, 0)
        launch(p, 1)

    def second(p):
        buf3[p] = collect(p, 1)
        launch(p, 2)

    half = PARTS // 2
    groups = (range(half), range(half, PARTS))
    shares = []

    def share(kind, src, dst):
        dst[dp] = src[...]
        for k in range(1, 8):
            j = (dp + k) % 8

            def copy(slot, j=j):
                return to(
                    {"dp": j, "ctx": ctx}, src, dst.at[slot],
                    out_s.at[kind, j], out_r.at[kind, slot],
                )

            copy(dp).start()
            shares.append((kind, j, lambda copy=copy: copy(dp), lambda copy=copy, j=j: copy(j)))

    for group in groups:
        for p in group:
            first(p)
    for group in groups:
        for p in group:
            second(p)
    for p in groups[0]:
        last0[:, p * COLS : (p + 1) * COLS] = collect(p, 2).astype(BF)
    share(0, last0, out0)
    for p in groups[1]:
        piece = collect(p, 2)
        at0 = (p - half) * COLS
        if p == PARTS - 1:
            last2[...] = piece[:, COLS - 256 :]
            piece = piece[:, : COLS - 256]
        last1[:, at0 : at0 + piece.shape[1]] = piece.astype(BF)
    share(2, last2, out2)
    share(1, last1, out1)

    def arrived(kind):
        for which, j, out, back in shares:
            if which == kind:
                back().wait_recv()

    edge = half * COLS
    for kind, dst in ((0, out0), (2, out2), (1, out1)):
        arrived(kind)
        for k in range(8):
            rows = slice(k * 16, (k + 1) * 16)
            if kind == 0:
                gx_ref[rows, 0:edge] = dst[k].astype(F32)
            elif kind == 1:
                gx_ref[rows, edge:D] = dst[k].astype(F32)
            else:
                gs_ref[rows, :] = dst[k][:, 0:160]

    for swap in swaps:
        swap.wait_send()
    for p in range(PARTS):
        for stage in range(3):
            for v, out, back in moves(p, stage):
                out().wait_send()
    for which, j, out, back in shares:
        out().wait_send()


def grads(rt, dx):
    vmem = pl.BlockSpec(memory_space=pltpu.VMEM)
    V = pltpu.VMEM
    dma = pltpu.SemaphoreType.DMA
    return pl.pallas_call(
        grads_kernel,
        in_specs=[vmem] * 2,
        out_specs=[vmem] * 2,
        out_shape=[
            jax.ShapeDtypeStruct((128, D), F32),
            jax.ShapeDtypeStruct((128, 160), F32),
        ],
        scratch_shapes=[
            V((8, 128, T2), BF),
            V((PARTS, COLS, T2), BF),
            V((PARTS, 1024, COLS), F32),
            V((PARTS, 4, 4, 4, 16, COLS), BF),
            V((PARTS, 4, 4, 4, 16, COLS), BF),
            V((PARTS, 4, 4, 16, COLS), BF),
            V((PARTS, 4, 4, 16, COLS), BF),
            V((PARTS, 4, 16, COLS), F32),
            V((PARTS, 4, 16, COLS), F32),
            V((16, WIDE // 2), BF),
            V((16, WIDE // 2 - 256), BF),
            V((16, 256), F32),
            V((8, 16, WIDE // 2), BF),
            V((8, 16, WIDE // 2 - 256), BF),
            V((8, 16, 256), F32),
            dma((PARTS + 1,)),
            dma((PARTS + 1,)),
            dma((PARTS, 3, 4)),
            dma((PARTS, 3, 4)),
            dma((3, 8)),
            dma((3, 8)),
        ],
        compiler_params=pltpu.CompilerParams(
            collective_id=1, has_side_effects=True, vmem_limit_bytes=56 * 2**20
        ),
        name="grads",
    )(rt.reshape(8, 2, 128, T2), dx.reshape(PARTS, COLS, T2))


def shards(hidden, x_weight, state_weight, log_rates, step_bias, out_gain, cotangent):
    rt, xt, proj = project(hidden[0], x_weight, state_weight)
    mixed, dx = scan(
        xt, proj, cotangent[0], out_gain[None], log_rates[None], step_bias[None]
    )
    grad_x, grad_small = grads(rt, dx)
    return (mixed[None], grad_x, grad_small)


def solution(mesh):
    return jax.shard_map(
        shards,
        mesh=mesh,
        in_specs=(P("dp", "ctx", None), P(), P(), P(), P(), P(), P("dp", "ctx", None)),
        out_specs=(P("dp", "ctx", None), P("ctx", None), P("ctx", None)),
        check_vma=False,
    )
```

```python
import jax
import jax.numpy as jnp
from jax import lax
from jax.experimental import pallas as pl
from jax.experimental.pallas import tpu as pltpu
from jax.sharding import PartitionSpec as P

HEAD = 64
STATE = 64
D = 2048
ROWS = 256
T2 = 2 * ROWS
HEADS = 32
PAIRS = 16
PEERS = 16
SLOT = 144
WIDE = 2304
COLS = 256
PARTS = WIDE // COLS
MESH = pl.DeviceIdType.MESH
BF = jnp.bfloat16
F32 = jnp.float32
LOG2E = 1.4426950408889634

NN = (((1,), (0,)), ((), ()))
NT = (((1,), (1,)), ((), ()))
TN = (((0,), (0,)), ((), ()))


def dot(a, b, dims=NN):
    return lax.dot_general(a, b, dims, preferred_element_type=F32)


def dot_exact(a, b, dims=NN):
    return lax.dot_general(
        a, b, dims, preferred_element_type=F32, precision=lax.Precision.HIGHEST
    )


def iota2(shape, dim):
    return lax.broadcasted_iota(jnp.int32, shape, dim)


def flip_matrix(n):
    return (iota2((n, n), 0) + iota2((n, n), 1) == n - 1).astype(F32).astype(BF)


def scan_kernel(
    rows_ref, w_hbm, wst_ref, cot_ref, gain_ref, lr_ref, sb_ref,
    mixed_ref, gx_ref, gs_ref,
    xt_ref, proj_ref, w_sem,
    small, zt, step_t, weight, l2_t, l2_n, el_t, bdb, bdbt, bdc, bdct, scm, dsc,
    wx, ct, u, g, du, vdu, mst, dec, tot, prow, qrow, q2row, asrow,
    send_a, recv_a, send_a2, recv_a2, send_b, recv_b, send_b2, recv_b2, up,
    rt_in, dx_in, in1, in2, buf3, in3, last, last2, outs, out2,
    sa, ra, sa2, ra2, sb, rb, sb2, rb2, core_s, core_r, ss, rs, out_s, out_r,
):
    me = lax.axis_index("ctx")
    dp = lax.axis_index("dp")
    chip, core = me // 2, me % 2
    zz, x_hi = dp // 2, dp % 2
    yy, x_lo = chip // 2, chip % 2
    xx = x_hi * 2 + x_lo
    coords = {"z": zz, "y": yy, "x": xx}
    sibling = {"dp": dp, "ctx": chip * 2 + (1 - core)}
    dx = du

    def at_axis(axis, v):
        if axis == "z":
            return {"dp": v * 2 + x_hi, "ctx": me}
        if axis == "y":
            return {"dp": dp, "ctx": (v * 2 + x_lo) * 2 + core}
        return {"dp": zz * 2 + v // 2, "ctx": (yy * 2 + v % 2) * 2 + core}

    def to(friend, src, dst, ssem, rsem):
        return pltpu.make_async_remote_copy(
            src_ref=src, dst_ref=dst, send_sem=ssem, recv_sem=rsem,
            device_id=friend, device_id_type=MESH,
        )

    barrier = pltpu.get_barrier_semaphore()

    def w_block(j):
        return pltpu.make_async_copy(
            w_hbm.at[:, pl.ds(pl.multiple_of(j * 256, 256), 256)],
            dec.at[pl.ds(pl.multiple_of(j * D, D), D), :],
            w_sem.at[j],
        )

    turns = [lax.rem(chip + k, 8) for k in range(8)]
    for j in turns:
        w_block(j).start()

    friends = [{"dp": dp, "ctx": (me + k) % PEERS} for k in range(1, PEERS)]
    friends += [{"dp": (dp + k) % 8, "ctx": me} for k in range(1, 8)]
    friends += [{"dp": zz * 2 + (1 - x_hi), "ctx": (yy * 2 + (1 - x_lo)) * 2 + core}]
    for friend in friends:
        pl.semaphore_signal(barrier, inc=1, device_id=friend, device_id_type=MESH)

    def copy(src, dst, ssem, rsem, peer, slot):
        return pltpu.make_async_remote_copy(
            src_ref=src.at[peer], dst_ref=dst.at[slot], send_sem=ssem.at[peer],
            recv_sem=rsem.at[slot], device_id={"dp": dp, "ctx": peer}, device_id_type=MESH,
        )

    def send_all(src, dst, ssem, rsem):
        def one(k, c):
            j = lax.rem(me + k, PEERS)
            copy(src, dst, ssem, rsem, j, me).start()
            return c
        lax.fori_loop(1, PEERS, one, 0)

    def recv_all(src, dst, ssem, rsem):
        def one(k, c):
            j = lax.rem(me + k, PEERS)
            copy(src, dst, ssem, rsem, j, j).wait_recv()
            return c
        lax.fori_loop(1, PEERS, one, 0)

    def sent_all(src, dst, ssem, rsem):
        def one(k, c):
            j = lax.rem(me + k, PEERS)
            copy(src, dst, ssem, rsem, j, me).wait_send()
            return c
        lax.fori_loop(1, PEERS, one, 0)

    low = iota2((1, 128), 1) < 64
    row_i = iota2((ROWS, ROWS), 0)
    col_i = iota2((ROWS, ROWS), 1)
    causal = (row_i >= col_i, row_i <= col_i)
    tri = [m.astype(F32) for m in causal]
    halves = (slice(0, ROWS), slice(ROWS, T2))

    flip = flip_matrix(256)
    for k in range(8):
        part = rows_ref[:, k * 256 : (k + 1) * 256]
        mst[k * T2 : k * T2 + ROWS, :] = part
        mst[(7 - k) * T2 + ROWS : (8 - k) * T2, :] = dot(part, flip).astype(BF)

    def both_rows():
        return jnp.concatenate([mst[k * T2 : (k + 1) * T2, :] for k in range(8)], axis=1)

    proj_ref[:, 160:256] = jnp.zeros((T2, 96), F32)
    proj_ref[:, 0:160] = dot(both_rows(), wst_ref[...], NT)
    small[...] = jnp.zeros_like(small)
    small[0:1, 0:HEADS] = -jnp.exp(lr_ref[...])
    small[1:2, 0:HEADS] = sb_ref[...]
    neg_rate = small[0:1, :]
    z = proj_ref[:, 128:256] + small[1:2, :]
    step_n = jnp.maximum(z, 0.0) + jnp.log1p(jnp.exp(-jnp.abs(z)))
    log_n = step_n * (neg_rate * LOG2E)
    zt[...] = z.T[0:HEADS]
    step_t[...] = step_n.T[0:HEADS]
    for b in range(2):
        l2 = dot_exact(tri[b], log_n[halves[b]])
        l2_n[b] = l2
        l2_t[:, halves[b]] = l2.T[0:HEADS]
    el_t[...] = jnp.exp2(l2_t[...])
    ends = (l2_t[:, ROWS - 1 : ROWS], l2_t[:, ROWS : ROWS + 1])
    tot[...] = jnp.exp2(jnp.where(low, ends[0], ends[1]))
    for b in range(2):
        weight[:, halves[b]] = step_t[:, halves[b]] * jnp.exp2(ends[b] - l2_t[:, halves[b]])

    both = proj_ref[:, 0:128]
    turned = pltpu.roll(both, 64, 1)
    own = (iota2((T2, 128), 0) < ROWS) == (iota2((T2, 128), 1) < 64)
    maps_b = jnp.where(low, both, turned)
    maps_c = jnp.where(low, turned, both)
    b_diag = jnp.where(own, maps_b, 0.0)
    c_diag = jnp.where(own, maps_c, 0.0)
    for full, by_rows, by_cols in ((b_diag, bdb, bdbt), (c_diag, bdc, bdct)):
        coarse = full.astype(BF).astype(F32)
        for k, term in enumerate((coarse, full - coarse)):
            by_rows[:, k * 128 : (k + 1) * 128] = term.astype(BF)
            by_cols[k * 128 : (k + 1) * 128, :] = term.T.astype(BF)

    def to_state(lhs, by_rows):
        out = dot(lhs, by_rows[...])
        return (out[:, 0:128] + out[:, 128:256]).astype(BF)

    def from_state(state, by_cols):
        return dot(jnp.concatenate([state, state], axis=1), by_cols[...])

    def local_end(hp, c):
        base = pl.multiple_of(hp * 128, 128)
        for hh in range(2):
            rows = pl.ds(pl.multiple_of(base + hh * 64, 64), 64)
            h = pl.ds(2 * hp + hh, 1)
            wx[rows, :] = (xt_ref[rows, :].astype(F32) * weight[h, :]).astype(BF)
        send_a[hp, 0:128, :] = to_state(wx[pl.ds(base, 128), :], bdb)
        t0 = tot[pl.ds(2 * hp, 1), :]
        t1 = tot[pl.ds(2 * hp + 1, 1), :]
        h0 = t0.astype(BF).astype(F32)
        h1 = t1.astype(BF).astype(F32)
        at = iota2((16, 128), 0)
        extra = jnp.where(at == 0, h0, jnp.where(at == 1, t0 - h0, jnp.where(at == 2, h1, t1 - h1)))
        send_a[hp, 128:144, :] = extra.astype(BF)
        return c

    def early(step, src, dst, ssem, rsem):
        def one(k, c):
            j = lax.rem(me + k, PEERS)
            step(j, 0)
            copy(src, dst, ssem, rsem, j, me).start()
            return c
        lax.fori_loop(1, PEERS, one, 0, unroll=5)
        step(me, 0)
        dst[me] = src[me]

    pl.semaphore_wait(barrier, len(friends))
    for k, j in enumerate(turns):
        w_block(j).wait()
        values = dot(both_rows(), dec[pl.ds(pl.multiple_of(j * D, D), D), :]).astype(BF)
        xt_ref[pl.ds(pl.multiple_of(j * 256, 256), 256), :] = values.T
        if k == 0:
            hp = sibling["ctx"]
            local_end(hp, 0)
            copy(send_a, recv_a, sa, ra, hp, me).start()
            local_end(me, 0)
            recv_a[me] = send_a[me]
        else:
            for hh in range(2):
                hp = 2 * j + hh
                local_end(hp, 0)
                copy(send_a, recv_a, sa, ra, hp, me).start()

    for b in range(2):
        sc = dot_exact(
            jnp.where(low, maps_c[halves[b]], 0.0), maps_b[halves[b]], NT
        )
        scm[b] = jnp.where(causal[b], sc, 0.0)

    zero_half = jnp.zeros((128, 128), BF)
    blocks = (((0, 0), (1, 0), (1, 1)), ((0, 0), (0, 1), (1, 1)))

    def span(i):
        return slice(i * 128, (i + 1) * 128)

    def tile(b, h, i, rows=128):
        return pl.ds(pl.multiple_of((b * HEADS + h) * ROWS + i * 128, 128), rows)

    def forward(hp, c):
        for hh in range(2):
            h = 2 * hp + hh
            rows = pl.ds(pl.multiple_of(h * 64, 64), 64)
            for b in range(2):
                column = pltpu.roll(l2_n[b], 128 - h, 1)[:, 0:1]
                line = l2_t[pl.ds(h, 1), halves[b]]
                size = step_t[pl.ds(h, 1), halves[b]]
                for i, j in blocks[b]:
                    d = jnp.exp2(jnp.minimum(column[span(i)] - line[:, span(j)], 0.0))
                    d = d * size[:, span(j)]
                    dec[tile(b, h, i), span(j)] = d.astype(BF)
                    mst[tile(b, h, i), span(j)] = (d * scm[b, span(i), span(j)]).astype(BF)
                mst[tile(b, h, b), span(1 - b)] = zero_half
                u[rows, halves[b]] = dot(xt_ref[rows, halves[b]], mst[tile(b, h, 0, ROWS), :], NT)
        return c

    def chain(recv, out, fwd_up):
        def totals(i):
            t = recv_a[i, 128:144, :].astype(F32)
            rows = iota2((128, 128), 0) < 64
            return jnp.where(rows, t[0:1] + t[1:2], t[2:3] + t[3:4])

        def climb(i, carry):
            up[i] = carry
            return totals(i) * carry + recv[i, 0:128, :].astype(F32)

        zero = jnp.zeros((128, 128), F32)
        lax.fori_loop(0, PEERS, climb, zero)

        def descend(k, carry):
            i = PEERS - 1 - k
            pick = low if fwd_up else jnp.logical_not(low)
            out[i] = jnp.where(pick, up[i], carry).astype(BF)
            return totals(i) * carry + recv[i, 0:128, :].astype(F32)

        lax.fori_loop(0, PEERS, descend, zero)

    lax.fori_loop(0, PAIRS // 2, forward, 0)
    recv_all(send_a, recv_a, sa, ra)
    chain(recv_a, send_a2, True)
    recv_a2[me] = send_a2[me]
    send_all(send_a2, recv_a2, sa2, ra2)
    lax.fori_loop(PAIRS // 2, PAIRS, forward, 0)

    for blk in range(8):
        turned_c = cot_ref[:, blk * 256 : (blk + 1) * 256].T
        flipped_c = dot(flip, turned_c).astype(BF)
        for hh in range(2):
            ct[blk, hh, :, 0:ROWS] = turned_c[hh * 128 : hh * 128 + 128]
            ct[7 - blk, hh, :, ROWS:T2] = flipped_c[hh * 128 : hh * 128 + 128]

    recv_all(send_a2, recv_a2, sa2, ra2)

    def gains(hp):
        lane = pl.ds(pl.multiple_of(hp * 128, 128), 128)
        column = jnp.broadcast_to(gain_ref[:, lane], (128, 128)).T
        return jnp.concatenate([column] * 4, axis=1)

    def readout(hp, c):
        q, e = c
        base = pl.multiple_of(hp * 128, 128)
        out = from_state(recv_a2[hp], bdct)
        gain = gains(hp)
        for hh in range(2):
            rows = pl.ds(pl.multiple_of(base + hh * 64, 64), 64)
            part = slice(hh * 64, hh * 64 + 64)
            v = u[rows, :] + out[part] * el_t[pl.ds(2 * hp + hh, 1), :]
            u[rows, :] = v
            q = q + jnp.sum(v * v, axis=0, keepdims=True)
            e = e + jnp.sum(v * gain[part] * ct[lax.div(hp, 2), lax.rem(hp, 2), part, :].astype(F32), axis=0, keepdims=True)
        return q, e

    none = jnp.zeros((1, T2), F32)
    q, e = lax.fori_loop(0, PAIRS, readout, (none, none), unroll=4)
    scale = lax.rsqrt(q * (1.0 / D) + 1e-05)
    pull = scale * scale * scale * e * (1.0 / D)

    def normed(hp, c):
        base = pl.multiple_of(hp * 128, 128)
        gain = gains(hp)
        for hh in range(2):
            rows = pl.ds(pl.multiple_of(base + hh * 64, 64), 64)
            h = pl.ds(2 * hp + hh, 1)
            part = slice(hh * 64, hh * 64 + 64)
            v = u[rows, :]
            gs = gain[part] * scale
            back = gs * ct[lax.div(hp, 2), lax.rem(hp, 2), part, :].astype(F32) - v * pull
            vdu[rows, :] = (back * el_t[h, :]).astype(BF)
            back = back.astype(BF)
            du[rows, :] = back
            prow[h, :] = jnp.sum(back.astype(F32) * v, axis=0, keepdims=True)
            u[rows, :] = v * gs
        send_b[hp] = to_state(vdu[pl.ds(base, 128), :], bdc)
        return c

    early(normed, send_b, recv_b, sb, rb)
    dsc[...] = jnp.zeros_like(dsc)

    def backward(hp, c):
        for b in range(2):
            pair = []
            for hh in range(2):
                h = 2 * hp + hh
                rows = pl.ds(pl.multiple_of(h * 64, 64), 64)
                d = du[rows, halves[b]]
                g[rows, halves[b]] = dot(d, mst[tile(b, h, 0, ROWS), :])
                pair.append(dot(d, xt_ref[rows, halves[b]], TN))
            for i, j in blocks[b]:
                acc = dsc[b, span(i), span(j)]
                for hh in range(2):
                    acc = acc + pair[hh][span(i), span(j)] * dec[
                        tile(b, 2 * hp + hh, i), span(j)
                    ].astype(F32)
                dsc[b, span(i), span(j)] = acc
        return c

    lax.fori_loop(0, PAIRS // 2, backward, 0)
    for blk in range(8):
        y_rc = u[(7 - blk) * 256 : (8 - blk) * 256, ROWS:T2].astype(BF)
        y = u[blk * 256 : (blk + 1) * 256, 0:ROWS] + dot(flip, y_rc)
        mixed_ref[:, blk * 256 : (blk + 1) * 256] = y.astype(BF).T

    def read_maps(hp, acc):
        return acc + dot(recv_a2[hp], vdu[pl.ds(pl.multiple_of(hp * 128, 128), 128), :], TN)

    dc_state = lax.fori_loop(0, PAIRS, read_maps, jnp.zeros((128, T2), F32), unroll=4)
    recv_all(send_b, recv_b, sb, rb)
    chain(recv_b, send_b2, False)
    recv_b2[me] = send_b2[me]
    send_all(send_b2, recv_b2, sb2, rb2)
    lax.fori_loop(PAIRS // 2, PAIRS, backward, 0)

    own_maps = []
    for b in range(2):
        lanes = halves[b]
        d_scores = jnp.where(causal[b], dsc[b], 0.0)
        part = slice(b * 64, b * 64 + 64)
        fine = slice(128 + b * 64, 192 + b * 64)
        own_b = bdbt[part, lanes].astype(F32) + bdbt[fine, lanes].astype(F32)
        own_c = bdct[part, lanes].astype(F32) + bdct[fine, lanes].astype(F32)
        dc = dot_exact(own_b, d_scores, NT) + dc_state[part, lanes]
        dx[D + 64 : D + 128, lanes] = dc.astype(BF)
        own_maps.append(dot_exact(own_c, d_scores))
    dx[D + 160 : WIDE, :] = jnp.zeros((WIDE - D - 160, T2), BF)
    for blk in range(8):
        across = rows_ref[:, blk * 256 : (blk + 1) * 256].T
        flipped = dot(flip, across).astype(BF)
        for hh in range(2):
            ct[blk, hh, :, 0:ROWS] = across[hh * 128 : hh * 128 + 128]
            ct[7 - blk, hh, :, ROWS:T2] = flipped[hh * 128 : hh * 128 + 128]
    rows_swap = to(sibling, ct.at[:, 1 - core], rt_in, core_s.at[PARTS], core_r.at[PARTS])
    rows_swap.start()

    def swap(p):
        return to(
            sibling, dx.at[pl.ds(p * COLS, COLS), :], dx_in.at[p], core_s.at[p], core_r.at[p]
        )

    recv_all(send_b2, recv_b2, sb2, rb2)

    def finish(hp, acc):
        base = pl.multiple_of(hp * 128, 128)
        after = recv_b2[hp]
        acc = acc + dot(after, wx[pl.ds(base, 128), :], TN)
        out = from_state(after, bdbt)
        meet = after.astype(F32) * recv_a2[hp].astype(F32)
        for hh in range(2):
            rows = pl.ds(pl.multiple_of(base + hh * 64, 64), 64)
            h = pl.ds(2 * hp + hh, 1)
            part = slice(hh * 64, hh * 64 + 64)
            asrow[h, :] = jnp.sum(meet[part], axis=0, keepdims=True)
            far = out[part] * weight[h, :]
            whole = g[rows, :] + far
            dx[rows, :] = whole.astype(BF)
            x = xt_ref[rows, :].astype(F32)
            qrow[h, :] = jnp.sum(x * whole, axis=0, keepdims=True)
            q2row[h, :] = jnp.sum(x * far, axis=0, keepdims=True)
        return acc

    db_state = jnp.zeros((128, T2), F32)
    for p in range(8):
        db_state = finish(2 * p + 1, finish(2 * p, db_state))
        swap(p).start()

    def small_part():
        met = asrow[...] * tot[...]
        neg_col = jnp.broadcast_to(neg_rate, (128, 128)).T[0:HEADS, 0:1]
        for b in range(2):
            lanes = halves[b]
            mine = low if b == 0 else jnp.logical_not(low)
            end_grad = jnp.sum(jnp.where(mine, met, 0.0), axis=1, keepdims=True) + jnp.sum(
                q2row[:, lanes], axis=1, keepdims=True
            )
            dl = prow[:, lanes] - qrow[:, lanes]
            da = dot_exact(dl, tri[b]) + end_grad
            zb = zt[:, lanes]
            small_e = jnp.exp(-jnp.abs(zb))
            sig = jnp.where(zb >= 0, 1.0, small_e) / (1.0 + small_e)
            ratio = jnp.where(zb < -20.0, 1.0, sig / step_t[:, lanes])
            dz = qrow[:, lanes] * ratio + da * neg_col * sig
            dx[D + 128 : D + 160, lanes] = dz.astype(BF)
            part = slice(b * 64, b * 64 + 64)
            db = own_maps[b] + db_state[part, lanes]
            dx[D : D + 64, lanes] = db.astype(BF)
        swap(8).start()

    orders = (("z", "y", "x"), ("y", "x", "z"), ("x", "z", "y")) * 3

    def moves(p, stage):
        axis = orders[p][stage]
        here = coords[axis]
        found = []
        for k in (2, 1, 3):
            v = (here + k) % 4

            def copy_out(slot, v=v):
                if stage == 0:
                    src, dst = dec.at[pl.ds(pl.multiple_of(p * 1024 + v * 256, 256), 256), :], in1
                elif stage == 1:
                    first_row = PARTS * 1024 + p * 256
                    src, dst = dec.at[pl.ds(pl.multiple_of(first_row + v * 64, 64), 64), :], in2
                else:
                    src, dst = buf3.at[p, v], in3
                return to(
                    at_axis(axis, v), src, dst.at[p, slot],
                    ss.at[p, stage, v], rs.at[p, stage, slot],
                )

            found.append((v, lambda c=copy_out: c(here), lambda c=copy_out, v=v: c(v)))
        return found

    def launch(p, stage):
        for v, out, back in moves(p, stage):
            out().start()

    def arrived(p, stage):
        found = moves(p, stage)
        for v, out, back in found:
            back().wait_recv()
        return [v for v, out, back in found], coords[orders[p][stage]]

    def gradient(p):
        swap(p).wait_recv()
        left = jnp.concatenate(
            [ct[:, core].reshape(1024, T2), rt_in[...].reshape(1024, T2)], axis=1
        )
        right = jnp.concatenate([dx[p * COLS : (p + 1) * COLS, :], dx_in[p]], axis=1)
        tile = dot(left, right, NT).astype(BF)
        for k in range(64):
            jj, m = k // 8, k % 8
            where = {"z": m // 2, "y": jj // 2, "x": (m % 2) * 2 + jj % 2}
            a, b, d = (where[axis] for axis in orders[p])
            first_row = p * 1024 + ((a * 4 + b) * 4 + d) * 16
            dec[first_row : first_row + 16, :] = tile[k * 16 : (k + 1) * 16]
        launch(p, 0)

    def first(p):
        peers, here = arrived(p, 0)
        mine = pl.ds(pl.multiple_of(p * 1024 + here * 256, 256), 256)
        total = dec[mine, :].astype(F32)
        for v in peers:
            total = total + in1[p, v].astype(F32)
        dec[PARTS * 1024 + p * 256 : PARTS * 1024 + (p + 1) * 256, :] = total.astype(BF)
        launch(p, 1)

    def second(p):
        peers, here = arrived(p, 1)
        mine = pl.ds(pl.multiple_of(PARTS * 1024 + p * 256 + here * 64, 64), 64)
        total = dec[mine, :].astype(F32)
        for v in peers:
            total = total + in2[p, v].astype(F32)
        for v in range(4):
            buf3[p, v] = total[v * 16 : (v + 1) * 16]
        launch(p, 2)

    def third(p):
        peers, here = arrived(p, 2)
        total = buf3[p, here]
        for v in peers:
            total = total + in3[p, v]
        return total

    shares = []

    def share(kind, src, dst):
        dst[dp] = src[...]
        for k in range(1, 8):
            j = (dp + k) % 8

            def copy_out(slot, j=j):
                return to(
                    {"dp": j, "ctx": me}, src, dst.at[slot],
                    out_s.at[kind, j], out_r.at[kind, slot],
                )

            copy_out(dp).start()
            shares.append((kind, lambda c=copy_out: c(dp), lambda c=copy_out, j=j: c(j)))

    def finals(group):
        for p in (3 * group, 3 * group + 1, 3 * group + 2):
            piece = third(p)
            if p == PARTS - 1:
                last2[...] = piece
                share(3, last2, out2)
            else:
                n = p - 3 * group
                last[group, :, n * COLS : (n + 1) * COLS] = piece.astype(BF)
        share(group, last.at[group], outs.at[group])

    last[2, :, 512:768] = jnp.zeros((16, 256), BF)
    rows_swap.wait_recv()
    for p in range(4):
        gradient(p)
    small_part()
    for p in range(4, PARTS):
        gradient(p)

    for p in range(0, 6):
        first(p)
    for p in range(0, 3):
        second(p)
    for p in range(6, 9):
        first(p)
    for p in range(3, 6):
        second(p)
    finals(0)
    for p in range(6, 9):
        second(p)
    finals(1)
    finals(2)

    def gathered(kind):
        for which, out, back in shares:
            if which == kind:
                back().wait_recv()

    for kind in (0, 1, 3, 2):
        gathered(kind)
        for k in range(8):
            rows = slice(k * 16, (k + 1) * 16)
            if kind == 3:
                gs_ref[:, rows] = out2[k].T[0:160]
            else:
                width = 768 if kind < 2 else 512
                cols = slice(kind * 768, kind * 768 + width)
                gx_ref[rows, cols] = outs[kind, k][:, 0:width].astype(F32)

    sent_all(send_a, recv_a, sa, ra)
    sent_all(send_a2, recv_a2, sa2, ra2)
    sent_all(send_b, recv_b, sb, rb)
    sent_all(send_b2, recv_b2, sb2, rb2)
    rows_swap.wait_send()
    for p in range(PARTS):
        swap(p).wait_send()
        for stage in range(3):
            for v, out, back in moves(p, stage):
                out().wait_send()
    for which, out, back in shares:
        out().wait_send()


def scan(rows, x_weight, small_weight, cot, gain, log_rates, step_bias):
    vmem = pl.BlockSpec(memory_space=pltpu.VMEM)
    V = pltpu.VMEM
    dma = pltpu.SemaphoreType.DMA
    slots = [V((PEERS, SLOT, 128), BF)] * 2 + [V((PEERS, 128, 128), BF)] * 6
    return pl.pallas_call(
        scan_kernel,
        in_specs=[vmem, pl.BlockSpec(memory_space=pl.ANY)] + [vmem] * 5,
        out_specs=[vmem] * 3,
        out_shape=[
            jax.ShapeDtypeStruct((ROWS, D), BF),
            jax.ShapeDtypeStruct((128, D), F32),
            jax.ShapeDtypeStruct((160, 128), F32),
        ],
        scratch_shapes=[
            V((D, T2), BF),
            V((T2, 256), F32),
            pltpu.SemaphoreType.DMA((8,)),
            V((8, 128), F32),
            V((HEADS, T2), F32),
            V((HEADS, T2), F32),
            V((HEADS, T2), F32),
            V((HEADS, T2), F32),
            V((2, ROWS, 128), F32),
            V((HEADS, T2), F32),
            V((T2, 256), BF),
            V((256, T2), BF),
            V((T2, 256), BF),
            V((256, T2), BF),
            V((2, ROWS, ROWS), F32),
            V((2, ROWS, ROWS), F32),
            V((D, T2), BF),
            V((8, 2, 128, T2), BF),
            V((D, T2), F32),
            V((D, T2), F32),
            V((WIDE, T2), BF),
            V((D, T2), BF),
            V((2 * HEADS * ROWS, ROWS), BF),
            V((2 * HEADS * ROWS, ROWS), BF),
            V((HEADS, 128), F32),
            V((HEADS, T2), F32),
            V((HEADS, T2), F32),
            V((HEADS, T2), F32),
            V((HEADS, 128), F32),
        ]
        + slots
        + [
            V((PEERS, 128, 128), F32),
            V((8, 128, T2), BF),
            V((PARTS, COLS, T2), BF),
            V((PARTS, 4, 256, COLS), BF),
            V((PARTS, 4, 64, COLS), BF),
            V((PARTS, 4, 16, COLS), F32),
            V((PARTS, 4, 16, COLS), F32),
            V((3, 16, 768), BF),
            V((16, 256), F32),
            V((3, 8, 16, 768), BF),
            V((8, 16, 256), F32),
        ]
        + [dma((PEERS,))] * 8
        + [
            dma((PARTS + 1,)),
            dma((PARTS + 1,)),
            dma((PARTS, 3, 4)),
            dma((PARTS, 3, 4)),
            dma((4, 8)),
            dma((4, 8)),
        ],
        compiler_params=pltpu.CompilerParams(
            collective_id=0, has_side_effects=True, vmem_limit_bytes=62 * 2**20
        ),
        name="layer",
    )(rows, x_weight, small_weight, cot, gain, log_rates, step_bias)


def shards(hidden, x_weight, state_weight, log_rates, step_bias, out_gain, cotangent):
    mixed, grad_x, grad_small = scan(
        hidden[0], x_weight, state_weight.T, cotangent[0],
        out_gain[None], log_rates[None], step_bias[None],
    )
    return (mixed[None], grad_x, grad_small.T)


def solution(mesh):
    return jax.shard_map(
        shards,
        mesh=mesh,
        in_specs=(P("dp", "ctx", None), P(), P(), P(), P(), P(), P("dp", "ctx", None)),
        out_specs=(P("dp", "ctx", None), P("ctx", None), P("ctx", None)),
        check_vma=False,
    )
```

```python
import jax
import jax.numpy as jnp
from jax import lax
from jax.experimental import pallas as pl
from jax.experimental.pallas import tpu as pltpu
from jax.sharding import PartitionSpec as P

HEAD = 64
STATE = 64
D = 2048
ROWS = 256
T2 = 2 * ROWS
HEADS = 32
PAIRS = 16
PEERS = 16
SLOT = 144
WIDE = 2304
COLS = 256
PARTS = WIDE // COLS
MESH = pl.DeviceIdType.MESH
BF = jnp.bfloat16
F32 = jnp.float32
LOG2E = 1.4426950408889634

NN = (((1,), (0,)), ((), ()))
NT = (((1,), (1,)), ((), ()))
TN = (((0,), (0,)), ((), ()))


def dot(a, b, dims=NN):
    return lax.dot_general(a, b, dims, preferred_element_type=F32)


def dot_exact(a, b, dims=NN):
    return lax.dot_general(
        a, b, dims, preferred_element_type=F32, precision=lax.Precision.HIGHEST
    )


def iota2(shape, dim):
    return lax.broadcasted_iota(jnp.int32, shape, dim)


def flip_matrix(n):
    return (iota2((n, n), 0) + iota2((n, n), 1) == n - 1).astype(F32).astype(BF)


def scan_kernel(
    rows_ref, w_hbm, wst_ref, cot_ref, gain_ref, lr_ref, sb_ref,
    mixed_ref, gx_ref, gs_ref,
    xt_ref, proj_ref, w_sem,
    small, zt, step_t, weight, l2_t, l2_n, el_t, bdb, bdbt, bdc, bdct, scm, dsc,
    wx, ct, u, g, du, vdu, mst, dec, tot, prow, qrow, q2row, asrow,
    send_a, recv_a, send_a2, recv_a2, send_b, recv_b, send_b2, recv_b2, up,
    rt_in, dx_in, in1, in2, buf3, in3, last, last2, outs, out2,
    sa, ra, sa2, ra2, sb, rb, sb2, rb2, core_s, core_r, ss, rs, out_s, out_r,
):
    me = lax.axis_index("ctx")
    dp = lax.axis_index("dp")
    chip, core = me // 2, me % 2
    zz, x_hi = dp // 2, dp % 2
    yy, x_lo = chip // 2, chip % 2
    xx = x_hi * 2 + x_lo
    coords = {"z": zz, "y": yy, "x": xx}
    sibling = {"dp": dp, "ctx": chip * 2 + (1 - core)}
    dx = du

    def at_axis(axis, v):
        if axis == "z":
            return {"dp": v * 2 + x_hi, "ctx": me}
        if axis == "y":
            return {"dp": dp, "ctx": (v * 2 + x_lo) * 2 + core}
        return {"dp": zz * 2 + v // 2, "ctx": (yy * 2 + v % 2) * 2 + core}

    def to(friend, src, dst, ssem, rsem):
        return pltpu.make_async_remote_copy(
            src_ref=src, dst_ref=dst, send_sem=ssem, recv_sem=rsem,
            device_id=friend, device_id_type=MESH,
        )

    barrier = pltpu.get_barrier_semaphore()

    def w_block(j):
        return pltpu.make_async_copy(
            w_hbm.at[:, pl.ds(pl.multiple_of(j * 256, 256), 256)],
            dec.at[pl.ds(pl.multiple_of(j * D, D), D), :],
            w_sem.at[j],
        )

    turns = [lax.rem(chip + k, 8) for k in range(8)]
    for j in turns:
        w_block(j).start()

    friends = [{"dp": dp, "ctx": (me + k) % PEERS} for k in range(1, PEERS)]
    friends += [{"dp": (dp + k) % 8, "ctx": me} for k in range(1, 8)]
    friends += [{"dp": zz * 2 + (1 - x_hi), "ctx": (yy * 2 + (1 - x_lo)) * 2 + core}]
    for friend in friends:
        pl.semaphore_signal(barrier, inc=1, device_id=friend, device_id_type=MESH)

    def copy(src, dst, ssem, rsem, peer, slot):
        return pltpu.make_async_remote_copy(
            src_ref=src.at[peer], dst_ref=dst.at[slot], send_sem=ssem.at[peer],
            recv_sem=rsem.at[slot], device_id={"dp": dp, "ctx": peer}, device_id_type=MESH,
        )

    def send_all(src, dst, ssem, rsem):
        def one(k, c):
            j = lax.rem(me + k, PEERS)
            copy(src, dst, ssem, rsem, j, me).start()
            return c
        lax.fori_loop(1, PEERS, one, 0)

    def recv_all(src, dst, ssem, rsem):
        def one(k, c):
            j = lax.rem(me + k, PEERS)
            copy(src, dst, ssem, rsem, j, j).wait_recv()
            return c
        lax.fori_loop(1, PEERS, one, 0)

    def sent_all(src, dst, ssem, rsem):
        def one(k, c):
            j = lax.rem(me + k, PEERS)
            copy(src, dst, ssem, rsem, j, me).wait_send()
            return c
        lax.fori_loop(1, PEERS, one, 0)

    low = iota2((1, 128), 1) < 64
    row_i = iota2((ROWS, ROWS), 0)
    col_i = iota2((ROWS, ROWS), 1)
    causal = (row_i >= col_i, row_i <= col_i)
    tri = [m.astype(F32) for m in causal]
    halves = (slice(0, ROWS), slice(ROWS, T2))

    flip = flip_matrix(256)
    for k in range(8):
        part = rows_ref[:, k * 256 : (k + 1) * 256]
        mst[k * T2 : k * T2 + ROWS, :] = part
        mst[(7 - k) * T2 + ROWS : (8 - k) * T2, :] = dot(part, flip).astype(BF)

    def both_rows():
        return jnp.concatenate([mst[k * T2 : (k + 1) * T2, :] for k in range(8)], axis=1)

    proj_ref[:, 160:256] = jnp.zeros((T2, 96), F32)
    proj_ref[:, 0:160] = dot(both_rows(), wst_ref[...], NT)
    small[...] = jnp.zeros_like(small)
    small[0:1, 0:HEADS] = -jnp.exp(lr_ref[...])
    small[1:2, 0:HEADS] = sb_ref[...]
    neg_rate = small[0:1, :]
    z = proj_ref[:, 128:256] + small[1:2, :]
    step_n = jnp.maximum(z, 0.0) + jnp.log1p(jnp.exp(-jnp.abs(z)))
    log_n = step_n * (neg_rate * LOG2E)
    zt[...] = z.T[0:HEADS]
    step_t[...] = step_n.T[0:HEADS]
    for b in range(2):
        l2 = dot_exact(tri[b], log_n[halves[b]])
        l2_n[b] = l2
        l2_t[:, halves[b]] = l2.T[0:HEADS]
    el_t[...] = jnp.exp2(l2_t[...])
    ends = (l2_t[:, ROWS - 1 : ROWS], l2_t[:, ROWS : ROWS + 1])
    tot[...] = jnp.exp2(jnp.where(low, ends[0], ends[1]))
    for b in range(2):
        weight[:, halves[b]] = step_t[:, halves[b]] * jnp.exp2(ends[b] - l2_t[:, halves[b]])

    both = proj_ref[:, 0:128]
    turned = pltpu.roll(both, 64, 1)
    own = (iota2((T2, 128), 0) < ROWS) == (iota2((T2, 128), 1) < 64)
    maps_b = jnp.where(low, both, turned)
    maps_c = jnp.where(low, turned, both)
    b_diag = jnp.where(own, maps_b, 0.0)
    c_diag = jnp.where(own, maps_c, 0.0)
    for full, by_rows, by_cols in ((b_diag, bdb, bdbt), (c_diag, bdc, bdct)):
        coarse = full.astype(BF).astype(F32)
        for k, term in enumerate((coarse, full - coarse)):
            by_rows[:, k * 128 : (k + 1) * 128] = term.astype(BF)
            by_cols[k * 128 : (k + 1) * 128, :] = term.T.astype(BF)

    def to_state(lhs, by_rows):
        out = dot(lhs, by_rows[...])
        return (out[:, 0:128] + out[:, 128:256]).astype(BF)

    def from_state(state, by_cols):
        return dot(jnp.concatenate([state, state], axis=1), by_cols[...])

    def local_end(hp, c):
        base = pl.multiple_of(hp * 128, 128)
        for hh in range(2):
            rows = pl.ds(pl.multiple_of(base + hh * 64, 64), 64)
            h = pl.ds(2 * hp + hh, 1)
            wx[rows, :] = (xt_ref[rows, :].astype(F32) * weight[h, :]).astype(BF)
        send_a[hp, 0:128, :] = to_state(wx[pl.ds(base, 128), :], bdb)
        t0 = tot[pl.ds(2 * hp, 1), :]
        t1 = tot[pl.ds(2 * hp + 1, 1), :]
        h0 = t0.astype(BF).astype(F32)
        h1 = t1.astype(BF).astype(F32)
        at = iota2((16, 128), 0)
        extra = jnp.where(at == 0, h0, jnp.where(at == 1, t0 - h0, jnp.where(at == 2, h1, t1 - h1)))
        send_a[hp, 128:144, :] = extra.astype(BF)
        return c

    def early(step, src, dst, ssem, rsem):
        def one(k, c):
            j = lax.rem(me + k, PEERS)
            step(j, 0)
            copy(src, dst, ssem, rsem, j, me).start()
            return c
        lax.fori_loop(1, PEERS, one, 0, unroll=5)
        step(me, 0)
        dst[me] = src[me]

    pl.semaphore_wait(barrier, len(friends))
    for k, j in enumerate(turns):
        w_block(j).wait()
        values = dot(both_rows(), dec[pl.ds(pl.multiple_of(j * D, D), D), :]).astype(BF)
        xt_ref[pl.ds(pl.multiple_of(j * 256, 256), 256), :] = values.T
        if k == 0:
            hp = sibling["ctx"]
            local_end(hp, 0)
            copy(send_a, recv_a, sa, ra, hp, me).start()
            local_end(me, 0)
            recv_a[me] = send_a[me]
        else:
            for hh in range(2):
                hp = 2 * j + hh
                local_end(hp, 0)
                copy(send_a, recv_a, sa, ra, hp, me).start()

    for b in range(2):
        sc = dot_exact(
            jnp.where(low, maps_c[halves[b]], 0.0), maps_b[halves[b]], NT
        )
        scm[b] = jnp.where(causal[b], sc, 0.0)

    zero_half = jnp.zeros((128, 128), BF)
    blocks = (((0, 0), (1, 0), (1, 1)), ((0, 0), (0, 1), (1, 1)))

    def span(i):
        return slice(i * 128, (i + 1) * 128)

    def tile(b, h, i, rows=128):
        return pl.ds(pl.multiple_of((b * HEADS + h) * ROWS + i * 128, 128), rows)

    def forward(hp, c):
        for hh in range(2):
            h = 2 * hp + hh
            rows = pl.ds(pl.multiple_of(h * 64, 64), 64)
            for b in range(2):
                column = pltpu.roll(l2_n[b], 128 - h, 1)[:, 0:1]
                line = l2_t[pl.ds(h, 1), halves[b]]
                size = step_t[pl.ds(h, 1), halves[b]]
                for i, j in blocks[b]:
                    d = jnp.exp2(jnp.minimum(column[span(i)] - line[:, span(j)], 0.0))
                    d = d * size[:, span(j)]
                    dec[tile(b, h, i), span(j)] = d.astype(BF)
                    mst[tile(b, h, i), span(j)] = (d * scm[b, span(i), span(j)]).astype(BF)
                mst[tile(b, h, b), span(1 - b)] = zero_half
                u[rows, halves[b]] = dot(xt_ref[rows, halves[b]], mst[tile(b, h, 0, ROWS), :], NT)
        return c

    def chain(recv, out, fwd_up):
        def totals(i):
            t = recv_a[i, 128:144, :].astype(F32)
            rows = iota2((128, 128), 0) < 64
            return jnp.where(rows, t[0:1] + t[1:2], t[2:3] + t[3:4])

        def climb(i, carry):
            up[i] = carry
            return totals(i) * carry + recv[i, 0:128, :].astype(F32)

        zero = jnp.zeros((128, 128), F32)
        lax.fori_loop(0, PEERS, climb, zero)

        def descend(k, carry):
            i = PEERS - 1 - k
            pick = low if fwd_up else jnp.logical_not(low)
            out[i] = jnp.where(pick, up[i], carry).astype(BF)
            return totals(i) * carry + recv[i, 0:128, :].astype(F32)

        lax.fori_loop(0, PEERS, descend, zero)

    lax.fori_loop(0, PAIRS // 4, forward, 0)
    recv_all(send_a, recv_a, sa, ra)
    chain(recv_a, send_a2, True)
    recv_a2[me] = send_a2[me]
    send_all(send_a2, recv_a2, sa2, ra2)
    lax.fori_loop(PAIRS // 4, PAIRS, forward, 0)

    for blk in range(8):
        turned_c = cot_ref[:, blk * 256 : (blk + 1) * 256].T
        flipped_c = dot(flip, turned_c).astype(BF)
        for hh in range(2):
            ct[blk, hh, :, 0:ROWS] = turned_c[hh * 128 : hh * 128 + 128]
            ct[7 - blk, hh, :, ROWS:T2] = flipped_c[hh * 128 : hh * 128 + 128]

    recv_all(send_a2, recv_a2, sa2, ra2)

    def gains(hp):
        lane = pl.ds(pl.multiple_of(hp * 128, 128), 128)
        column = jnp.broadcast_to(gain_ref[:, lane], (128, 128)).T
        return jnp.concatenate([column] * 4, axis=1)

    def readout(hp, c):
        q, e = c
        base = pl.multiple_of(hp * 128, 128)
        out = from_state(recv_a2[hp], bdct)
        gain = gains(hp)
        for hh in range(2):
            rows = pl.ds(pl.multiple_of(base + hh * 64, 64), 64)
            part = slice(hh * 64, hh * 64 + 64)
            v = u[rows, :] + out[part] * el_t[pl.ds(2 * hp + hh, 1), :]
            u[rows, :] = v
            q = q + jnp.sum(v * v, axis=0, keepdims=True)
            e = e + jnp.sum(v * gain[part] * ct[lax.div(hp, 2), lax.rem(hp, 2), part, :].astype(F32), axis=0, keepdims=True)
        return q, e

    none = jnp.zeros((1, T2), F32)
    q, e = lax.fori_loop(0, PAIRS, readout, (none, none), unroll=4)
    scale = lax.rsqrt(q * (1.0 / D) + 1e-05)
    pull = scale * scale * scale * e * (1.0 / D)

    def normed(hp, c):
        base = pl.multiple_of(hp * 128, 128)
        gain = gains(hp)
        for hh in range(2):
            rows = pl.ds(pl.multiple_of(base + hh * 64, 64), 64)
            h = pl.ds(2 * hp + hh, 1)
            part = slice(hh * 64, hh * 64 + 64)
            v = u[rows, :]
            gs = gain[part] * scale
            back = gs * ct[lax.div(hp, 2), lax.rem(hp, 2), part, :].astype(F32) - v * pull
            vdu[rows, :] = (back * el_t[h, :]).astype(BF)
            back = back.astype(BF)
            du[rows, :] = back
            prow[h, :] = jnp.sum(back.astype(F32) * v, axis=0, keepdims=True)
            u[rows, :] = v * gs
        send_b[hp] = to_state(vdu[pl.ds(base, 128), :], bdc)
        return c

    early(normed, send_b, recv_b, sb, rb)
    dsc[...] = jnp.zeros_like(dsc)

    def backward(hp, c):
        for b in range(2):
            pair = []
            for hh in range(2):
                h = 2 * hp + hh
                rows = pl.ds(pl.multiple_of(h * 64, 64), 64)
                d = du[rows, halves[b]]
                g[rows, halves[b]] = dot(d, mst[tile(b, h, 0, ROWS), :])
                pair.append(dot(d, xt_ref[rows, halves[b]], TN))
            for i, j in blocks[b]:
                acc = dsc[b, span(i), span(j)]
                for hh in range(2):
                    acc = acc + pair[hh][span(i), span(j)] * dec[
                        tile(b, 2 * hp + hh, i), span(j)
                    ].astype(F32)
                dsc[b, span(i), span(j)] = acc
        return c

    lax.fori_loop(0, PAIRS // 2, backward, 0)
    for blk in range(8):
        y_rc = u[(7 - blk) * 256 : (8 - blk) * 256, ROWS:T2].astype(BF)
        y = u[blk * 256 : (blk + 1) * 256, 0:ROWS] + dot(flip, y_rc)
        mixed_ref[:, blk * 256 : (blk + 1) * 256] = y.astype(BF).T

    def read_maps(hp, acc):
        return acc + dot(recv_a2[hp], vdu[pl.ds(pl.multiple_of(hp * 128, 128), 128), :], TN)

    dc_state = lax.fori_loop(0, PAIRS, read_maps, jnp.zeros((128, T2), F32), unroll=4)
    recv_all(send_b, recv_b, sb, rb)
    chain(recv_b, send_b2, False)
    recv_b2[me] = send_b2[me]
    send_all(send_b2, recv_b2, sb2, rb2)
    lax.fori_loop(PAIRS // 2, PAIRS, backward, 0)

    own_maps = []
    for b in range(2):
        lanes = halves[b]
        d_scores = jnp.where(causal[b], dsc[b], 0.0)
        part = slice(b * 64, b * 64 + 64)
        fine = slice(128 + b * 64, 192 + b * 64)
        own_b = bdbt[part, lanes].astype(F32) + bdbt[fine, lanes].astype(F32)
        own_c = bdct[part, lanes].astype(F32) + bdct[fine, lanes].astype(F32)
        dc = dot_exact(own_b, d_scores, NT) + dc_state[part, lanes]
        dx[D + 64 : D + 128, lanes] = dc.astype(BF)
        own_maps.append(dot_exact(own_c, d_scores))
    dx[D + 160 : WIDE, :] = jnp.zeros((WIDE - D - 160, T2), BF)
    for blk in range(8):
        across = rows_ref[:, blk * 256 : (blk + 1) * 256].T
        flipped = dot(flip, across).astype(BF)
        for hh in range(2):
            ct[blk, hh, :, 0:ROWS] = across[hh * 128 : hh * 128 + 128]
            ct[7 - blk, hh, :, ROWS:T2] = flipped[hh * 128 : hh * 128 + 128]
    rows_swap = to(sibling, ct.at[:, 1 - core], rt_in, core_s.at[PARTS], core_r.at[PARTS])
    rows_swap.start()

    def swap(p):
        return to(
            sibling, dx.at[pl.ds(p * COLS, COLS), :], dx_in.at[p], core_s.at[p], core_r.at[p]
        )

    recv_all(send_b2, recv_b2, sb2, rb2)

    def finish(hp, acc):
        base = pl.multiple_of(hp * 128, 128)
        after = recv_b2[hp]
        acc = acc + dot(after, wx[pl.ds(base, 128), :], TN)
        out = from_state(after, bdbt)
        meet = after.astype(F32) * recv_a2[hp].astype(F32)
        for hh in range(2):
            rows = pl.ds(pl.multiple_of(base + hh * 64, 64), 64)
            h = pl.ds(2 * hp + hh, 1)
            part = slice(hh * 64, hh * 64 + 64)
            asrow[h, :] = jnp.sum(meet[part], axis=0, keepdims=True)
            far = out[part] * weight[h, :]
            whole = g[rows, :] + far
            dx[rows, :] = whole.astype(BF)
            x = xt_ref[rows, :].astype(F32)
            qrow[h, :] = jnp.sum(x * whole, axis=0, keepdims=True)
            q2row[h, :] = jnp.sum(x * far, axis=0, keepdims=True)
        return acc


    def small_part(db_state):
        met = asrow[...] * tot[...]
        neg_col = jnp.broadcast_to(neg_rate, (128, 128)).T[0:HEADS, 0:1]
        for b in range(2):
            lanes = halves[b]
            mine = low if b == 0 else jnp.logical_not(low)
            end_grad = jnp.sum(jnp.where(mine, met, 0.0), axis=1, keepdims=True) + jnp.sum(
                q2row[:, lanes], axis=1, keepdims=True
            )
            dl = prow[:, lanes] - qrow[:, lanes]
            da = dot_exact(dl, tri[b]) + end_grad
            zb = zt[:, lanes]
            small_e = jnp.exp(-jnp.abs(zb))
            sig = jnp.where(zb >= 0, 1.0, small_e) / (1.0 + small_e)
            ratio = jnp.where(zb < -20.0, 1.0, sig / step_t[:, lanes])
            dz = qrow[:, lanes] * ratio + da * neg_col * sig
            dx[D + 128 : D + 160, lanes] = dz.astype(BF)
            part = slice(b * 64, b * 64 + 64)
            db = own_maps[b] + db_state[part, lanes]
            dx[D : D + 64, lanes] = db.astype(BF)
        swap(8).start()

    orders = (("z", "y", "x"), ("y", "x", "z"), ("x", "z", "y")) * 3

    def moves(p, stage):
        axis = orders[p][stage]
        here = coords[axis]
        found = []
        for k in (2, 1, 3):
            v = (here + k) % 4

            def copy_out(slot, v=v):
                if stage == 0:
                    src, dst = dec.at[pl.ds(pl.multiple_of(p * 1024 + v * 256, 256), 256), :], in1
                elif stage == 1:
                    first_row = PARTS * 1024 + p * 256
                    src, dst = dec.at[pl.ds(pl.multiple_of(first_row + v * 64, 64), 64), :], in2
                else:
                    src, dst = buf3.at[p, v], in3
                return to(
                    at_axis(axis, v), src, dst.at[p, slot],
                    ss.at[p, stage, v], rs.at[p, stage, slot],
                )

            found.append((v, lambda c=copy_out: c(here), lambda c=copy_out, v=v: c(v)))
        return found

    def launch(p, stage):
        for v, out, back in moves(p, stage):
            out().start()

    def arrived(p, stage):
        found = moves(p, stage)
        for v, out, back in found:
            back().wait_recv()
        return [v for v, out, back in found], coords[orders[p][stage]]

    def gradient(p):
        swap(p).wait_recv()
        left = jnp.concatenate(
            [ct[:, core].reshape(1024, T2), rt_in[...].reshape(1024, T2)], axis=1
        )
        right = jnp.concatenate([dx[p * COLS : (p + 1) * COLS, :], dx_in[p]], axis=1)
        tile = dot(left, right, NT).astype(BF)
        for k in range(64):
            jj, m = k // 8, k % 8
            where = {"z": m // 2, "y": jj // 2, "x": (m % 2) * 2 + jj % 2}
            a, b, d = (where[axis] for axis in orders[p])
            first_row = p * 1024 + ((a * 4 + b) * 4 + d) * 16
            dec[first_row : first_row + 16, :] = tile[k * 16 : (k + 1) * 16]
        launch(p, 0)

    def first(p):
        peers, here = arrived(p, 0)
        mine = pl.ds(pl.multiple_of(p * 1024 + here * 256, 256), 256)
        total = dec[mine, :].astype(F32)
        for v in peers:
            total = total + in1[p, v].astype(F32)
        dec[PARTS * 1024 + p * 256 : PARTS * 1024 + (p + 1) * 256, :] = total.astype(BF)
        launch(p, 1)

    def second(p):
        peers, here = arrived(p, 1)
        mine = pl.ds(pl.multiple_of(PARTS * 1024 + p * 256 + here * 64, 64), 64)
        total = dec[mine, :].astype(F32)
        for v in peers:
            total = total + in2[p, v].astype(F32)
        for v in range(4):
            buf3[p, v] = total[v * 16 : (v + 1) * 16]
        launch(p, 2)

    def third(p):
        peers, here = arrived(p, 2)
        total = buf3[p, here]
        for v in peers:
            total = total + in3[p, v]
        return total

    shares = []

    def share(kind, src, dst):
        dst[dp] = src[...]
        for k in range(1, 8):
            j = (dp + k) % 8

            def copy_out(slot, j=j):
                return to(
                    {"dp": j, "ctx": me}, src, dst.at[slot],
                    out_s.at[kind, j], out_r.at[kind, slot],
                )

            copy_out(dp).start()
            shares.append((kind, lambda c=copy_out: c(dp), lambda c=copy_out, j=j: c(j)))

    def finals(group):
        for p in (3 * group, 3 * group + 1, 3 * group + 2):
            piece = third(p)
            if p == PARTS - 1:
                last2[...] = piece
                share(3, last2, out2)
            else:
                n = p - 3 * group
                last[group, :, n * COLS : (n + 1) * COLS] = piece.astype(BF)
        share(group, last.at[group], outs.at[group])

    last[2, :, 512:768] = jnp.zeros((16, 256), BF)
    db_state = jnp.zeros((128, T2), F32)
    for p in range(8):
        db_state = finish(2 * p + 1, finish(2 * p, db_state))
        swap(p).start()
        if p == 2:
            rows_swap.wait_recv()
        if p >= 2:
            gradient(p - 2)
    small_part(db_state)
    for p in range(6, PARTS):
        gradient(p)

    sent_all(send_a, recv_a, sa, ra)
    sent_all(send_a2, recv_a2, sa2, ra2)
    sent_all(send_b, recv_b, sb, rb)
    sent_all(send_b2, recv_b2, sb2, rb2)
    for p in range(0, 6):
        first(p)
    for p in range(0, 3):
        second(p)
    for p in range(6, 9):
        first(p)
    for p in range(3, 6):
        second(p)
    finals(0)
    for p in range(6, 9):
        second(p)
    finals(1)
    finals(2)

    def gathered(kind):
        for which, out, back in shares:
            if which == kind:
                back().wait_recv()

    for kind in (0, 1, 3, 2):
        gathered(kind)
        for k in range(8):
            rows = slice(k * 16, (k + 1) * 16)
            if kind == 3:
                gs_ref[:, rows] = out2[k].T[0:160]
            else:
                width = 768 if kind < 2 else 512
                cols = slice(kind * 768, kind * 768 + width)
                gx_ref[rows, cols] = outs[kind, k][:, 0:width].astype(F32)

    rows_swap.wait_send()
    for p in range(PARTS):
        swap(p).wait_send()
        for stage in range(3):
            for v, out, back in moves(p, stage):
                out().wait_send()
    for which, out, back in shares:
        out().wait_send()


def scan(rows, x_weight, small_weight, cot, gain, log_rates, step_bias):
    vmem = pl.BlockSpec(memory_space=pltpu.VMEM)
    V = pltpu.VMEM
    dma = pltpu.SemaphoreType.DMA
    slots = [V((PEERS, SLOT, 128), BF)] * 2 + [V((PEERS, 128, 128), BF)] * 6
    return pl.pallas_call(
        scan_kernel,
        in_specs=[vmem, pl.BlockSpec(memory_space=pl.ANY)] + [vmem] * 5,
        out_specs=[vmem] * 3,
        out_shape=[
            jax.ShapeDtypeStruct((ROWS, D), BF),
            jax.ShapeDtypeStruct((128, D), F32),
            jax.ShapeDtypeStruct((160, 128), F32),
        ],
        scratch_shapes=[
            V((D, T2), BF),
            V((T2, 256), F32),
            pltpu.SemaphoreType.DMA((8,)),
            V((8, 128), F32),
            V((HEADS, T2), F32),
            V((HEADS, T2), F32),
            V((HEADS, T2), F32),
            V((HEADS, T2), F32),
            V((2, ROWS, 128), F32),
            V((HEADS, T2), F32),
            V((T2, 256), BF),
            V((256, T2), BF),
            V((T2, 256), BF),
            V((256, T2), BF),
            V((2, ROWS, ROWS), F32),
            V((2, ROWS, ROWS), F32),
            V((D, T2), BF),
            V((8, 2, 128, T2), BF),
            V((D, T2), F32),
            V((D, T2), F32),
            V((WIDE, T2), BF),
            V((D, T2), BF),
            V((2 * HEADS * ROWS, ROWS), BF),
            V((2 * HEADS * ROWS, ROWS), BF),
            V((HEADS, 128), F32),
            V((HEADS, T2), F32),
            V((HEADS, T2), F32),
            V((HEADS, T2), F32),
            V((HEADS, 128), F32),
        ]
        + slots
        + [
            V((PEERS, 128, 128), F32),
            V((8, 128, T2), BF),
            V((PARTS, COLS, T2), BF),
            V((PARTS, 4, 256, COLS), BF),
            V((PARTS, 4, 64, COLS), BF),
            V((PARTS, 4, 16, COLS), F32),
            V((PARTS, 4, 16, COLS), F32),
            V((3, 16, 768), BF),
            V((16, 256), F32),
            V((3, 8, 16, 768), BF),
            V((8, 16, 256), F32),
        ]
        + [dma((PEERS,))] * 8
        + [
            dma((PARTS + 1,)),
            dma((PARTS + 1,)),
            dma((PARTS, 3, 4)),
            dma((PARTS, 3, 4)),
            dma((4, 8)),
            dma((4, 8)),
        ],
        compiler_params=pltpu.CompilerParams(
            collective_id=0, has_side_effects=True, vmem_limit_bytes=62 * 2**20
        ),
        name="layer",
    )(rows, x_weight, small_weight, cot, gain, log_rates, step_bias)


def hand_on_kernel(*refs):
    half = len(refs) // 2
    sems = refs[-1]
    pairs = list(zip(refs[:half], refs[half : 2 * half]))
    moves = []
    for src, dst in pairs:
        rows = src.shape[0] // 4
        for k in range(4):
            part = pl.ds(k * rows, rows)
            moves.append((src.at[part, :], dst.at[part, :]))
    copies = [
        pltpu.make_async_copy(src, dst, sems.at[k]) for k, (src, dst) in enumerate(moves)
    ]
    for c in copies:
        c.start()
    for c in copies:
        c.wait()


def hand_on(*arrays):
    anywhere = pl.BlockSpec(memory_space=pl.ANY)
    return pl.pallas_call(
        hand_on_kernel,
        in_specs=[anywhere] * len(arrays),
        out_specs=[anywhere] * len(arrays),
        out_shape=[jax.ShapeDtypeStruct(a.shape, a.dtype) for a in arrays],
        scratch_shapes=[pltpu.SemaphoreType.DMA((4 * len(arrays),))],
        name="hand_on",
    )(*arrays)


def shards(hidden, x_weight, state_weight, log_rates, step_bias, out_gain, cotangent):
    mixed, grad_x, grad_small = hand_on(*scan(
        hidden[0], x_weight, state_weight.T, cotangent[0],
        out_gain[None], log_rates[None], step_bias[None],
    ))
    return (mixed[None], grad_x, grad_small.T)


def solution(mesh):
    return jax.shard_map(
        shards,
        mesh=mesh,
        in_specs=(P("dp", "ctx", None), P(), P(), P(), P(), P(), P("dp", "ctx", None)),
        out_specs=(P("dp", "ctx", None), P("ctx", None), P("ctx", None)),
        check_vma=False,
    )
```

```python
import jax
import jax.numpy as jnp
from jax import lax
from jax.experimental import pallas as pl
from jax.experimental.pallas import tpu as pltpu
from jax.sharding import PartitionSpec as P

HEAD = 64
STATE = 64
D = 2048
ROWS = 256
T2 = 2 * ROWS
HEADS = 32
PAIRS = 16
PEERS = 16
SLOT = 144
WIDE = 2304
COLS = 256
PARTS = WIDE // COLS
MESH = pl.DeviceIdType.MESH
BF = jnp.bfloat16
F32 = jnp.float32
LOG2E = 1.4426950408889634

NN = (((1,), (0,)), ((), ()))
NT = (((1,), (1,)), ((), ()))
TN = (((0,), (0,)), ((), ()))


def dot(a, b, dims=NN):
    return lax.dot_general(a, b, dims, preferred_element_type=F32)


def dot_exact(a, b, dims=NN):
    return lax.dot_general(
        a, b, dims, preferred_element_type=F32, precision=lax.Precision.HIGHEST
    )


def iota2(shape, dim):
    return lax.broadcasted_iota(jnp.int32, shape, dim)


def flip_matrix(n):
    return (iota2((n, n), 0) + iota2((n, n), 1) == n - 1).astype(F32).astype(BF)


def scan_kernel(
    rows_ref, w_hbm, wst_ref, cot_ref, gain_ref, lr_ref, sb_ref,
    mixed_ref, gx_ref, gs_ref,
    xt_ref, proj_ref, w_sem,
    small, zt, step_t, weight, l2_t, l2_n, el_t, bdb, bdbt, bdc, bdct, scm, dsc,
    wx, ct, u, g, du, vdu, mst, dec, tot, prow, qrow, q2row, asrow,
    send_a, recv_a, send_a2, recv_a2, send_b, recv_b, send_b2, recv_b2, up,
    rt_in, dx_in, in1, in2, buf3, in3, last0, last1, outs0, outs1,
    sa, ra, sa2, ra2, sb, rb, sb2, rb2, core_s, core_r, ss, rs, out_s, out_r,
):
    me = lax.axis_index("ctx")
    dp = lax.axis_index("dp")
    chip, core = me // 2, me % 2
    zz, x_hi = dp // 2, dp % 2
    yy, x_lo = chip // 2, chip % 2
    xx = x_hi * 2 + x_lo
    coords = {"z": zz, "y": yy, "x": xx}
    sibling = {"dp": dp, "ctx": chip * 2 + (1 - core)}
    dx = du

    def at_axis(axis, v):
        if axis == "z":
            return {"dp": v * 2 + x_hi, "ctx": me}
        if axis == "y":
            return {"dp": dp, "ctx": (v * 2 + x_lo) * 2 + core}
        return {"dp": zz * 2 + v // 2, "ctx": (yy * 2 + v % 2) * 2 + core}

    def to(friend, src, dst, ssem, rsem):
        return pltpu.make_async_remote_copy(
            src_ref=src, dst_ref=dst, send_sem=ssem, recv_sem=rsem,
            device_id=friend, device_id_type=MESH,
        )

    barrier = pltpu.get_barrier_semaphore()

    def w_block(j):
        return pltpu.make_async_copy(
            w_hbm.at[:, pl.ds(pl.multiple_of(j * 256, 256), 256)],
            dec.at[pl.ds(pl.multiple_of(j * D, D), D), :],
            w_sem.at[j],
        )

    turns = [lax.rem(chip + k, 8) for k in range(8)]
    for j in turns:
        w_block(j).start()

    friends = [{"dp": dp, "ctx": (me + k) % PEERS} for k in range(1, PEERS)]
    friends += [{"dp": (dp + k) % 8, "ctx": me} for k in range(1, 8)]
    friends += [{"dp": zz * 2 + (1 - x_hi), "ctx": (yy * 2 + (1 - x_lo)) * 2 + core}]
    for friend in friends:
        pl.semaphore_signal(barrier, inc=1, device_id=friend, device_id_type=MESH)

    def copy(src, dst, ssem, rsem, peer, slot):
        return pltpu.make_async_remote_copy(
            src_ref=src.at[peer], dst_ref=dst.at[slot], send_sem=ssem.at[peer],
            recv_sem=rsem.at[slot], device_id={"dp": dp, "ctx": peer}, device_id_type=MESH,
        )

    def send_all(src, dst, ssem, rsem):
        def one(k, c):
            j = lax.rem(me + k, PEERS)
            copy(src, dst, ssem, rsem, j, me).start()
            return c
        lax.fori_loop(1, PEERS, one, 0)

    def recv_all(src, dst, ssem, rsem):
        def one(k, c):
            j = lax.rem(me + k, PEERS)
            copy(src, dst, ssem, rsem, j, j).wait_recv()
            return c
        lax.fori_loop(1, PEERS, one, 0)

    def sent_all(src, dst, ssem, rsem):
        def one(k, c):
            j = lax.rem(me + k, PEERS)
            copy(src, dst, ssem, rsem, j, me).wait_send()
            return c
        lax.fori_loop(1, PEERS, one, 0)

    low = iota2((1, 128), 1) < 64
    row_i = iota2((ROWS, ROWS), 0)
    col_i = iota2((ROWS, ROWS), 1)
    causal = (row_i >= col_i, row_i <= col_i)
    tri = [m.astype(F32) for m in causal]
    halves = (slice(0, ROWS), slice(ROWS, T2))

    flip = flip_matrix(256)
    for k in range(8):
        part = rows_ref[:, k * 256 : (k + 1) * 256]
        mst[k * T2 : k * T2 + ROWS, :] = part
        mst[(7 - k) * T2 + ROWS : (8 - k) * T2, :] = dot(part, flip).astype(BF)

    def both_rows():
        return jnp.concatenate([mst[k * T2 : (k + 1) * T2, :] for k in range(8)], axis=1)

    proj_ref[:, 160:256] = jnp.zeros((T2, 96), F32)
    proj_ref[:, 0:160] = dot(both_rows(), wst_ref[...], NT)
    small[...] = jnp.zeros_like(small)
    small[0:1, 0:HEADS] = -jnp.exp(lr_ref[...])
    small[1:2, 0:HEADS] = sb_ref[...]
    neg_rate = small[0:1, :]
    z = proj_ref[:, 128:256] + small[1:2, :]
    step_n = jnp.maximum(z, 0.0) + jnp.log1p(jnp.exp(-jnp.abs(z)))
    log_n = step_n * (neg_rate * LOG2E)
    zt[...] = z.T[0:HEADS]
    step_t[...] = step_n.T[0:HEADS]
    for b in range(2):
        l2 = dot_exact(tri[b], log_n[halves[b]])
        l2_n[b] = l2
        l2_t[:, halves[b]] = l2.T[0:HEADS]
    el_t[...] = jnp.exp2(l2_t[...])
    ends = (l2_t[:, ROWS - 1 : ROWS], l2_t[:, ROWS : ROWS + 1])
    tot[...] = jnp.exp2(jnp.where(low, ends[0], ends[1]))
    for b in range(2):
        weight[:, halves[b]] = step_t[:, halves[b]] * jnp.exp2(ends[b] - l2_t[:, halves[b]])

    both = proj_ref[:, 0:128]
    turned = pltpu.roll(both, 64, 1)
    own = (iota2((T2, 128), 0) < ROWS) == (iota2((T2, 128), 1) < 64)
    maps_b = jnp.where(low, both, turned)
    maps_c = jnp.where(low, turned, both)
    b_diag = jnp.where(own, maps_b, 0.0)
    c_diag = jnp.where(own, maps_c, 0.0)
    for full, by_rows, by_cols in ((b_diag, bdb, bdbt), (c_diag, bdc, bdct)):
        coarse = full.astype(BF).astype(F32)
        for k, term in enumerate((coarse, full - coarse)):
            by_rows[:, k * 128 : (k + 1) * 128] = term.astype(BF)
            by_cols[k * 128 : (k + 1) * 128, :] = term.T.astype(BF)

    def to_state(lhs, by_rows):
        out = dot(lhs, by_rows[...])
        return (out[:, 0:128] + out[:, 128:256]).astype(BF)

    def from_state(state, by_cols):
        return dot(jnp.concatenate([state, state], axis=1), by_cols[...])

    def local_end(hp, c):
        base = pl.multiple_of(hp * 128, 128)
        for hh in range(2):
            rows = pl.ds(pl.multiple_of(base + hh * 64, 64), 64)
            h = pl.ds(2 * hp + hh, 1)
            wx[rows, :] = (xt_ref[rows, :].astype(F32) * weight[h, :]).astype(BF)
        send_a[hp, 0:128, :] = to_state(wx[pl.ds(base, 128), :], bdb)
        t0 = tot[pl.ds(2 * hp, 1), :]
        t1 = tot[pl.ds(2 * hp + 1, 1), :]
        h0 = t0.astype(BF).astype(F32)
        h1 = t1.astype(BF).astype(F32)
        at = iota2((16, 128), 0)
        extra = jnp.where(at == 0, h0, jnp.where(at == 1, t0 - h0, jnp.where(at == 2, h1, t1 - h1)))
        send_a[hp, 128:144, :] = extra.astype(BF)
        return c

    def early(step, src, dst, ssem, rsem):
        def one(k, c):
            j = lax.rem(me + k, PEERS)
            step(j, 0)
            copy(src, dst, ssem, rsem, j, me).start()
            return c
        lax.fori_loop(1, PEERS, one, 0, unroll=5)
        step(me, 0)
        dst[me] = src[me]

    pl.semaphore_wait(barrier, len(friends))
    for k, j in enumerate(turns):
        w_block(j).wait()
        values = dot(both_rows(), dec[pl.ds(pl.multiple_of(j * D, D), D), :]).astype(BF)
        xt_ref[pl.ds(pl.multiple_of(j * 256, 256), 256), :] = values.T
        if k == 0:
            hp = sibling["ctx"]
            local_end(hp, 0)
            copy(send_a, recv_a, sa, ra, hp, me).start()
            local_end(me, 0)
            recv_a[me] = send_a[me]
        else:
            for hh in range(2):
                hp = 2 * j + hh
                local_end(hp, 0)
                copy(send_a, recv_a, sa, ra, hp, me).start()

    for b in range(2):
        sc = dot_exact(
            jnp.where(low, maps_c[halves[b]], 0.0), maps_b[halves[b]], NT
        )
        scm[b] = jnp.where(causal[b], sc, 0.0)

    zero_half = jnp.zeros((128, 128), BF)
    blocks = (((0, 0), (1, 0), (1, 1)), ((0, 0), (0, 1), (1, 1)))

    def span(i):
        return slice(i * 128, (i + 1) * 128)

    def tile(b, h, i, rows=128):
        return pl.ds(pl.multiple_of((b * HEADS + h) * ROWS + i * 128, 128), rows)

    def forward(hp, c):
        for hh in range(2):
            h = 2 * hp + hh
            rows = pl.ds(pl.multiple_of(h * 64, 64), 64)
            for b in range(2):
                column = pltpu.roll(l2_n[b], 128 - h, 1)[:, 0:1]
                line = l2_t[pl.ds(h, 1), halves[b]]
                size = step_t[pl.ds(h, 1), halves[b]]
                for i, j in blocks[b]:
                    d = jnp.exp2(jnp.minimum(column[span(i)] - line[:, span(j)], 0.0))
                    d = d * size[:, span(j)]
                    dec[tile(b, h, i), span(j)] = d.astype(BF)
                    mst[tile(b, h, i), span(j)] = (d * scm[b, span(i), span(j)]).astype(BF)
                mst[tile(b, h, b), span(1 - b)] = zero_half
                u[rows, halves[b]] = dot(xt_ref[rows, halves[b]], mst[tile(b, h, 0, ROWS), :], NT)
        return c

    def chain(recv, out, fwd_up):
        def totals(i):
            t = recv_a[i, 128:144, :].astype(F32)
            rows = iota2((128, 128), 0) < 64
            return jnp.where(rows, t[0:1] + t[1:2], t[2:3] + t[3:4])

        def climb(i, carry):
            up[i] = carry
            return totals(i) * carry + recv[i, 0:128, :].astype(F32)

        zero = jnp.zeros((128, 128), F32)
        lax.fori_loop(0, PEERS, climb, zero)

        def descend(k, carry):
            i = PEERS - 1 - k
            pick = low if fwd_up else jnp.logical_not(low)
            out[i] = jnp.where(pick, up[i], carry).astype(BF)
            return totals(i) * carry + recv[i, 0:128, :].astype(F32)

        lax.fori_loop(0, PEERS, descend, zero)

    lax.fori_loop(0, PAIRS // 4, forward, 0)
    recv_all(send_a, recv_a, sa, ra)
    chain(recv_a, send_a2, True)
    recv_a2[me] = send_a2[me]
    send_all(send_a2, recv_a2, sa2, ra2)
    lax.fori_loop(PAIRS // 4, PAIRS, forward, 0)

    for blk in range(8):
        turned_c = cot_ref[:, blk * 256 : (blk + 1) * 256].T
        flipped_c = dot(flip, turned_c).astype(BF)
        for hh in range(2):
            ct[blk, hh, :, 0:ROWS] = turned_c[hh * 128 : hh * 128 + 128]
            ct[7 - blk, hh, :, ROWS:T2] = flipped_c[hh * 128 : hh * 128 + 128]

    recv_all(send_a2, recv_a2, sa2, ra2)

    def gains(hp):
        lane = pl.ds(pl.multiple_of(hp * 128, 128), 128)
        column = jnp.broadcast_to(gain_ref[:, lane], (128, 128)).T
        return jnp.concatenate([column] * 4, axis=1)

    def readout(hp, c):
        q, e = c
        base = pl.multiple_of(hp * 128, 128)
        out = from_state(recv_a2[hp], bdct)
        gain = gains(hp)
        for hh in range(2):
            rows = pl.ds(pl.multiple_of(base + hh * 64, 64), 64)
            part = slice(hh * 64, hh * 64 + 64)
            v = u[rows, :] + out[part] * el_t[pl.ds(2 * hp + hh, 1), :]
            u[rows, :] = v
            q = q + jnp.sum(v * v, axis=0, keepdims=True)
            e = e + jnp.sum(v * gain[part] * ct[lax.div(hp, 2), lax.rem(hp, 2), part, :].astype(F32), axis=0, keepdims=True)
        return q, e

    none = jnp.zeros((1, T2), F32)
    q, e = lax.fori_loop(0, PAIRS, readout, (none, none), unroll=4)
    scale = lax.rsqrt(q * (1.0 / D) + 1e-05)
    pull = scale * scale * scale * e * (1.0 / D)

    def normed(hp, c):
        base = pl.multiple_of(hp * 128, 128)
        gain = gains(hp)
        for hh in range(2):
            rows = pl.ds(pl.multiple_of(base + hh * 64, 64), 64)
            h = pl.ds(2 * hp + hh, 1)
            part = slice(hh * 64, hh * 64 + 64)
            v = u[rows, :]
            gs = gain[part] * scale
            back = gs * ct[lax.div(hp, 2), lax.rem(hp, 2), part, :].astype(F32) - v * pull
            vdu[rows, :] = (back * el_t[h, :]).astype(BF)
            back = back.astype(BF)
            du[rows, :] = back
            prow[h, :] = jnp.sum(back.astype(F32) * v, axis=0, keepdims=True)
            u[rows, :] = v * gs
        send_b[hp] = to_state(vdu[pl.ds(base, 128), :], bdc)
        return c

    early(normed, send_b, recv_b, sb, rb)
    dsc[...] = jnp.zeros_like(dsc)

    def backward(hp, c):
        for b in range(2):
            pair = []
            for hh in range(2):
                h = 2 * hp + hh
                rows = pl.ds(pl.multiple_of(h * 64, 64), 64)
                d = du[rows, halves[b]]
                g[rows, halves[b]] = dot(d, mst[tile(b, h, 0, ROWS), :])
                pair.append(dot(d, xt_ref[rows, halves[b]], TN))
            for i, j in blocks[b]:
                acc = dsc[b, span(i), span(j)]
                for hh in range(2):
                    acc = acc + pair[hh][span(i), span(j)] * dec[
                        tile(b, 2 * hp + hh, i), span(j)
                    ].astype(F32)
                dsc[b, span(i), span(j)] = acc
        return c

    lax.fori_loop(0, PAIRS // 2, backward, 0)
    for blk in range(8):
        y_rc = u[(7 - blk) * 256 : (8 - blk) * 256, ROWS:T2].astype(BF)
        y = u[blk * 256 : (blk + 1) * 256, 0:ROWS] + dot(flip, y_rc)
        mixed_ref[:, blk * 256 : (blk + 1) * 256] = y.astype(BF).T

    def read_maps(hp, acc):
        return acc + dot(recv_a2[hp], vdu[pl.ds(pl.multiple_of(hp * 128, 128), 128), :], TN)

    dc_state = lax.fori_loop(0, PAIRS, read_maps, jnp.zeros((128, T2), F32), unroll=4)
    recv_all(send_b, recv_b, sb, rb)
    chain(recv_b, send_b2, False)
    recv_b2[me] = send_b2[me]
    send_all(send_b2, recv_b2, sb2, rb2)
    lax.fori_loop(PAIRS // 2, PAIRS, backward, 0)

    own_maps = []
    for b in range(2):
        lanes = halves[b]
        d_scores = jnp.where(causal[b], dsc[b], 0.0)
        part = slice(b * 64, b * 64 + 64)
        fine = slice(128 + b * 64, 192 + b * 64)
        own_b = bdbt[part, lanes].astype(F32) + bdbt[fine, lanes].astype(F32)
        own_c = bdct[part, lanes].astype(F32) + bdct[fine, lanes].astype(F32)
        dc = dot_exact(own_b, d_scores, NT) + dc_state[part, lanes]
        dx[D + 64 : D + 128, lanes] = dc.astype(BF)
        own_maps.append(dot_exact(own_c, d_scores))
    dx[D + 160 : WIDE, :] = jnp.zeros((WIDE - D - 160, T2), BF)
    for blk in range(8):
        across = rows_ref[:, blk * 256 : (blk + 1) * 256].T
        flipped = dot(flip, across).astype(BF)
        for hh in range(2):
            ct[blk, hh, :, 0:ROWS] = across[hh * 128 : hh * 128 + 128]
            ct[7 - blk, hh, :, ROWS:T2] = flipped[hh * 128 : hh * 128 + 128]
    rows_swap = to(sibling, ct.at[:, 1 - core], rt_in, core_s.at[PARTS], core_r.at[PARTS])
    rows_swap.start()

    def swap(p):
        return to(
            sibling, dx.at[pl.ds(p * COLS, COLS), :], dx_in.at[p], core_s.at[p], core_r.at[p]
        )

    recv_all(send_b2, recv_b2, sb2, rb2)

    def finish(hp, acc):
        base = pl.multiple_of(hp * 128, 128)
        after = recv_b2[hp]
        acc = acc + dot(after, wx[pl.ds(base, 128), :], TN)
        out = from_state(after, bdbt)
        meet = after.astype(F32) * recv_a2[hp].astype(F32)
        for hh in range(2):
            rows = pl.ds(pl.multiple_of(base + hh * 64, 64), 64)
            h = pl.ds(2 * hp + hh, 1)
            part = slice(hh * 64, hh * 64 + 64)
            asrow[h, :] = jnp.sum(meet[part], axis=0, keepdims=True)
            far = out[part] * weight[h, :]
            whole = g[rows, :] + far
            dx[rows, :] = whole.astype(BF)
            x = xt_ref[rows, :].astype(F32)
            qrow[h, :] = jnp.sum(x * whole, axis=0, keepdims=True)
            q2row[h, :] = jnp.sum(x * far, axis=0, keepdims=True)
        return acc


    def small_part(db_state):
        met = asrow[...] * tot[...]
        neg_col = jnp.broadcast_to(neg_rate, (128, 128)).T[0:HEADS, 0:1]
        for b in range(2):
            lanes = halves[b]
            mine = low if b == 0 else jnp.logical_not(low)
            end_grad = jnp.sum(jnp.where(mine, met, 0.0), axis=1, keepdims=True) + jnp.sum(
                q2row[:, lanes], axis=1, keepdims=True
            )
            dl = prow[:, lanes] - qrow[:, lanes]
            da = dot_exact(dl, tri[b]) + end_grad
            zb = zt[:, lanes]
            small_e = jnp.exp(-jnp.abs(zb))
            sig = jnp.where(zb >= 0, 1.0, small_e) / (1.0 + small_e)
            ratio = jnp.where(zb < -20.0, 1.0, sig / step_t[:, lanes])
            dz = qrow[:, lanes] * ratio + da * neg_col * sig
            dx[D + 128 : D + 160, lanes] = dz.astype(BF)
            part = slice(b * 64, b * 64 + 64)
            db = own_maps[b] + db_state[part, lanes]
            dx[D : D + 64, lanes] = db.astype(BF)
        swap(8).start()

    orders = (("z", "y", "x"), ("y", "x", "z"), ("x", "z", "y")) * 3

    def moves(p, stage):
        axis = orders[p][stage]
        here = coords[axis]
        found = []
        for k in (2, 1, 3):
            v = (here + k) % 4

            def copy_out(slot, v=v):
                if stage == 0:
                    src, dst = dec.at[pl.ds(pl.multiple_of(p * 1024 + v * 256, 256), 256), :], in1
                elif stage == 1:
                    first_row = PARTS * 1024 + p * 256
                    src, dst = dec.at[pl.ds(pl.multiple_of(first_row + v * 64, 64), 64), :], in2
                else:
                    src, dst = buf3.at[p, v], in3
                return to(
                    at_axis(axis, v), src, dst.at[p, slot],
                    ss.at[p, stage, v], rs.at[p, stage, slot],
                )

            found.append((v, lambda c=copy_out: c(here), lambda c=copy_out, v=v: c(v)))
        return found

    def launch(p, stage):
        for v, out, back in moves(p, stage):
            out().start()

    def arrived(p, stage):
        found = moves(p, stage)
        for v, out, back in found:
            back().wait_recv()
        return [v for v, out, back in found], coords[orders[p][stage]]

    def gradient(p):
        swap(p).wait_recv()
        left = jnp.concatenate(
            [ct[:, core].reshape(1024, T2), rt_in[...].reshape(1024, T2)], axis=1
        )
        right = jnp.concatenate([dx[p * COLS : (p + 1) * COLS, :], dx_in[p]], axis=1)
        tile = dot(left, right, NT).astype(BF)
        for k in range(64):
            jj, m = k // 8, k % 8
            where = {"z": m // 2, "y": jj // 2, "x": (m % 2) * 2 + jj % 2}
            a, b, d = (where[axis] for axis in orders[p])
            first_row = p * 1024 + ((a * 4 + b) * 4 + d) * 16
            dec[first_row : first_row + 16, :] = tile[k * 16 : (k + 1) * 16]
        launch(p, 0)

    def first(p):
        peers, here = arrived(p, 0)
        mine = pl.ds(pl.multiple_of(p * 1024 + here * 256, 256), 256)
        total = dec[mine, :].astype(F32)
        for v in peers:
            total = total + in1[p, v].astype(F32)
        dec[PARTS * 1024 + p * 256 : PARTS * 1024 + (p + 1) * 256, :] = total.astype(BF)
        launch(p, 1)

    def second(p):
        peers, here = arrived(p, 1)
        mine = pl.ds(pl.multiple_of(PARTS * 1024 + p * 256 + here * 64, 64), 64)
        total = dec[mine, :].astype(F32)
        for v in peers:
            total = total + in2[p, v].astype(F32)
        for v in range(4):
            buf3[p, v] = total[v * 16 : (v + 1) * 16]
        launch(p, 2)

    def third(p):
        peers, here = arrived(p, 2)
        total = buf3[p, here]
        for v in peers:
            total = total + in3[p, v]
        return total

    shares = []

    def share(kind, src, dst):
        dst[dp] = src[...]
        for k in range(1, 8):
            j = (dp + k) % 8

            def copy_out(slot, j=j):
                return to(
                    {"dp": j, "ctx": me}, src, dst.at[slot],
                    out_s.at[kind, j], out_r.at[kind, slot],
                )

            copy_out(dp).start()
            shares.append((kind, lambda c=copy_out: c(dp), lambda c=copy_out, j=j: c(j)))

    def finals(parts):
        for p in parts:
            piece = third(p)
            whole = piece.astype(BF)
            if p < 6:
                last0[:, p * COLS : (p + 1) * COLS] = whole
            else:
                last1[:, (p - 6) * COLS : (p - 5) * COLS] = whole
            if p == PARTS - 1:
                last1[:, 3 * COLS : 4 * COLS] = (piece - whole.astype(F32)).astype(BF)

    db_state = jnp.zeros((128, T2), F32)
    for p in range(8):
        db_state = finish(2 * p + 1, finish(2 * p, db_state))
        swap(p).start()
        if p == 2:
            rows_swap.wait_recv()
        if p >= 2:
            gradient(p - 2)
    small_part(db_state)
    for p in range(6, PARTS):
        gradient(p)

    sent_all(send_a, recv_a, sa, ra)
    sent_all(send_a2, recv_a2, sa2, ra2)
    sent_all(send_b, recv_b, sb, rb)
    sent_all(send_b2, recv_b2, sb2, rb2)
    for p in range(0, 6):
        first(p)
    for p in range(0, 3):
        second(p)
    for p in range(6, 9):
        first(p)
    for p in range(3, 6):
        second(p)
    for p in range(6, 9):
        second(p)
    finals(range(0, 6))
    share(0, last0, outs0)
    finals(range(6, 9))
    share(1, last1, outs1)

    def gathered(kind):
        for which, out, back in shares:
            if which == kind:
                back().wait_recv()

    gathered(0)
    for k in range(8):
        gx_ref[k * 16 : (k + 1) * 16, 0:1536] = outs0[k].astype(F32)
    gathered(1)
    for k in range(8):
        rows = slice(k * 16, (k + 1) * 16)
        gx_ref[rows, 1536:D] = outs1[k, :, 0:512].astype(F32)
        narrow = outs1[k, :, 512:768].astype(F32) + outs1[k, :, 768:1024].astype(F32)
        gs_ref[:, rows] = narrow.T[0:160]

    rows_swap.wait_send()
    for p in range(PARTS):
        swap(p).wait_send()
        for stage in range(3):
            for v, out, back in moves(p, stage):
                out().wait_send()
    for which, out, back in shares:
        out().wait_send()


def scan(rows, x_weight, small_weight, cot, gain, log_rates, step_bias):
    vmem = pl.BlockSpec(memory_space=pltpu.VMEM)
    V = pltpu.VMEM
    dma = pltpu.SemaphoreType.DMA
    slots = [V((PEERS, SLOT, 128), BF)] * 2 + [V((PEERS, 128, 128), BF)] * 6
    return pl.pallas_call(
        scan_kernel,
        in_specs=[vmem, pl.BlockSpec(memory_space=pl.ANY)] + [vmem] * 5,
        out_specs=[vmem] * 3,
        out_shape=[
            jax.ShapeDtypeStruct((ROWS, D), BF),
            jax.ShapeDtypeStruct((128, D), F32),
            jax.ShapeDtypeStruct((160, 128), F32),
        ],
        scratch_shapes=[
            V((D, T2), BF),
            V((T2, 256), F32),
            pltpu.SemaphoreType.DMA((8,)),
            V((8, 128), F32),
            V((HEADS, T2), F32),
            V((HEADS, T2), F32),
            V((HEADS, T2), F32),
            V((HEADS, T2), F32),
            V((2, ROWS, 128), F32),
            V((HEADS, T2), F32),
            V((T2, 256), BF),
            V((256, T2), BF),
            V((T2, 256), BF),
            V((256, T2), BF),
            V((2, ROWS, ROWS), F32),
            V((2, ROWS, ROWS), F32),
            V((D, T2), BF),
            V((8, 2, 128, T2), BF),
            V((D, T2), F32),
            V((D, T2), F32),
            V((WIDE, T2), BF),
            V((D, T2), BF),
            V((2 * HEADS * ROWS, ROWS), BF),
            V((2 * HEADS * ROWS, ROWS), BF),
            V((HEADS, 128), F32),
            V((HEADS, T2), F32),
            V((HEADS, T2), F32),
            V((HEADS, T2), F32),
            V((HEADS, 128), F32),
        ]
        + slots
        + [
            V((PEERS, 128, 128), F32),
            V((8, 128, T2), BF),
            V((PARTS, COLS, T2), BF),
            V((PARTS, 4, 256, COLS), BF),
            V((PARTS, 4, 64, COLS), BF),
            V((PARTS, 4, 16, COLS), F32),
            V((PARTS, 4, 16, COLS), F32),
            V((16, 1536), BF),
            V((16, 1024), BF),
            V((8, 16, 1536), BF),
            V((8, 16, 1024), BF),
        ]
        + [dma((PEERS,))] * 8
        + [
            dma((PARTS + 1,)),
            dma((PARTS + 1,)),
            dma((PARTS, 3, 4)),
            dma((PARTS, 3, 4)),
            dma((2, 8)),
            dma((2, 8)),
        ],
        compiler_params=pltpu.CompilerParams(
            collective_id=0, has_side_effects=True, vmem_limit_bytes=62 * 2**20
        ),
        name="layer",
    )(rows, x_weight, small_weight, cot, gain, log_rates, step_bias)


def hand_on_kernel(*refs):
    count = (len(refs) - 2) // 3
    ins, outs, held = refs[:count], refs[count : 2 * count], refs[2 * count : 3 * count]
    read_sem, write_sem = refs[3 * count :]
    chunks = []
    for src, dst, buf in zip(ins, outs, held):
        rows = src.shape[0] // 4
        for k in range(4):
            part = pl.ds(k * rows, rows)
            i = len(chunks)
            chunks.append((
                pltpu.make_async_copy(src.at[part, :], buf.at[part, :], read_sem.at[i]),
                pltpu.make_async_copy(buf.at[part, :], dst.at[part, :], write_sem.at[i]),
            ))
    for read, write in chunks:
        read.start()
    for read, write in chunks:
        read.wait()
        write.start()
    for read, write in chunks:
        write.wait()


def hand_on(*arrays):
    anywhere = pl.BlockSpec(memory_space=pl.ANY)
    dma = pltpu.SemaphoreType.DMA
    return pl.pallas_call(
        hand_on_kernel,
        in_specs=[anywhere] * len(arrays),
        out_specs=[anywhere] * len(arrays),
        out_shape=[jax.ShapeDtypeStruct(a.shape, a.dtype) for a in arrays],
        scratch_shapes=[pltpu.VMEM(a.shape, a.dtype) for a in arrays]
        + [dma((4 * len(arrays),)), dma((4 * len(arrays),))],
        name="hand_on",
    )(*arrays)


def shards(hidden, x_weight, state_weight, log_rates, step_bias, out_gain, cotangent):
    mixed, grad_x, grad_small = hand_on(*scan(
        hidden[0], x_weight, state_weight.T, cotangent[0],
        out_gain[None], log_rates[None], step_bias[None],
    ))
    return (mixed[None], grad_x, grad_small.T)


def solution(mesh):
    return jax.shard_map(
        shards,
        mesh=mesh,
        in_specs=(P("dp", "ctx", None), P(), P(), P(), P(), P(), P("dp", "ctx", None)),
        out_specs=(P("dp", "ctx", None), P("ctx", None), P("ctx", None)),
        check_vma=False,
    )
```

```python
import jax
import jax.numpy as jnp
from jax import lax
from jax.experimental import pallas as pl
from jax.experimental.pallas import tpu as pltpu
from jax.sharding import PartitionSpec as P

HEAD = 64
STATE = 64
D = 2048
ROWS = 256
T2 = 2 * ROWS
HEADS = 32
PAIRS = 16
PEERS = 16
SLOT = 144
WIDE = 2304
COLS = 256
PARTS = WIDE // COLS
MESH = pl.DeviceIdType.MESH
BF = jnp.bfloat16
F32 = jnp.float32
LOG2E = 1.4426950408889634

NN = (((1,), (0,)), ((), ()))
NT = (((1,), (1,)), ((), ()))
TN = (((0,), (0,)), ((), ()))


def dot(a, b, dims=NN):
    return lax.dot_general(a, b, dims, preferred_element_type=F32)


def dot_exact(a, b, dims=NN):
    return lax.dot_general(
        a, b, dims, preferred_element_type=F32, precision=lax.Precision.HIGHEST
    )


def iota2(shape, dim):
    return lax.broadcasted_iota(jnp.int32, shape, dim)


def flip_matrix(n):
    return (iota2((n, n), 0) + iota2((n, n), 1) == n - 1).astype(F32).astype(BF)


def scan_kernel(
    rows_ref, w_hbm, wst_ref, cot_ref, gain_ref, lr_ref, sb_ref,
    mixed_ref, gx_ref, gs_ref,
    xt_ref, proj_ref, w_sem,
    small, zt, step_t, weight, l2_t, l2_n, el_t, bdb, bdbt, bdc, bdct, scm, dsc,
    wx, ct, u, g, du, vdu, mst, dec, tot, prow, qrow, q2row, asrow,
    send_a, recv_a, send_a2, recv_a2, send_b, recv_b, send_b2, recv_b2, up,
    rt_in, dx_in, in1, in2, buf3, in3, last0, last1, outs0, outs1,
    sa, ra, sa2, ra2, sb, rb, sb2, rb2, core_s, core_r, ss, rs, out_s, out_r,
):
    me = lax.axis_index("ctx")
    dp = lax.axis_index("dp")
    chip, core = me // 2, me % 2
    zz, x_hi = dp // 2, dp % 2
    yy, x_lo = chip // 2, chip % 2
    xx = x_hi * 2 + x_lo
    coords = {"z": zz, "y": yy, "x": xx}
    sibling = {"dp": dp, "ctx": chip * 2 + (1 - core)}
    dx = du

    def at_axis(axis, v):
        if axis == "z":
            return {"dp": v * 2 + x_hi, "ctx": me}
        if axis == "y":
            return {"dp": dp, "ctx": (v * 2 + x_lo) * 2 + core}
        return {"dp": zz * 2 + v // 2, "ctx": (yy * 2 + v % 2) * 2 + core}

    def to(friend, src, dst, ssem, rsem):
        return pltpu.make_async_remote_copy(
            src_ref=src, dst_ref=dst, send_sem=ssem, recv_sem=rsem,
            device_id=friend, device_id_type=MESH,
        )

    barrier = pltpu.get_barrier_semaphore()

    def w_block(j):
        return pltpu.make_async_copy(
            w_hbm.at[:, pl.ds(pl.multiple_of(j * 256, 256), 256)],
            dec.at[pl.ds(pl.multiple_of(j * D, D), D), :],
            w_sem.at[j],
        )

    turns = [lax.rem(chip + k, 8) for k in range(8)]
    for j in turns:
        w_block(j).start()

    friends = [{"dp": dp, "ctx": (me + k) % PEERS} for k in range(1, PEERS)]
    friends += [{"dp": (dp + k) % 8, "ctx": me} for k in range(1, 8)]
    friends += [{"dp": zz * 2 + (1 - x_hi), "ctx": (yy * 2 + (1 - x_lo)) * 2 + core}]
    for friend in friends:
        pl.semaphore_signal(barrier, inc=1, device_id=friend, device_id_type=MESH)

    def copy(src, dst, ssem, rsem, peer, slot):
        return pltpu.make_async_remote_copy(
            src_ref=src.at[peer], dst_ref=dst.at[slot], send_sem=ssem.at[peer],
            recv_sem=rsem.at[slot], device_id={"dp": dp, "ctx": peer}, device_id_type=MESH,
        )

    def send_all(src, dst, ssem, rsem):
        def one(k, c):
            j = lax.rem(me + k, PEERS)
            copy(src, dst, ssem, rsem, j, me).start()
            return c
        lax.fori_loop(1, PEERS, one, 0)

    def recv_all(src, dst, ssem, rsem):
        def one(k, c):
            j = lax.rem(me + k, PEERS)
            copy(src, dst, ssem, rsem, j, j).wait_recv()
            return c
        lax.fori_loop(1, PEERS, one, 0)

    def sent_all(src, dst, ssem, rsem):
        def one(k, c):
            j = lax.rem(me + k, PEERS)
            copy(src, dst, ssem, rsem, j, me).wait_send()
            return c
        lax.fori_loop(1, PEERS, one, 0)

    low = iota2((1, 128), 1) < 64
    row_i = iota2((ROWS, ROWS), 0)
    col_i = iota2((ROWS, ROWS), 1)
    causal = (row_i >= col_i, row_i <= col_i)
    tri = [m.astype(F32) for m in causal]
    halves = (slice(0, ROWS), slice(ROWS, T2))

    flip = flip_matrix(256)
    for k in range(8):
        part = rows_ref[:, k * 256 : (k + 1) * 256]
        mst[k * T2 : k * T2 + ROWS, :] = part
        mst[(7 - k) * T2 + ROWS : (8 - k) * T2, :] = dot(part, flip).astype(BF)

    def both_rows():
        return jnp.concatenate([mst[k * T2 : (k + 1) * T2, :] for k in range(8)], axis=1)

    proj_ref[:, 160:256] = jnp.zeros((T2, 96), F32)
    proj_ref[:, 0:160] = dot(both_rows(), wst_ref[...], NT)
    small[...] = jnp.zeros_like(small)
    small[0:1, 0:HEADS] = -jnp.exp(lr_ref[...])
    small[1:2, 0:HEADS] = sb_ref[...]
    neg_rate = small[0:1, :]
    z = proj_ref[:, 128:256] + small[1:2, :]
    step_n = jnp.maximum(z, 0.0) + jnp.log1p(jnp.exp(-jnp.abs(z)))
    log_n = step_n * (neg_rate * LOG2E)
    zt[...] = z.T[0:HEADS]
    step_t[...] = step_n.T[0:HEADS]
    for b in range(2):
        l2 = dot_exact(tri[b], log_n[halves[b]])
        l2_n[b] = l2
        l2_t[:, halves[b]] = l2.T[0:HEADS]
    el_t[...] = jnp.exp2(l2_t[...])
    ends = (l2_t[:, ROWS - 1 : ROWS], l2_t[:, ROWS : ROWS + 1])
    tot[...] = jnp.exp2(jnp.where(low, ends[0], ends[1]))
    for b in range(2):
        weight[:, halves[b]] = step_t[:, halves[b]] * jnp.exp2(ends[b] - l2_t[:, halves[b]])

    both = proj_ref[:, 0:128]
    turned = pltpu.roll(both, 64, 1)
    own = (iota2((T2, 128), 0) < ROWS) == (iota2((T2, 128), 1) < 64)
    maps_b = jnp.where(low, both, turned)
    maps_c = jnp.where(low, turned, both)
    b_diag = jnp.where(own, maps_b, 0.0)
    c_diag = jnp.where(own, maps_c, 0.0)
    for full, by_rows, by_cols in ((b_diag, bdb, bdbt), (c_diag, bdc, bdct)):
        coarse = full.astype(BF).astype(F32)
        for k, term in enumerate((coarse, full - coarse)):
            by_rows[:, k * 128 : (k + 1) * 128] = term.astype(BF)
            by_cols[k * 128 : (k + 1) * 128, :] = term.T.astype(BF)

    def to_state(lhs, by_rows):
        out = dot(lhs, by_rows[...])
        return (out[:, 0:128] + out[:, 128:256]).astype(BF)

    def from_state(state, by_cols):
        return dot(jnp.concatenate([state, state], axis=1), by_cols[...])

    def local_end(hp, c):
        base = pl.multiple_of(hp * 128, 128)
        for hh in range(2):
            rows = pl.ds(pl.multiple_of(base + hh * 64, 64), 64)
            h = pl.ds(2 * hp + hh, 1)
            wx[rows, :] = (xt_ref[rows, :].astype(F32) * weight[h, :]).astype(BF)
        send_a[hp, 0:128, :] = to_state(wx[pl.ds(base, 128), :], bdb)
        t0 = tot[pl.ds(2 * hp, 1), :]
        t1 = tot[pl.ds(2 * hp + 1, 1), :]
        h0 = t0.astype(BF).astype(F32)
        h1 = t1.astype(BF).astype(F32)
        at = iota2((16, 128), 0)
        extra = jnp.where(at == 0, h0, jnp.where(at == 1, t0 - h0, jnp.where(at == 2, h1, t1 - h1)))
        send_a[hp, 128:144, :] = extra.astype(BF)
        return c

    def early(step, src, dst, ssem, rsem):
        def one(k, c):
            j = lax.rem(me + k, PEERS)
            step(j, 0)
            copy(src, dst, ssem, rsem, j, me).start()
            return c
        lax.fori_loop(1, PEERS, one, 0, unroll=5)
        step(me, 0)
        dst[me] = src[me]

    pl.semaphore_wait(barrier, len(friends))
    for k, j in enumerate(turns):
        w_block(j).wait()
        values = dot(both_rows(), dec[pl.ds(pl.multiple_of(j * D, D), D), :]).astype(BF)
        xt_ref[pl.ds(pl.multiple_of(j * 256, 256), 256), :] = values.T
        if k == 0:
            hp = sibling["ctx"]
            local_end(hp, 0)
            copy(send_a, recv_a, sa, ra, hp, me).start()
            local_end(me, 0)
            recv_a[me] = send_a[me]
        else:
            for hh in range(2):
                hp = 2 * j + hh
                local_end(hp, 0)
                copy(send_a, recv_a, sa, ra, hp, me).start()

    for b in range(2):
        sc = dot_exact(
            jnp.where(low, maps_c[halves[b]], 0.0), maps_b[halves[b]], NT
        )
        scm[b] = jnp.where(causal[b], sc, 0.0)

    zero_half = jnp.zeros((128, 128), BF)
    blocks = (((0, 0), (1, 0), (1, 1)), ((0, 0), (0, 1), (1, 1)))

    def span(i):
        return slice(i * 128, (i + 1) * 128)

    def tile(b, h, i, rows=128):
        return pl.ds(pl.multiple_of((b * HEADS + h) * ROWS + i * 128, 128), rows)

    def forward(hp, c):
        for hh in range(2):
            h = 2 * hp + hh
            rows = pl.ds(pl.multiple_of(h * 64, 64), 64)
            for b in range(2):
                column = pltpu.roll(l2_n[b], 128 - h, 1)[:, 0:1]
                line = l2_t[pl.ds(h, 1), halves[b]]
                size = step_t[pl.ds(h, 1), halves[b]]
                for i, j in blocks[b]:
                    d = jnp.exp2(jnp.minimum(column[span(i)] - line[:, span(j)], 0.0))
                    d = d * size[:, span(j)]
                    dec[tile(b, h, i), span(j)] = d.astype(BF)
                    mst[tile(b, h, i), span(j)] = (d * scm[b, span(i), span(j)]).astype(BF)
                mst[tile(b, h, b), span(1 - b)] = zero_half
                u[rows, halves[b]] = dot(xt_ref[rows, halves[b]], mst[tile(b, h, 0, ROWS), :], NT)
        return c

    def chain(recv, out, fwd_up):
        def totals(i):
            t = recv_a[i, 128:144, :].astype(F32)
            rows = iota2((128, 128), 0) < 64
            return jnp.where(rows, t[0:1] + t[1:2], t[2:3] + t[3:4])

        def climb(i, carry):
            up[i] = carry
            return totals(i) * carry + recv[i, 0:128, :].astype(F32)

        zero = jnp.zeros((128, 128), F32)
        lax.fori_loop(0, PEERS, climb, zero)

        def descend(k, carry):
            i = PEERS - 1 - k
            pick = low if fwd_up else jnp.logical_not(low)
            out[i] = jnp.where(pick, up[i], carry).astype(BF)
            return totals(i) * carry + recv[i, 0:128, :].astype(F32)

        lax.fori_loop(0, PEERS, descend, zero)

    lax.fori_loop(0, PAIRS // 4, forward, 0)
    recv_all(send_a, recv_a, sa, ra)
    chain(recv_a, send_a2, True)
    recv_a2[me] = send_a2[me]
    send_all(send_a2, recv_a2, sa2, ra2)
    lax.fori_loop(PAIRS // 4, PAIRS, forward, 0)

    for blk in range(8):
        turned_c = cot_ref[:, blk * 256 : (blk + 1) * 256].T
        flipped_c = dot(flip, turned_c).astype(BF)
        for hh in range(2):
            ct[blk, hh, :, 0:ROWS] = turned_c[hh * 128 : hh * 128 + 128]
            ct[7 - blk, hh, :, ROWS:T2] = flipped_c[hh * 128 : hh * 128 + 128]

    recv_all(send_a2, recv_a2, sa2, ra2)

    def gains(hp):
        lane = pl.ds(pl.multiple_of(hp * 128, 128), 128)
        column = jnp.broadcast_to(gain_ref[:, lane], (128, 128)).T
        return jnp.concatenate([column] * 4, axis=1)

    def readout(hp, c):
        q, e = c
        base = pl.multiple_of(hp * 128, 128)
        out = from_state(recv_a2[hp], bdct)
        gain = gains(hp)
        for hh in range(2):
            rows = pl.ds(pl.multiple_of(base + hh * 64, 64), 64)
            part = slice(hh * 64, hh * 64 + 64)
            v = u[rows, :] + out[part] * el_t[pl.ds(2 * hp + hh, 1), :]
            u[rows, :] = v
            q = q + jnp.sum(v * v, axis=0, keepdims=True)
            e = e + jnp.sum(v * gain[part] * ct[lax.div(hp, 2), lax.rem(hp, 2), part, :].astype(F32), axis=0, keepdims=True)
        return q, e

    none = jnp.zeros((1, T2), F32)
    q, e = lax.fori_loop(0, PAIRS, readout, (none, none), unroll=4)
    scale = lax.rsqrt(q * (1.0 / D) + 1e-05)
    pull = scale * scale * scale * e * (1.0 / D)

    def normed(hp, c):
        base = pl.multiple_of(hp * 128, 128)
        gain = gains(hp)
        for hh in range(2):
            rows = pl.ds(pl.multiple_of(base + hh * 64, 64), 64)
            h = pl.ds(2 * hp + hh, 1)
            part = slice(hh * 64, hh * 64 + 64)
            v = u[rows, :]
            gs = gain[part] * scale
            back = gs * ct[lax.div(hp, 2), lax.rem(hp, 2), part, :].astype(F32) - v * pull
            vdu[rows, :] = (back * el_t[h, :]).astype(BF)
            back = back.astype(BF)
            du[rows, :] = back
            prow[h, :] = jnp.sum(back.astype(F32) * v, axis=0, keepdims=True)
            u[rows, :] = v * gs
        send_b[hp] = to_state(vdu[pl.ds(base, 128), :], bdc)
        return c

    early(normed, send_b, recv_b, sb, rb)
    dsc[...] = jnp.zeros_like(dsc)

    def backward(hp, c):
        for b in range(2):
            pair = []
            for hh in range(2):
                h = 2 * hp + hh
                rows = pl.ds(pl.multiple_of(h * 64, 64), 64)
                d = du[rows, halves[b]]
                g[rows, halves[b]] = dot(d, mst[tile(b, h, 0, ROWS), :])
                pair.append(dot(d, xt_ref[rows, halves[b]], TN))
            for i, j in blocks[b]:
                acc = dsc[b, span(i), span(j)]
                for hh in range(2):
                    acc = acc + pair[hh][span(i), span(j)] * dec[
                        tile(b, 2 * hp + hh, i), span(j)
                    ].astype(F32)
                dsc[b, span(i), span(j)] = acc
        return c

    lax.fori_loop(0, PAIRS // 2, backward, 0)
    for blk in range(8):
        y_rc = u[(7 - blk) * 256 : (8 - blk) * 256, ROWS:T2].astype(BF)
        y = u[blk * 256 : (blk + 1) * 256, 0:ROWS] + dot(flip, y_rc)
        mixed_ref[:, blk * 256 : (blk + 1) * 256] = y.astype(BF).T

    def read_maps(hp, acc):
        return acc + dot(recv_a2[hp], vdu[pl.ds(pl.multiple_of(hp * 128, 128), 128), :], TN)

    dc_state = lax.fori_loop(0, PAIRS, read_maps, jnp.zeros((128, T2), F32), unroll=4)
    recv_all(send_b, recv_b, sb, rb)
    chain(recv_b, send_b2, False)
    recv_b2[me] = send_b2[me]
    send_all(send_b2, recv_b2, sb2, rb2)
    lax.fori_loop(PAIRS // 2, PAIRS, backward, 0)

    own_maps = []
    for b in range(2):
        lanes = halves[b]
        d_scores = jnp.where(causal[b], dsc[b], 0.0)
        part = slice(b * 64, b * 64 + 64)
        fine = slice(128 + b * 64, 192 + b * 64)
        own_b = bdbt[part, lanes].astype(F32) + bdbt[fine, lanes].astype(F32)
        own_c = bdct[part, lanes].astype(F32) + bdct[fine, lanes].astype(F32)
        dc = dot_exact(own_b, d_scores, NT) + dc_state[part, lanes]
        dx[D + 64 : D + 128, lanes] = dc.astype(BF)
        own_maps.append(dot_exact(own_c, d_scores))
    dx[D + 160 : WIDE, :] = jnp.zeros((WIDE - D - 160, T2), BF)
    for blk in range(8):
        across = rows_ref[:, blk * 256 : (blk + 1) * 256].T
        flipped = dot(flip, across).astype(BF)
        for hh in range(2):
            ct[blk, hh, :, 0:ROWS] = across[hh * 128 : hh * 128 + 128]
            ct[7 - blk, hh, :, ROWS:T2] = flipped[hh * 128 : hh * 128 + 128]
    rows_swap = to(sibling, ct.at[:, 1 - core], rt_in, core_s.at[PARTS], core_r.at[PARTS])
    rows_swap.start()

    def swap(p):
        return to(
            sibling, dx.at[pl.ds(p * COLS, COLS), :], dx_in.at[p], core_s.at[p], core_r.at[p]
        )

    recv_all(send_b2, recv_b2, sb2, rb2)

    def finish(hp, acc):
        base = pl.multiple_of(hp * 128, 128)
        after = recv_b2[hp]
        acc = acc + dot(after, wx[pl.ds(base, 128), :], TN)
        out = from_state(after, bdbt)
        meet = after.astype(F32) * recv_a2[hp].astype(F32)
        for hh in range(2):
            rows = pl.ds(pl.multiple_of(base + hh * 64, 64), 64)
            h = pl.ds(2 * hp + hh, 1)
            part = slice(hh * 64, hh * 64 + 64)
            asrow[h, :] = jnp.sum(meet[part], axis=0, keepdims=True)
            far = out[part] * weight[h, :]
            whole = g[rows, :] + far
            dx[rows, :] = whole.astype(BF)
            x = xt_ref[rows, :].astype(F32)
            qrow[h, :] = jnp.sum(x * whole, axis=0, keepdims=True)
            q2row[h, :] = jnp.sum(x * far, axis=0, keepdims=True)
        return acc


    def small_part(db_state):
        met = asrow[...] * tot[...]
        neg_col = jnp.broadcast_to(neg_rate, (128, 128)).T[0:HEADS, 0:1]
        for b in range(2):
            lanes = halves[b]
            mine = low if b == 0 else jnp.logical_not(low)
            end_grad = jnp.sum(jnp.where(mine, met, 0.0), axis=1, keepdims=True) + jnp.sum(
                q2row[:, lanes], axis=1, keepdims=True
            )
            dl = prow[:, lanes] - qrow[:, lanes]
            da = dot_exact(dl, tri[b]) + end_grad
            zb = zt[:, lanes]
            small_e = jnp.exp(-jnp.abs(zb))
            sig = jnp.where(zb >= 0, 1.0, small_e) / (1.0 + small_e)
            ratio = jnp.where(zb < -20.0, 1.0, sig / step_t[:, lanes])
            dz = qrow[:, lanes] * ratio + da * neg_col * sig
            dx[D + 128 : D + 160, lanes] = dz.astype(BF)
            part = slice(b * 64, b * 64 + 64)
            db = own_maps[b] + db_state[part, lanes]
            dx[D : D + 64, lanes] = db.astype(BF)
        swap(8).start()

    orders = (("z", "y", "x"), ("y", "x", "z"), ("x", "z", "y")) * 3

    def moves(p, stage):
        axis = orders[p][stage]
        here = coords[axis]
        found = []
        for k in (2, 1, 3):
            v = (here + k) % 4

            def copy_out(slot, v=v):
                if stage == 0:
                    src, dst = dec.at[pl.ds(pl.multiple_of(p * 1024 + v * 256, 256), 256), :], in1
                elif stage == 1:
                    first_row = PARTS * 1024 + p * 256
                    src, dst = dec.at[pl.ds(pl.multiple_of(first_row + v * 64, 64), 64), :], in2
                else:
                    src, dst = buf3.at[p, v], in3
                return to(
                    at_axis(axis, v), src, dst.at[p, slot],
                    ss.at[p, stage, v], rs.at[p, stage, slot],
                )

            found.append((v, lambda c=copy_out: c(here), lambda c=copy_out, v=v: c(v)))
        return found

    def launch(p, stage):
        for v, out, back in moves(p, stage):
            out().start()

    def arrived(p, stage):
        found = moves(p, stage)
        for v, out, back in found:
            back().wait_recv()
        return [v for v, out, back in found], coords[orders[p][stage]]

    def gradient(p):
        swap(p).wait_recv()
        left = jnp.concatenate(
            [ct[:, core].reshape(1024, T2), rt_in[...].reshape(1024, T2)], axis=1
        )
        right = jnp.concatenate([dx[p * COLS : (p + 1) * COLS, :], dx_in[p]], axis=1)
        tile = dot(left, right, NT).astype(BF)
        for k in range(64):
            jj, m = k // 8, k % 8
            where = {"z": m // 2, "y": jj // 2, "x": (m % 2) * 2 + jj % 2}
            a, b, d = (where[axis] for axis in orders[p])
            first_row = p * 1024 + ((a * 4 + b) * 4 + d) * 16
            dec[first_row : first_row + 16, :] = tile[k * 16 : (k + 1) * 16]
        launch(p, 0)

    def first(p):
        peers, here = arrived(p, 0)
        mine = pl.ds(pl.multiple_of(p * 1024 + here * 256, 256), 256)
        total = dec[mine, :].astype(F32)
        for v in peers:
            total = total + in1[p, v].astype(F32)
        dec[PARTS * 1024 + p * 256 : PARTS * 1024 + (p + 1) * 256, :] = total.astype(BF)
        launch(p, 1)

    def second(p):
        peers, here = arrived(p, 1)
        mine = pl.ds(pl.multiple_of(PARTS * 1024 + p * 256 + here * 64, 64), 64)
        total = dec[mine, :].astype(F32)
        for v in peers:
            total = total + in2[p, v].astype(F32)
        for v in range(4):
            buf3[p, v] = total[v * 16 : (v + 1) * 16]
        launch(p, 2)

    def third(p):
        peers, here = arrived(p, 2)
        total = buf3[p, here]
        for v in peers:
            total = total + in3[p, v]
        return total

    shares = []

    def share(kind, src, dst):
        dst[dp] = src[...]
        for k in range(1, 8):
            j = (dp + k) % 8

            def copy_out(slot, j=j):
                return to(
                    {"dp": j, "ctx": me}, src, dst.at[slot],
                    out_s.at[kind, j], out_r.at[kind, slot],
                )

            copy_out(dp).start()
            shares.append((kind, lambda c=copy_out: c(dp), lambda c=copy_out, j=j: c(j)))

    def finals(parts):
        for p in parts:
            piece = third(p)
            whole = piece.astype(BF)
            if p < 6:
                last0[:, p * COLS : (p + 1) * COLS] = whole
            else:
                last1[:, (p - 6) * COLS : (p - 5) * COLS] = whole
            if p == PARTS - 1:
                last1[:, 3 * COLS : 4 * COLS] = (piece - whole.astype(F32)).astype(BF)

    db_state = jnp.zeros((128, T2), F32)
    for p in range(8):
        db_state = finish(2 * p + 1, finish(2 * p, db_state))
        swap(p).start()
        if p == 2:
            rows_swap.wait_recv()
        if p >= 2:
            gradient(p - 2)
    small_part(db_state)
    for p in range(6, PARTS):
        gradient(p)
        first(p - 6)

    sent_all(send_a, recv_a, sa, ra)
    sent_all(send_a2, recv_a2, sa2, ra2)
    sent_all(send_b, recv_b, sb, rb)
    sent_all(send_b2, recv_b2, sb2, rb2)
    for p in range(3, 6):
        first(p)
    for p in range(0, 3):
        second(p)
    for p in range(6, 9):
        first(p)
    for p in range(3, 6):
        second(p)
    for p in range(6, 9):
        second(p)
    finals(range(0, 6))
    share(0, last0, outs0)
    finals(range(6, 9))
    share(1, last1, outs1)

    def gathered(kind):
        for which, out, back in shares:
            if which == kind:
                back().wait_recv()

    gathered(0)
    for k in range(8):
        gx_ref[k * 16 : (k + 1) * 16, 0:1536] = outs0[k].astype(F32)
    gathered(1)
    for k in range(8):
        rows = slice(k * 16, (k + 1) * 16)
        gx_ref[rows, 1536:D] = outs1[k, :, 0:512].astype(F32)
        narrow = outs1[k, :, 512:768].astype(F32) + outs1[k, :, 768:1024].astype(F32)
        gs_ref[:, rows] = narrow.T[0:160]

    rows_swap.wait_send()
    for p in range(PARTS):
        swap(p).wait_send()
        for stage in range(3):
            for v, out, back in moves(p, stage):
                out().wait_send()
    for which, out, back in shares:
        out().wait_send()


def scan(rows, x_weight, small_weight, cot, gain, log_rates, step_bias):
    vmem = pl.BlockSpec(memory_space=pltpu.VMEM)
    V = pltpu.VMEM
    dma = pltpu.SemaphoreType.DMA
    slots = [V((PEERS, SLOT, 128), BF)] * 2 + [V((PEERS, 128, 128), BF)] * 6
    return pl.pallas_call(
        scan_kernel,
        in_specs=[vmem, pl.BlockSpec(memory_space=pl.ANY)] + [vmem] * 5,
        out_specs=[vmem] * 3,
        out_shape=[
            jax.ShapeDtypeStruct((ROWS, D), BF),
            jax.ShapeDtypeStruct((128, D), F32),
            jax.ShapeDtypeStruct((160, 128), F32),
        ],
        scratch_shapes=[
            V((D, T2), BF),
            V((T2, 256), F32),
            pltpu.SemaphoreType.DMA((8,)),
            V((8, 128), F32),
            V((HEADS, T2), F32),
            V((HEADS, T2), F32),
            V((HEADS, T2), F32),
            V((HEADS, T2), F32),
            V((2, ROWS, 128), F32),
            V((HEADS, T2), F32),
            V((T2, 256), BF),
            V((256, T2), BF),
            V((T2, 256), BF),
            V((256, T2), BF),
            V((2, ROWS, ROWS), F32),
            V((2, ROWS, ROWS), F32),
            V((D, T2), BF),
            V((8, 2, 128, T2), BF),
            V((D, T2), F32),
            V((D, T2), F32),
            V((WIDE, T2), BF),
            V((D, T2), BF),
            V((2 * HEADS * ROWS, ROWS), BF),
            V((2 * HEADS * ROWS, ROWS), BF),
            V((HEADS, 128), F32),
            V((HEADS, T2), F32),
            V((HEADS, T2), F32),
            V((HEADS, T2), F32),
            V((HEADS, 128), F32),
        ]
        + slots
        + [
            V((PEERS, 128, 128), F32),
            V((8, 128, T2), BF),
            V((PARTS, COLS, T2), BF),
            V((PARTS, 4, 256, COLS), BF),
            V((PARTS, 4, 64, COLS), BF),
            V((PARTS, 4, 16, COLS), F32),
            V((PARTS, 4, 16, COLS), F32),
            V((16, 1536), BF),
            V((16, 1024), BF),
            V((8, 16, 1536), BF),
            V((8, 16, 1024), BF),
        ]
        + [dma((PEERS,))] * 8
        + [
            dma((PARTS + 1,)),
            dma((PARTS + 1,)),
            dma((PARTS, 3, 4)),
            dma((PARTS, 3, 4)),
            dma((2, 8)),
            dma((2, 8)),
        ],
        compiler_params=pltpu.CompilerParams(
            collective_id=0, has_side_effects=True, vmem_limit_bytes=62 * 2**20
        ),
        name="layer",
    )(rows, x_weight, small_weight, cot, gain, log_rates, step_bias)


def hand_on_kernel(*refs):
    count = (len(refs) - 2) // 3
    ins, outs, held = refs[:count], refs[count : 2 * count], refs[2 * count : 3 * count]
    read_sem, write_sem = refs[3 * count :]
    chunks = []
    for src, dst, buf in zip(ins, outs, held):
        rows = src.shape[0] // 4
        for k in range(4):
            part = pl.ds(k * rows, rows)
            i = len(chunks)
            chunks.append((
                pltpu.make_async_copy(src.at[part, :], buf.at[part, :], read_sem.at[i]),
                pltpu.make_async_copy(buf.at[part, :], dst.at[part, :], write_sem.at[i]),
            ))
    for read, write in chunks:
        read.start()
    for read, write in chunks:
        read.wait()
        write.start()
    for read, write in chunks:
        write.wait()


def hand_on(*arrays):
    anywhere = pl.BlockSpec(memory_space=pl.ANY)
    dma = pltpu.SemaphoreType.DMA
    return pl.pallas_call(
        hand_on_kernel,
        in_specs=[anywhere] * len(arrays),
        out_specs=[anywhere] * len(arrays),
        out_shape=[jax.ShapeDtypeStruct(a.shape, a.dtype) for a in arrays],
        scratch_shapes=[pltpu.VMEM(a.shape, a.dtype) for a in arrays]
        + [dma((4 * len(arrays),)), dma((4 * len(arrays),))],
        name="hand_on",
    )(*arrays)


def shards(hidden, x_weight, state_weight, log_rates, step_bias, out_gain, cotangent):
    mixed, grad_x, grad_small = hand_on(*scan(
        hidden[0], x_weight, state_weight.T, cotangent[0],
        out_gain[None], log_rates[None], step_bias[None],
    ))
    return (mixed[None], grad_x, grad_small.T)


def solution(mesh):
    return jax.shard_map(
        shards,
        mesh=mesh,
        in_specs=(P("dp", "ctx", None), P(), P(), P(), P(), P(), P("dp", "ctx", None)),
        out_specs=(P("dp", "ctx", None), P("ctx", None), P("ctx", None)),
        check_vma=False,
    )
```

```python
import jax
import jax.numpy as jnp
from jax import lax
from jax.experimental import pallas as pl
from jax.experimental.pallas import tpu as pltpu
from jax.sharding import PartitionSpec as P

HEAD = 64
STATE = 64
D = 2048
ROWS = 256
T2 = 2 * ROWS
HEADS = 32
PAIRS = 16
PEERS = 16
SLOT = 144
WIDE = 2304
COLS = 256
PARTS = WIDE // COLS
MESH = pl.DeviceIdType.MESH
BF = jnp.bfloat16
F32 = jnp.float32
LOG2E = 1.4426950408889634

NN = (((1,), (0,)), ((), ()))
NT = (((1,), (1,)), ((), ()))
TN = (((0,), (0,)), ((), ()))


def dot(a, b, dims=NN):
    return lax.dot_general(a, b, dims, preferred_element_type=F32)


def dot_exact(a, b, dims=NN):
    return lax.dot_general(
        a, b, dims, preferred_element_type=F32, precision=lax.Precision.HIGHEST
    )


def iota2(shape, dim):
    return lax.broadcasted_iota(jnp.int32, shape, dim)


def flip_matrix(n):
    return (iota2((n, n), 0) + iota2((n, n), 1) == n - 1).astype(F32).astype(BF)


def scan_kernel(
    rows_ref, w_hbm, wst_ref, cot_ref, gain_ref, lr_ref, sb_ref,
    mixed_ref, gx_ref, gs_ref,
    xt_ref, proj_ref, w_sem,
    small, zt, step_t, weight, l2_t, l2_n, el_t, bdb, bdbt, bdc, bdct, scm, dsc,
    wx, ct, u, g, du, vdu, mst, dec, tot, prow, qrow, q2row, asrow,
    send_a, recv_a, send_a2, recv_a2, send_b, recv_b, send_b2, recv_b2, up,
    rt_in, dx_in, in1, in2, buf3, in3, last0, last1, outs0, outs1,
    sa, ra, sa2, ra2, sb, rb, sb2, rb2, core_s, core_r, ss, rs, out_s, out_r,
):
    me = lax.axis_index("ctx")
    dp = lax.axis_index("dp")
    chip, core = me // 2, me % 2
    zz, x_hi = dp // 2, dp % 2
    yy, x_lo = chip // 2, chip % 2
    xx = x_hi * 2 + x_lo
    coords = {"z": zz, "y": yy, "x": xx}
    sibling = {"dp": dp, "ctx": chip * 2 + (1 - core)}
    dx = du

    def at_axis(axis, v):
        if axis == "z":
            return {"dp": v * 2 + x_hi, "ctx": me}
        if axis == "y":
            return {"dp": dp, "ctx": (v * 2 + x_lo) * 2 + core}
        return {"dp": zz * 2 + v // 2, "ctx": (yy * 2 + v % 2) * 2 + core}

    def to(friend, src, dst, ssem, rsem):
        return pltpu.make_async_remote_copy(
            src_ref=src, dst_ref=dst, send_sem=ssem, recv_sem=rsem,
            device_id=friend, device_id_type=MESH,
        )

    barrier = pltpu.get_barrier_semaphore()

    def w_block(j):
        return pltpu.make_async_copy(
            w_hbm.at[:, pl.ds(pl.multiple_of(j * 256, 256), 256)],
            dec.at[pl.ds(pl.multiple_of(j * D, D), D), :],
            w_sem.at[j],
        )

    turns = [lax.rem(chip + k, 8) for k in range(8)]
    for j in turns:
        w_block(j).start()

    friends = [{"dp": dp, "ctx": (me + k) % PEERS} for k in range(1, PEERS)]
    friends += [{"dp": (dp + k) % 8, "ctx": me} for k in range(1, 8)]
    friends += [{"dp": zz * 2 + (1 - x_hi), "ctx": (yy * 2 + (1 - x_lo)) * 2 + core}]
    for friend in friends:
        pl.semaphore_signal(barrier, inc=1, device_id=friend, device_id_type=MESH)

    def copy(src, dst, ssem, rsem, peer, slot):
        return pltpu.make_async_remote_copy(
            src_ref=src.at[peer], dst_ref=dst.at[slot], send_sem=ssem.at[peer],
            recv_sem=rsem.at[slot], device_id={"dp": dp, "ctx": peer}, device_id_type=MESH,
        )

    def send_all(src, dst, ssem, rsem):
        def one(k, c):
            j = lax.rem(me + k, PEERS)
            copy(src, dst, ssem, rsem, j, me).start()
            return c
        lax.fori_loop(1, PEERS, one, 0)

    def recv_all(src, dst, ssem, rsem):
        def one(k, c):
            j = lax.rem(me + k, PEERS)
            copy(src, dst, ssem, rsem, j, j).wait_recv()
            return c
        lax.fori_loop(1, PEERS, one, 0)

    def sent_all(src, dst, ssem, rsem):
        def one(k, c):
            j = lax.rem(me + k, PEERS)
            copy(src, dst, ssem, rsem, j, me).wait_send()
            return c
        lax.fori_loop(1, PEERS, one, 0)

    low = iota2((1, 128), 1) < 64
    row_i = iota2((ROWS, ROWS), 0)
    col_i = iota2((ROWS, ROWS), 1)
    causal = (row_i >= col_i, row_i <= col_i)
    tri = [m.astype(F32) for m in causal]
    halves = (slice(0, ROWS), slice(ROWS, T2))

    flip = flip_matrix(256)
    for k in range(8):
        part = rows_ref[:, k * 256 : (k + 1) * 256]
        mst[k * T2 : k * T2 + ROWS, :] = part
        mst[(7 - k) * T2 + ROWS : (8 - k) * T2, :] = dot(part, flip).astype(BF)

    def both_rows():
        return jnp.concatenate([mst[k * T2 : (k + 1) * T2, :] for k in range(8)], axis=1)

    proj_ref[:, 160:256] = jnp.zeros((T2, 96), F32)
    proj_ref[:, 0:160] = dot(both_rows(), wst_ref[...], NT)
    small[...] = jnp.zeros_like(small)
    small[0:1, 0:HEADS] = -jnp.exp(lr_ref[...])
    small[1:2, 0:HEADS] = sb_ref[...]
    neg_rate = small[0:1, :]
    z = proj_ref[:, 128:256] + small[1:2, :]
    step_n = jnp.maximum(z, 0.0) + jnp.log1p(jnp.exp(-jnp.abs(z)))
    log_n = step_n * (neg_rate * LOG2E)
    zt[...] = z.T[0:HEADS]
    step_t[...] = step_n.T[0:HEADS]
    for b in range(2):
        l2 = dot_exact(tri[b], log_n[halves[b]])
        l2_n[b] = l2
        l2_t[:, halves[b]] = l2.T[0:HEADS]
    el_t[...] = jnp.exp2(l2_t[...])
    ends = (l2_t[:, ROWS - 1 : ROWS], l2_t[:, ROWS : ROWS + 1])
    tot[...] = jnp.exp2(jnp.where(low, ends[0], ends[1]))
    for b in range(2):
        weight[:, halves[b]] = step_t[:, halves[b]] * jnp.exp2(ends[b] - l2_t[:, halves[b]])

    both = proj_ref[:, 0:128]
    turned = pltpu.roll(both, 64, 1)
    own = (iota2((T2, 128), 0) < ROWS) == (iota2((T2, 128), 1) < 64)
    maps_b = jnp.where(low, both, turned)
    maps_c = jnp.where(low, turned, both)
    b_diag = jnp.where(own, maps_b, 0.0)
    c_diag = jnp.where(own, maps_c, 0.0)
    for full, by_rows, by_cols in ((b_diag, bdb, bdbt), (c_diag, bdc, bdct)):
        coarse = full.astype(BF).astype(F32)
        for k, term in enumerate((coarse, full - coarse)):
            by_rows[:, k * 128 : (k + 1) * 128] = term.astype(BF)
            by_cols[k * 128 : (k + 1) * 128, :] = term.T.astype(BF)

    def to_state(lhs, by_rows):
        out = dot(lhs, by_rows[...])
        return (out[:, 0:128] + out[:, 128:256]).astype(BF)

    def from_state(state, by_cols):
        return dot(jnp.concatenate([state, state], axis=1), by_cols[...])

    def local_end(hp, c):
        base = pl.multiple_of(hp * 128, 128)
        for hh in range(2):
            rows = pl.ds(pl.multiple_of(base + hh * 64, 64), 64)
            h = pl.ds(2 * hp + hh, 1)
            wx[rows, :] = (xt_ref[rows, :].astype(F32) * weight[h, :]).astype(BF)
        send_a[hp, 0:128, :] = to_state(wx[pl.ds(base, 128), :], bdb)
        t0 = tot[pl.ds(2 * hp, 1), :]
        t1 = tot[pl.ds(2 * hp + 1, 1), :]
        h0 = t0.astype(BF).astype(F32)
        h1 = t1.astype(BF).astype(F32)
        at = iota2((16, 128), 0)
        extra = jnp.where(at == 0, h0, jnp.where(at == 1, t0 - h0, jnp.where(at == 2, h1, t1 - h1)))
        send_a[hp, 128:144, :] = extra.astype(BF)
        return c

    def early(step, src, dst, ssem, rsem):
        def one(k, c):
            j = lax.rem(me + k, PEERS)
            step(j, 0)
            copy(src, dst, ssem, rsem, j, me).start()
            return c
        lax.fori_loop(1, PEERS, one, 0, unroll=5)
        step(me, 0)
        dst[me] = src[me]

    pl.semaphore_wait(barrier, len(friends))
    for k, j in enumerate(turns):
        w_block(j).wait()
        values = dot(both_rows(), dec[pl.ds(pl.multiple_of(j * D, D), D), :]).astype(BF)
        xt_ref[pl.ds(pl.multiple_of(j * 256, 256), 256), :] = values.T
        if k == 0:
            hp = sibling["ctx"]
            local_end(hp, 0)
            copy(send_a, recv_a, sa, ra, hp, me).start()
            local_end(me, 0)
            recv_a[me] = send_a[me]
        else:
            for hh in range(2):
                hp = 2 * j + hh
                local_end(hp, 0)
                copy(send_a, recv_a, sa, ra, hp, me).start()

    for b in range(2):
        sc = dot_exact(
            jnp.where(low, maps_c[halves[b]], 0.0), maps_b[halves[b]], NT
        )
        scm[b] = jnp.where(causal[b], sc, 0.0)

    zero_half = jnp.zeros((128, 128), BF)
    blocks = (((0, 0), (1, 0), (1, 1)), ((0, 0), (0, 1), (1, 1)))

    def span(i):
        return slice(i * 128, (i + 1) * 128)

    def tile(b, h, i, rows=128):
        return pl.ds(pl.multiple_of((b * HEADS + h) * ROWS + i * 128, 128), rows)

    def forward(hp, c):
        for hh in range(2):
            h = 2 * hp + hh
            rows = pl.ds(pl.multiple_of(h * 64, 64), 64)
            for b in range(2):
                column = pltpu.roll(l2_n[b], 128 - h, 1)[:, 0:1]
                line = l2_t[pl.ds(h, 1), halves[b]]
                size = step_t[pl.ds(h, 1), halves[b]]
                for i, j in blocks[b]:
                    d = jnp.exp2(jnp.minimum(column[span(i)] - line[:, span(j)], 0.0))
                    d = d * size[:, span(j)]
                    dec[tile(b, h, i), span(j)] = d.astype(BF)
                    mst[tile(b, h, i), span(j)] = (d * scm[b, span(i), span(j)]).astype(BF)
                mst[tile(b, h, b), span(1 - b)] = zero_half
                u[rows, halves[b]] = dot(xt_ref[rows, halves[b]], mst[tile(b, h, 0, ROWS), :], NT)
        return c

    def chain(recv, out, fwd_up):
        def totals(i):
            t = recv_a[i, 128:144, :].astype(F32)
            rows = iota2((128, 128), 0) < 64
            return jnp.where(rows, t[0:1] + t[1:2], t[2:3] + t[3:4])

        def climb(i, carry):
            up[i] = carry
            return totals(i) * carry + recv[i, 0:128, :].astype(F32)

        zero = jnp.zeros((128, 128), F32)
        lax.fori_loop(0, PEERS, climb, zero)

        def descend(k, carry):
            i = PEERS - 1 - k
            pick = low if fwd_up else jnp.logical_not(low)
            out[i] = jnp.where(pick, up[i], carry).astype(BF)
            return totals(i) * carry + recv[i, 0:128, :].astype(F32)

        lax.fori_loop(0, PEERS, descend, zero)

    lax.fori_loop(0, PAIRS // 4, forward, 0)
    recv_all(send_a, recv_a, sa, ra)
    chain(recv_a, send_a2, True)
    recv_a2[me] = send_a2[me]
    send_all(send_a2, recv_a2, sa2, ra2)
    lax.fori_loop(PAIRS // 4, PAIRS, forward, 0)

    for blk in range(8):
        turned_c = cot_ref[:, blk * 256 : (blk + 1) * 256].T
        flipped_c = dot(flip, turned_c).astype(BF)
        for hh in range(2):
            ct[blk, hh, :, 0:ROWS] = turned_c[hh * 128 : hh * 128 + 128]
            ct[7 - blk, hh, :, ROWS:T2] = flipped_c[hh * 128 : hh * 128 + 128]

    recv_all(send_a2, recv_a2, sa2, ra2)

    def gains(hp):
        lane = pl.ds(pl.multiple_of(hp * 128, 128), 128)
        column = jnp.broadcast_to(gain_ref[:, lane], (128, 128)).T
        return jnp.concatenate([column] * 4, axis=1)

    def readout(hp, c):
        q, e = c
        base = pl.multiple_of(hp * 128, 128)
        out = from_state(recv_a2[hp], bdct)
        gain = gains(hp)
        for hh in range(2):
            rows = pl.ds(pl.multiple_of(base + hh * 64, 64), 64)
            part = slice(hh * 64, hh * 64 + 64)
            v = u[rows, :] + out[part] * el_t[pl.ds(2 * hp + hh, 1), :]
            u[rows, :] = v
            q = q + jnp.sum(v * v, axis=0, keepdims=True)
            e = e + jnp.sum(v * gain[part] * ct[lax.div(hp, 2), lax.rem(hp, 2), part, :].astype(F32), axis=0, keepdims=True)
        return q, e

    none = jnp.zeros((1, T2), F32)
    q, e = lax.fori_loop(0, PAIRS, readout, (none, none), unroll=4)
    scale = lax.rsqrt(q * (1.0 / D) + 1e-05)
    pull = scale * scale * scale * e * (1.0 / D)

    def normed(hp, c):
        base = pl.multiple_of(hp * 128, 128)
        gain = gains(hp)
        for hh in range(2):
            rows = pl.ds(pl.multiple_of(base + hh * 64, 64), 64)
            h = pl.ds(2 * hp + hh, 1)
            part = slice(hh * 64, hh * 64 + 64)
            v = u[rows, :]
            gs = gain[part] * scale
            back = gs * ct[lax.div(hp, 2), lax.rem(hp, 2), part, :].astype(F32) - v * pull
            vdu[rows, :] = (back * el_t[h, :]).astype(BF)
            back = back.astype(BF)
            du[rows, :] = back
            prow[h, :] = jnp.sum(back.astype(F32) * v, axis=0, keepdims=True)
            u[rows, :] = v * gs
        send_b[hp] = to_state(vdu[pl.ds(base, 128), :], bdc)
        return c

    early(normed, send_b, recv_b, sb, rb)
    dsc[...] = jnp.zeros_like(dsc)

    def backward(hp, c):
        for b in range(2):
            pair = []
            for hh in range(2):
                h = 2 * hp + hh
                rows = pl.ds(pl.multiple_of(h * 64, 64), 64)
                d = du[rows, halves[b]]
                g[rows, halves[b]] = dot(d, mst[tile(b, h, 0, ROWS), :])
                pair.append(dot(d, xt_ref[rows, halves[b]], TN))
            for i, j in blocks[b]:
                acc = dsc[b, span(i), span(j)]
                for hh in range(2):
                    acc = acc + pair[hh][span(i), span(j)] * dec[
                        tile(b, 2 * hp + hh, i), span(j)
                    ].astype(F32)
                dsc[b, span(i), span(j)] = acc
        return c

    lax.fori_loop(0, 10, backward, 0)
    for blk in range(8):
        y_rc = u[(7 - blk) * 256 : (8 - blk) * 256, ROWS:T2].astype(BF)
        y = u[blk * 256 : (blk + 1) * 256, 0:ROWS] + dot(flip, y_rc)
        mixed_ref[:, blk * 256 : (blk + 1) * 256] = y.astype(BF).T

    def read_maps(hp, acc):
        return acc + dot(recv_a2[hp], vdu[pl.ds(pl.multiple_of(hp * 128, 128), 128), :], TN)

    dc_state = lax.fori_loop(0, PAIRS, read_maps, jnp.zeros((128, T2), F32), unroll=4)
    recv_all(send_b, recv_b, sb, rb)
    chain(recv_b, send_b2, False)
    recv_b2[me] = send_b2[me]
    send_all(send_b2, recv_b2, sb2, rb2)
    lax.fori_loop(10, PAIRS, backward, 0)

    own_maps = []
    for b in range(2):
        lanes = halves[b]
        d_scores = jnp.where(causal[b], dsc[b], 0.0)
        part = slice(b * 64, b * 64 + 64)
        fine = slice(128 + b * 64, 192 + b * 64)
        own_b = bdbt[part, lanes].astype(F32) + bdbt[fine, lanes].astype(F32)
        own_c = bdct[part, lanes].astype(F32) + bdct[fine, lanes].astype(F32)
        dc = dot_exact(own_b, d_scores, NT) + dc_state[part, lanes]
        dx[D + 64 : D + 128, lanes] = dc.astype(BF)
        own_maps.append(dot_exact(own_c, d_scores))
    dx[D + 160 : WIDE, :] = jnp.zeros((WIDE - D - 160, T2), BF)
    for blk in range(8):
        across = rows_ref[:, blk * 256 : (blk + 1) * 256].T
        flipped = dot(flip, across).astype(BF)
        for hh in range(2):
            ct[blk, hh, :, 0:ROWS] = across[hh * 128 : hh * 128 + 128]
            ct[7 - blk, hh, :, ROWS:T2] = flipped[hh * 128 : hh * 128 + 128]
    rows_swap = to(sibling, ct.at[:, 1 - core], rt_in, core_s.at[PARTS], core_r.at[PARTS])
    rows_swap.start()

    def swap(p):
        return to(
            sibling, dx.at[pl.ds(p * COLS, COLS), :], dx_in.at[p], core_s.at[p], core_r.at[p]
        )

    recv_all(send_b2, recv_b2, sb2, rb2)

    def finish(hp, acc):
        base = pl.multiple_of(hp * 128, 128)
        after = recv_b2[hp]
        acc = acc + dot(after, wx[pl.ds(base, 128), :], TN)
        out = from_state(after, bdbt)
        meet = after.astype(F32) * recv_a2[hp].astype(F32)
        for hh in range(2):
            rows = pl.ds(pl.multiple_of(base + hh * 64, 64), 64)
            h = pl.ds(2 * hp + hh, 1)
            part = slice(hh * 64, hh * 64 + 64)
            asrow[h, :] = jnp.sum(meet[part], axis=0, keepdims=True)
            far = out[part] * weight[h, :]
            whole = g[rows, :] + far
            dx[rows, :] = whole.astype(BF)
            x = xt_ref[rows, :].astype(F32)
            qrow[h, :] = jnp.sum(x * whole, axis=0, keepdims=True)
            q2row[h, :] = jnp.sum(x * far, axis=0, keepdims=True)
        return acc


    def small_part(db_state):
        met = asrow[...] * tot[...]
        neg_col = jnp.broadcast_to(neg_rate, (128, 128)).T[0:HEADS, 0:1]
        for b in range(2):
            lanes = halves[b]
            mine = low if b == 0 else jnp.logical_not(low)
            end_grad = jnp.sum(jnp.where(mine, met, 0.0), axis=1, keepdims=True) + jnp.sum(
                q2row[:, lanes], axis=1, keepdims=True
            )
            dl = prow[:, lanes] - qrow[:, lanes]
            da = dot_exact(dl, tri[b]) + end_grad
            zb = zt[:, lanes]
            small_e = jnp.exp(-jnp.abs(zb))
            sig = jnp.where(zb >= 0, 1.0, small_e) / (1.0 + small_e)
            ratio = jnp.where(zb < -20.0, 1.0, sig / step_t[:, lanes])
            dz = qrow[:, lanes] * ratio + da * neg_col * sig
            dx[D + 128 : D + 160, lanes] = dz.astype(BF)
            part = slice(b * 64, b * 64 + 64)
            db = own_maps[b] + db_state[part, lanes]
            dx[D : D + 64, lanes] = db.astype(BF)
        swap(8).start()

    orders = (("z", "y", "x"), ("y", "x", "z"), ("x", "z", "y")) * 3

    def moves(p, stage):
        axis = orders[p][stage]
        here = coords[axis]
        found = []
        for k in (2, 1, 3):
            v = (here + k) % 4

            def copy_out(slot, v=v):
                if stage == 0:
                    src, dst = dec.at[pl.ds(pl.multiple_of(p * 1024 + v * 256, 256), 256), :], in1
                elif stage == 1:
                    first_row = PARTS * 1024 + p * 256
                    src, dst = dec.at[pl.ds(pl.multiple_of(first_row + v * 64, 64), 64), :], in2
                else:
                    src, dst = buf3.at[p, v], in3
                return to(
                    at_axis(axis, v), src, dst.at[p, slot],
                    ss.at[p, stage, v], rs.at[p, stage, slot],
                )

            found.append((v, lambda c=copy_out: c(here), lambda c=copy_out, v=v: c(v)))
        return found

    def launch(p, stage):
        for v, out, back in moves(p, stage):
            out().start()

    def arrived(p, stage):
        found = moves(p, stage)
        for v, out, back in found:
            back().wait_recv()
        return [v for v, out, back in found], coords[orders[p][stage]]

    def gradient(p):
        swap(p).wait_recv()
        left = jnp.concatenate(
            [ct[:, core].reshape(1024, T2), rt_in[...].reshape(1024, T2)], axis=1
        )
        right = jnp.concatenate([dx[p * COLS : (p + 1) * COLS, :], dx_in[p]], axis=1)
        tile = dot(left, right, NT).astype(BF)
        for k in range(64):
            jj, m = k // 8, k % 8
            where = {"z": m // 2, "y": jj // 2, "x": (m % 2) * 2 + jj % 2}
            a, b, d = (where[axis] for axis in orders[p])
            first_row = p * 1024 + ((a * 4 + b) * 4 + d) * 16
            dec[first_row : first_row + 16, :] = tile[k * 16 : (k + 1) * 16]
        launch(p, 0)

    def first(p):
        peers, here = arrived(p, 0)
        mine = pl.ds(pl.multiple_of(p * 1024 + here * 256, 256), 256)
        total = dec[mine, :].astype(F32)
        for v in peers:
            total = total + in1[p, v].astype(F32)
        dec[PARTS * 1024 + p * 256 : PARTS * 1024 + (p + 1) * 256, :] = total.astype(BF)
        launch(p, 1)

    def second(p):
        peers, here = arrived(p, 1)
        mine = pl.ds(pl.multiple_of(PARTS * 1024 + p * 256 + here * 64, 64), 64)
        total = dec[mine, :].astype(F32)
        for v in peers:
            total = total + in2[p, v].astype(F32)
        for v in range(4):
            buf3[p, v] = total[v * 16 : (v + 1) * 16]
        launch(p, 2)

    def third(p):
        peers, here = arrived(p, 2)
        total = buf3[p, here]
        for v in peers:
            total = total + in3[p, v]
        return total

    shares = []

    def share(kind, src, dst):
        dst[dp] = src[...]
        for k in range(1, 8):
            j = (dp + k) % 8

            def copy_out(slot, j=j):
                return to(
                    {"dp": j, "ctx": me}, src, dst.at[slot],
                    out_s.at[kind, j], out_r.at[kind, slot],
                )

            copy_out(dp).start()
            shares.append((kind, lambda c=copy_out: c(dp), lambda c=copy_out, j=j: c(j)))

    def finals(parts):
        for p in parts:
            piece = third(p)
            whole = piece.astype(BF)
            if p < 6:
                last0[:, p * COLS : (p + 1) * COLS] = whole
            else:
                last1[:, (p - 6) * COLS : (p - 5) * COLS] = whole
            if p == PARTS - 1:
                last1[:, 3 * COLS : 4 * COLS] = (piece - whole.astype(F32)).astype(BF)

    db_state = jnp.zeros((128, T2), F32)
    for p in range(8):
        db_state = finish(2 * p + 1, finish(2 * p, db_state))
        swap(p).start()
        if p == 2:
            rows_swap.wait_recv()
        if p >= 2:
            gradient(p - 2)
    small_part(db_state)
    for p in range(6, PARTS):
        gradient(p)
        first(p - 6)

    sent_all(send_a, recv_a, sa, ra)
    sent_all(send_a2, recv_a2, sa2, ra2)
    sent_all(send_b, recv_b, sb, rb)
    sent_all(send_b2, recv_b2, sb2, rb2)
    for p in range(3, 6):
        first(p)
    for p in range(0, 3):
        second(p)
    for p in range(6, 9):
        first(p)
    for p in range(3, 6):
        second(p)
    for p in range(6, 9):
        second(p)
    finals(range(0, 6))
    share(0, last0, outs0)
    finals(range(6, 9))
    share(1, last1, outs1)

    def gathered(kind):
        for which, out, back in shares:
            if which == kind:
                back().wait_recv()

    gathered(0)
    for k in range(8):
        gx_ref[k * 16 : (k + 1) * 16, 0:1536] = outs0[k].astype(F32)
    gathered(1)
    for k in range(8):
        rows = slice(k * 16, (k + 1) * 16)
        gx_ref[rows, 1536:D] = outs1[k, :, 0:512].astype(F32)
        narrow = outs1[k, :, 512:768].astype(F32) + outs1[k, :, 768:1024].astype(F32)
        gs_ref[:, rows] = narrow.T[0:160]

    rows_swap.wait_send()
    for p in range(PARTS):
        swap(p).wait_send()
        for stage in range(3):
            for v, out, back in moves(p, stage):
                out().wait_send()
    for which, out, back in shares:
        out().wait_send()


def scan(rows, x_weight, small_weight, cot, gain, log_rates, step_bias):
    vmem = pl.BlockSpec(memory_space=pltpu.VMEM)
    V = pltpu.VMEM
    dma = pltpu.SemaphoreType.DMA
    slots = [V((PEERS, SLOT, 128), BF)] * 2 + [V((PEERS, 128, 128), BF)] * 6
    return pl.pallas_call(
        scan_kernel,
        in_specs=[vmem, pl.BlockSpec(memory_space=pl.ANY)] + [vmem] * 5,
        out_specs=[vmem] * 3,
        out_shape=[
            jax.ShapeDtypeStruct((ROWS, D), BF),
            jax.ShapeDtypeStruct((128, D), F32),
            jax.ShapeDtypeStruct((160, 128), F32),
        ],
        scratch_shapes=[
            V((D, T2), BF),
            V((T2, 256), F32),
            pltpu.SemaphoreType.DMA((8,)),
            V((8, 128), F32),
            V((HEADS, T2), F32),
            V((HEADS, T2), F32),
            V((HEADS, T2), F32),
            V((HEADS, T2), F32),
            V((2, ROWS, 128), F32),
            V((HEADS, T2), F32),
            V((T2, 256), BF),
            V((256, T2), BF),
            V((T2, 256), BF),
            V((256, T2), BF),
            V((2, ROWS, ROWS), F32),
            V((2, ROWS, ROWS), F32),
            V((D, T2), BF),
            V((8, 2, 128, T2), BF),
            V((D, T2), F32),
            V((D, T2), F32),
            V((WIDE, T2), BF),
            V((D, T2), BF),
            V((2 * HEADS * ROWS, ROWS), BF),
            V((2 * HEADS * ROWS, ROWS), BF),
            V((HEADS, 128), F32),
            V((HEADS, T2), F32),
            V((HEADS, T2), F32),
            V((HEADS, T2), F32),
            V((HEADS, 128), F32),
        ]
        + slots
        + [
            V((PEERS, 128, 128), F32),
            V((8, 128, T2), BF),
            V((PARTS, COLS, T2), BF),
            V((PARTS, 4, 256, COLS), BF),
            V((PARTS, 4, 64, COLS), BF),
            V((PARTS, 4, 16, COLS), F32),
            V((PARTS, 4, 16, COLS), F32),
            V((16, 1536), BF),
            V((16, 1024), BF),
            V((8, 16, 1536), BF),
            V((8, 16, 1024), BF),
        ]
        + [dma((PEERS,))] * 8
        + [
            dma((PARTS + 1,)),
            dma((PARTS + 1,)),
            dma((PARTS, 3, 4)),
            dma((PARTS, 3, 4)),
            dma((2, 8)),
            dma((2, 8)),
        ],
        compiler_params=pltpu.CompilerParams(
            collective_id=0, has_side_effects=True, vmem_limit_bytes=62 * 2**20
        ),
        name="layer",
    )(rows, x_weight, small_weight, cot, gain, log_rates, step_bias)


def hand_on_kernel(*refs):
    count = (len(refs) - 2) // 3
    ins, outs, held = refs[:count], refs[count : 2 * count], refs[2 * count : 3 * count]
    read_sem, write_sem = refs[3 * count :]
    chunks = []
    for src, dst, buf in zip(ins, outs, held):
        rows = src.shape[0] // 4
        for k in range(4):
            part = pl.ds(k * rows, rows)
            i = len(chunks)
            chunks.append((
                pltpu.make_async_copy(src.at[part, :], buf.at[part, :], read_sem.at[i]),
                pltpu.make_async_copy(buf.at[part, :], dst.at[part, :], write_sem.at[i]),
            ))
    for read, write in chunks:
        read.start()
    for read, write in chunks:
        read.wait()
        write.start()
    for read, write in chunks:
        write.wait()


def hand_on(*arrays):
    anywhere = pl.BlockSpec(memory_space=pl.ANY)
    dma = pltpu.SemaphoreType.DMA
    return pl.pallas_call(
        hand_on_kernel,
        in_specs=[anywhere] * len(arrays),
        out_specs=[anywhere] * len(arrays),
        out_shape=[jax.ShapeDtypeStruct(a.shape, a.dtype) for a in arrays],
        scratch_shapes=[pltpu.VMEM(a.shape, a.dtype) for a in arrays]
        + [dma((4 * len(arrays),)), dma((4 * len(arrays),))],
        name="hand_on",
    )(*arrays)


def shards(hidden, x_weight, state_weight, log_rates, step_bias, out_gain, cotangent):
    mixed, grad_x, grad_small = hand_on(*scan(
        hidden[0], x_weight, state_weight.T, cotangent[0],
        out_gain[None], log_rates[None], step_bias[None],
    ))
    return (mixed[None], grad_x, grad_small.T)


def solution(mesh):
    return jax.shard_map(
        shards,
        mesh=mesh,
        in_specs=(P("dp", "ctx", None), P(), P(), P(), P(), P(), P("dp", "ctx", None)),
        out_specs=(P("dp", "ctx", None), P("ctx", None), P("ctx", None)),
        check_vma=False,
    )
```
